256 devices in a mesh: dp: 16 (over x_hi, z), seq: 16 (over y, x_lo, core).
Axes of the slice: x: 4 (x_hi: 2, x_lo: 2; x = x_hi * 2 + x_lo), y: 4, z: 8, core: 2. Of those that a mesh axis runs over, the one named last changes fastest.
Arguments:
- inputs: bfloat16 [16, 2048, 1536], P('dp', 'seq'), may hold values from -6 to 6
- dilations: int32 [2], replicated, may hold values from 1 to 16, as said below
- taps: float32 [2, 3, 1536], replicated, may hold values from -3 to 3
- gains: float32 [3, 1536], replicated, may hold values from 0.5 to 1.5
- bias_table: float32 [64, 4], replicated
- buckets: int32 [4095], replicated, may hold values from 0 to 63, as said below
- w_query: bfloat16 [1536, 256], replicated, may hold values from -0.15625 to 0.15625
- w_key: bfloat16 [1536, 256], replicated, may hold values from -0.15625 to 0.15625
- w_value: bfloat16 [1536, 768], replicated, may hold values from -0.15625 to 0.15625
- w_out: bfloat16 [768, 1536], replicated, may hold values from -0.875 to 0.875
- cotangent: bfloat16 [16, 2048, 1536], P('dp', 'seq'), may hold values from -6 to 6
Outputs:
- result: bfloat16 [16, 2048, 1536], P('dp', 'seq')
- input_grad: bfloat16 [16, 2048, 1536], P('dp', 'seq')
- weight_grads: float32 [1536, 2048], P(('dp', 'seq'))
The draws below stay inside these ranges and needn't reach their ends.
Inputs may be any that keep to these rules, and one draw needn't show every extreme that they name: `dilations`: some block has dilation exactly 16. `buckets`: entry i - j + 2047 holds the bucket of query bin i and key bin j.
All inputs are finite; a program needn't handle non-finite values.
Results may differ from the reference program's by a relative error of at most 0.015.
Values may be sent and summed in bfloat16 or wider, within the bound.
No kernel may reach another device: no remote copies, remote signals or barrier semaphores. Data moves between devices by JAX's collectives and lax.ppermute only.
A program may use at most 128 MiB of HBM per device.

```python
import jax
import jax.numpy as jnp
from jax import lax

C = 1536
HEADS = 4
KEY = 64
VALUE = 192
TOK_DEV = 128
BLOCKS = 2
DMAX = 16
BUCKETS = 64
LOCI = 16
LENGTH = 2048
HQ = 256
INNER = 768
N_SEQ = 16


def draw_dilations(key, part):
    key = jax.random.fold_in(key, 11)
    key_spacing, key_widest = jax.random.split(key)
    spacing = jax.random.randint(key_spacing, (BLOCKS,), 1, DMAX + 1)
    widest = jax.random.randint(key_widest, (), 0, BLOCKS)
    return jnp.where(jnp.arange(BLOCKS) == widest, DMAX, spacing).astype(jnp.int32)


def draw_buckets(key, part):
    key = jax.random.fold_in(key, 23)
    half_count = BUCKETS // 2
    exact_bounds = jnp.arange(1, 8, dtype=jnp.int32)
    spread = jnp.sort(jax.random.randint(key, (half_count - 8,), 8, LENGTH)).astype(jnp.int32)
    bounds = jnp.concatenate([exact_bounds, spread])
    offsets = jnp.arange(2 * LENGTH - 1, dtype=jnp.int32) - (LENGTH - 1)
    distance = jnp.abs(offsets)
    level_index = jnp.sum((distance[:, None] >= bounds[None, :]).astype(jnp.int32), axis=1)
    return (level_index + half_count * (offsets > 0).astype(jnp.int32)).astype(jnp.int32)


def draw_bias_table(key, part):
    key = jax.random.fold_in(key, 37)
    key_base = jax.random.fold_in(key, 0)
    return jax.random.normal(key_base, (BUCKETS, HEADS), jnp.float32)


def strengthened(entries, rng, source, target, shards_of, factor):
    def block_of(dim):
        return (jnp.arange(entries.shape[dim]) // (entries.shape[dim] // shards_of)).reshape((-1,) + (1,) * (entries.ndim - 1 - dim))

    near = jax.random.permutation(rng, shards_of)[block_of(target)]
    other_side = (block_of(target) + shards_of // 2) % shards_of
    return jnp.where((block_of(source) == near) | (block_of(source) == other_side), factor * entries, entries)


def block_scale(key, extent, cuts, smallest, high):
    loudness = 1.0
    for dim, parts in cuts:
        draws = jax.random.uniform(jax.random.fold_in(jax.random.fold_in(key, 6), dim), (parts,), jnp.float32, smallest / len(cuts), high / len(cuts))
        loudness = loudness * jnp.repeat(jnp.exp(draws), extent[dim] // parts).reshape((-1,) + (1,) * (len(extent) - 1 - dim))
    return loudness


def gaussian(own_key, extent, scale, most, cuts=(), kind=jnp.bfloat16):
    loudness = block_scale(own_key, extent, cuts, -0.22, 0.18) if cuts else 1.0
    drawn = jax.random.normal(own_key, extent, jnp.float32) * scale * loudness
    return jnp.minimum(jnp.maximum(drawn, -most), most).astype(kind)


def bell_draw_with(own_key, extent, scale, bound, cuts, heavy, kind=jnp.bfloat16):
    values = scale * jax.random.normal(own_key, extent, jnp.float32)
    if cuts:
        values = values * block_scale(own_key, extent, cuts, -0.22, 0.18)
    return jnp.clip(strengthened(values, jax.random.fold_in(own_key, 3), *heavy), -bound, bound).astype(kind)


def setup_inputs(seed: int = 0) -> dict:
    streams_of = jax.random.split(jax.random.key(seed), 12)
    inputs = gaussian(streams_of[0], (LOCI, LENGTH, C), 1.0, 6.0, ((0, 16), (1, 16)))
    dilations = draw_dilations(jax.random.fold_in(streams_of[11], 71), 0)
    taps = gaussian(streams_of[2], (BLOCKS, 3, C), 0.5, 3.0, (), jnp.float32)
    gains = jnp.clip(1.0 + 0.1 * jax.random.normal(streams_of[3], (BLOCKS + 1, C), jnp.float32), 0.5, 1.5)
    bias_table = draw_bias_table(jax.random.fold_in(streams_of[11], 71), 0)
    buckets = draw_buckets(jax.random.fold_in(streams_of[11], 71), 0)
    w_query = gaussian(streams_of[6], (C, HQ), C ** -0.5, 0.15625)
    w_key = gaussian(streams_of[7], (C, HQ), C ** -0.5, 0.15625)
    w_value = gaussian(streams_of[8], (C, INNER), C ** -0.5, 0.15625)
    w_out = gaussian(streams_of[9], (INNER, C), (INNER // 16) ** -0.5, 0.875)
    cotangent = bell_draw_with(streams_of[10], (LOCI, LENGTH, C), 1.0, 6.0, ((0, 16), (1, 16)), (1, 2, 16, 2.0))
    return dict(inputs=inputs, dilations=dilations, taps=taps, gains=gains, bias_table=bias_table, buckets=buckets, w_query=w_query, w_key=w_key, w_value=w_value, w_out=w_out, cotangent=cotangent)


epsilon = 1e-06

def normalize(field_rows, gain_row):
    field_rows = field_rows.astype(jnp.float32)
    spread = lax.rsqrt(lax.optimization_barrier(jnp.mean(field_rows * field_rows, axis=-1, keepdims=True)) + epsilon)
    return field_rows * spread * gain_row

def activate(field_rows, gain_row):
    return jax.nn.gelu(normalize(field_rows, gain_row), approximate=False)

def dilated(activity, spacing, weights_taps):
    padded = jnp.pad(activity, ((DMAX, DMAX), (0, 0)))
    row_count = activity.shape[0]
    lower_rows = lax.dynamic_slice_in_dim(padded, DMAX - spacing, row_count, 0)
    upper_rows = lax.dynamic_slice_in_dim(padded, DMAX + spacing, row_count, 0)
    return weights_taps[0] * lower_rows + weights_taps[1] * activity + weights_taps[2] * upper_rows

def block_bias(per_offset, start_row):
    row_index = jnp.arange(TOK_DEV, dtype=jnp.int32)[:, None]
    col_index = jnp.arange(LENGTH, dtype=jnp.int32)[None, :]
    return per_offset[:, start_row + row_index - col_index + (LENGTH - 1)]

def one_locus(inputs_locus, cotangent_locus, dilations, taps, gains, per_offset, w_query, w_key, w_value, w_out):
    hidden = inputs_locus
    saved_rows = []
    for block_index in range(BLOCKS):
        saved_rows.append(hidden)
        activity = activate(hidden, gains[block_index]).astype(jnp.bfloat16)
        hidden = (hidden + dilated(activity, dilations[block_index], taps[block_index])).astype(jnp.bfloat16)
    normed = normalize(hidden, gains[BLOCKS]).astype(jnp.bfloat16)
    queries = jnp.dot(normed, w_query, preferred_element_type=jnp.float32).astype(jnp.bfloat16)
    key_rows = jnp.dot(normed, w_key, preferred_element_type=jnp.float32).astype(jnp.bfloat16)
    value_rows = jnp.dot(normed, w_value, preferred_element_type=jnp.float32).astype(jnp.bfloat16)
    score_scale = KEY ** (-0.5)
    starts = jnp.arange(N_SEQ, dtype=jnp.int32) * TOK_DEV

    def head_probs(query_block, pos_bias, head_index):
        query_head = query_block[:, head_index * KEY:(head_index + 1) * KEY]
        key_head = key_rows[:, head_index * KEY:(head_index + 1) * KEY]
        scores = jnp.dot(query_head, key_head.T, preferred_element_type=jnp.float32) * score_scale + pos_bias[head_index]
        row_max = lax.optimization_barrier(jnp.max(scores, axis=1, keepdims=True))
        exp_scores = jnp.exp(scores - row_max)
        return exp_scores / lax.optimization_barrier(jnp.sum(exp_scores, axis=1, keepdims=True))

    def forward_block(start_row):
        query_block = lax.dynamic_slice_in_dim(queries, start_row, TOK_DEV, 0)
        pos_bias = block_bias(per_offset, start_row)
        pieces = []
        for head_index in range(HEADS):
            soft_weights = head_probs(query_block, pos_bias, head_index).astype(jnp.bfloat16)
            value_head = value_rows[:, head_index * VALUE:(head_index + 1) * VALUE]
            pieces.append(jnp.dot(soft_weights, value_head, preferred_element_type=jnp.float32))
        return jnp.concatenate(pieces, axis=1).astype(jnp.bfloat16)
    attended = lax.map(forward_block, starts).reshape(LENGTH, HEADS * VALUE)
    result = (hidden + jnp.dot(attended, w_out, preferred_element_type=jnp.float32)).astype(jnp.bfloat16)
    d_attended = jnp.dot(cotangent_locus, w_out.T, preferred_element_type=jnp.float32).astype(jnp.bfloat16)

    def backward_block(kv_total, start_row):
        query_block = lax.dynamic_slice_in_dim(queries, start_row, TOK_DEV, 0)
        attended_block = lax.dynamic_slice_in_dim(attended, start_row, TOK_DEV, 0)
        grad_block = lax.dynamic_slice_in_dim(d_attended, start_row, TOK_DEV, 0)
        pos_bias = block_bias(per_offset, start_row)
        query_parts, key_parts, value_parts = ([], [], [])
        for head_index in range(HEADS):
            probs = head_probs(query_block, pos_bias, head_index)
            query_head = query_block[:, head_index * KEY:(head_index + 1) * KEY]
            key_head = key_rows[:, head_index * KEY:(head_index + 1) * KEY]
            value_head = value_rows[:, head_index * VALUE:(head_index + 1) * VALUE]
            out_head = attended_block[:, head_index * VALUE:(head_index + 1) * VALUE]
            grad_head = grad_block[:, head_index * VALUE:(head_index + 1) * VALUE]
            grad_probs = jnp.dot(grad_head, value_head.T, preferred_element_type=jnp.float32)
            row_delta = lax.optimization_barrier(jnp.sum(grad_head.astype(jnp.float32) * out_head.astype(jnp.float32), axis=1, keepdims=True))
            d_scores = (probs * (grad_probs - row_delta)).astype(jnp.bfloat16)
            query_parts.append(jnp.dot(d_scores, key_head, preferred_element_type=jnp.float32) * score_scale)
            key_parts.append(jnp.dot(d_scores.T, query_head, preferred_element_type=jnp.float32) * score_scale)
            value_parts.append(jnp.dot(probs.astype(jnp.bfloat16).T, grad_head, preferred_element_type=jnp.float32))
        partial_value = jnp.concatenate(key_parts + value_parts, axis=1).astype(jnp.bfloat16)
        return (kv_total + partial_value.astype(jnp.float32), jnp.concatenate(query_parts, axis=1).astype(jnp.bfloat16))
    kv_start = jnp.zeros((LENGTH, HEADS * (KEY + VALUE)), jnp.float32)
    kv_total, query_blocks = lax.scan(backward_block, kv_start, starts)
    grad_queries = query_blocks.reshape(LENGTH, HEADS * KEY)
    grad_kv = kv_total.astype(jnp.bfloat16)
    grad_keys = grad_kv[:, :HEADS * KEY]
    grad_values = grad_kv[:, HEADS * KEY:]
    grad_normed = jnp.dot(grad_queries, w_query.T, preferred_element_type=jnp.float32)
    grad_normed = grad_normed + jnp.dot(grad_keys, w_key.T, preferred_element_type=jnp.float32)
    grad_normed = grad_normed + jnp.dot(grad_values, w_value.T, preferred_element_type=jnp.float32)
    norm_out, pull_norm = jax.vjp(lambda field_rows: normalize(field_rows, gains[BLOCKS]), hidden.astype(jnp.float32))
    grad_hidden = (cotangent_locus + pull_norm(grad_normed)[0]).astype(jnp.bfloat16)
    grad_term = jnp.concatenate([jnp.dot(normed.T, grad_queries, preferred_element_type=jnp.float32), jnp.dot(normed.T, grad_keys, preferred_element_type=jnp.float32), jnp.dot(normed.T, grad_values, preferred_element_type=jnp.float32), jnp.dot(cotangent_locus.T, attended, preferred_element_type=jnp.float32)], axis=1)
    for block_index in reversed(range(BLOCKS)):
        grad_act = dilated(grad_hidden, dilations[block_index], taps[block_index][::-1])
        act_out, pull_act = jax.vjp(lambda field_rows: activate(field_rows, gains[block_index]), saved_rows[block_index].astype(jnp.float32))
        grad_hidden = (grad_hidden + pull_act(grad_act)[0]).astype(jnp.bfloat16)
    return (result, grad_hidden, grad_term)

def reference(inputs, dilations, taps, gains, bias_table, buckets, w_query, w_key, w_value, w_out, cotangent):
    per_offset = bias_table[buckets].T

    def per_locus(grad_total, locus_pair):
        result, grad_hidden, grad_term = one_locus(locus_pair[0], locus_pair[1], dilations, taps, gains, per_offset, w_query, w_key, w_value, w_out)
        return (grad_total + grad_term, (result, grad_hidden))
    grad_start = jnp.zeros((C, 2 * HEADS * (KEY + VALUE)), jnp.float32)
    grad_total, outputs = lax.scan(per_locus, grad_start, (inputs, cotangent))
    return (outputs[0], outputs[1], grad_total / LOCI)
```

```python
import functools

import jax
import jax.numpy as jnp
from jax import lax
from jax.experimental import pallas as pl
from jax.experimental.pallas import tpu as pltpu
from jax.sharding import Mesh, PartitionSpec as P

HEADS = 4
KEY = 64
VALUE = 192
WIDE = KEY + VALUE
BLOCKS = 2
DMAX = 16
HALO = BLOCKS * DMAX
EPS = 1e-06
STEP = 16
SEQ = ("y", "xl", "core")
EVERY = ("xh", "z", "y", "xl", "core")
F32 = jnp.float32
BF16 = jnp.bfloat16
ROOT_HALF = 0.7071067811865476
ROOT_TWO_PI = 0.3989422804014327


def contract(left, right, left_dim, right_dim):
    return lax.dot_general(
        left, right, (((left_dim,), (right_dim,)), ((), ())), preferred_element_type=F32
    )


def call(body, outs, args, scratch=(), smem=(), cost=1, limit=24):
    spaces = [pltpu.SMEM if i in smem else pltpu.VMEM for i in range(len(args))]
    return pl.pallas_call(
        body,
        out_shape=tuple(jax.ShapeDtypeStruct(s, d) for s, d in outs),
        in_specs=[pl.BlockSpec(memory_space=s) for s in spaces],
        out_specs=tuple(pl.BlockSpec(memory_space=pltpu.VMEM) for _ in outs),
        scratch_shapes=list(scratch),
        compiler_params=pltpu.CompilerParams(vmem_limit_bytes=limit << 20),
        cost_estimate=pl.CostEstimate(
            flops=int(cost * 1e9), bytes_accessed=int(cost * 3e6), transcendentals=0
        ),
        name=body.__name__ if hasattr(body, "__name__") else body.func.__name__,
    )(*args)


def inverse_norm(rows):
    return lax.rsqrt(jnp.mean(rows * rows, axis=1, keepdims=True) + EPS)


def activate(rows, gain):
    field = rows * inverse_norm(rows) * gain
    return 0.5 * field * (1.0 + lax.erf(field * ROOT_HALF))


def rounded(rows):
    return rows.astype(BF16).astype(F32)


def loop(count, body):
    def step(i, carry):
        body(pl.multiple_of(i * STEP, STEP))
        return carry

    lax.fori_loop(0, count // STEP, step, 0)


def inside(start, first, last, edge, count):
    out = (first & (start < edge)) | (last & (start >= count - edge))
    return jnp.where(out, 0.0, 1.0)


def move(moved, source, gap):
    count, total = moved.shape[0] // 2, source.shape[0]
    row = lax.broadcasted_iota(jnp.int32, (count, total), 0)
    col = lax.broadcasted_iota(jnp.int32, (count, total), 1)
    held = source[...]
    for i, at in enumerate((DMAX - gap, DMAX + gap)):
        pick = jnp.where(col == row + at, 1.0, 0.0).astype(BF16)
        moved[i * count : (i + 1) * count, :] = contract(pick, held, 1, 0)


def tapped(taps, first, moved, center, r):
    count = moved.shape[0] // 2
    return (
        taps[first : first + 1, :] * moved[pl.ds(r, STEP), :]
        + taps[first + 1 : first + 2, :] * center
        + taps[first + 2 : first + 3, :] * moved[pl.ds(pl.multiple_of(count + r, STEP), STEP), :]
    )


def prelude(where, table, buckets, rows, gains, upstream, w_out, act, d_att, master):
    head = where[0]
    held = buckets[...]
    line = jnp.zeros(held.shape, F32)
    for b in range(table.shape[0]):
        line = jnp.where(held == b, table[b, head], line)
    span = held.shape[1]
    for r in range(0, 128, 8):
        master[r : r + 8, :] = pltpu.roll(
            jnp.broadcast_to(line, (8, span)), (span - 127 + r) % span, 1, stride=1, stride_axis=0
        )
    gain = gains[0:1, :]

    def body(r):
        act[pl.ds(r, STEP), :] = activate(rows[pl.ds(r, STEP), :].astype(F32), gain).astype(BF16)

    loop(rows.shape[0], body)
    d_att[...] = contract(upstream[...], w_out[...], 1, 1).astype(BF16)


def forward(
    where, dil, left, right, rows, act, d_att, taps, gains, w_query, w_key, w_value,
    m0, m1, m2, m3, normed, z, near, x_ext, a_ext, b_ext, slots, moved1, moved2,
):
    iy, iseq, nseq = where[0], where[1], where[2]
    tok = rows.shape[0]
    x_ext[0:HALO, :] = left[...]
    x_ext[HALO : HALO + tok, :] = rows[...]
    x_ext[HALO + tok :, :] = right[...]
    a_ext[HALO : HALO + tok, :] = act[...]
    gain = gains[0:1, :]
    for r in [*range(0, HALO, STEP), *range(HALO + tok, 2 * HALO + tok, STEP)]:
        a_ext[r : r + STEP, :] = activate(x_ext[r : r + STEP, :].astype(F32), gain).astype(BF16)
    gap, wide = dil[0], dil[1]
    first, last = iseq == 0, iseq == nseq - 1
    count = tok + 2 * DMAX
    gain = gains[1:2, :]
    move(moved1, a_ext, gap)

    def middle(r):
        center = pl.ds(pl.multiple_of(r + DMAX, STEP), STEP)
        mixed = tapped(taps, 0, moved1, a_ext[center, :].astype(F32), r)
        hidden = (x_ext[center, :].astype(F32) + mixed).astype(BF16)
        near[pl.ds(r, STEP), :] = hidden
        keep = inside(r, first, last, DMAX, count)
        b_ext[pl.ds(r, STEP), :] = (activate(hidden.astype(F32), gain) * keep).astype(BF16)

    loop(count, middle)
    last_gain = gains[2:3, :]
    move(moved2, b_ext, wide)

    def top(r):
        center = pl.ds(pl.multiple_of(r + DMAX, STEP), STEP)
        mixed = tapped(taps, 3, moved2, b_ext[center, :].astype(F32), r)
        hidden = (near[center, :].astype(F32) + mixed).astype(BF16)
        z[pl.ds(r, STEP), :] = hidden
        hidden = hidden.astype(F32)
        normed[pl.ds(r, STEP), :] = (hidden * inverse_norm(hidden) * last_gain).astype(BF16)

    loop(tok, top)
    field = normed[...]
    queries = (rounded(contract(field, w_query[...], 1, 0)) * KEY**-0.5).astype(BF16)
    keys = contract(field, w_key[...], 1, 0).astype(BF16)
    values = contract(field, w_value[...], 1, 0).astype(BF16)
    for h in range(HEADS):
        k, v = slice(h * KEY, (h + 1) * KEY), slice(h * VALUE, (h + 1) * VALUE)
        slots[lax.rem(h - iy + HEADS, HEADS)] = jnp.concatenate(
            [keys[:, k], values[:, v], queries[:, k], d_att[:, v]], axis=1
        )
    for i, out in enumerate((m0, m1, m2, m3)):
        out[...] = slots[i]


def slopes(rows, near, gains, slope0, slope1):
    def fill(source, gain, out):
        def body(r):
            held = source[pl.ds(r, STEP), :].astype(F32)
            field = held * inverse_norm(held) * gain
            below = 0.5 * (1.0 + lax.erf(field * ROOT_HALF))
            out[pl.ds(r, STEP), :] = (
                below + field * (ROOT_TWO_PI * jnp.exp(-0.5 * field * field))
            ) * gain

        loop(source.shape[0], body)

    fill(near, gains[1:2, :], slope1)
    fill(rows, gains[0:1, :], slope0)


def attend(
    where, m0, m1, m2, m3, kv1, kv2, kv3, master,
    t0, t1, t2, t3, own, far, give, ask, kv0, score, pull, soft, d_soft,
):
    iy, c = where[0], where[3]
    tok = m0.shape[0]
    many = HEADS * tok
    for i, m in enumerate((m0, m1, m2, m3)):
        kv0[i * tok : (i + 1) * tok, :] = m[:, :WIDE]
        ask[i * tok : (i + 1) * tok, :] = m[:, WIDE:]
    both = ask[...]
    lane = lax.broadcasted_iota(jnp.int32, (1, WIDE), 1)
    is_key = lane < KEY
    zero = jnp.zeros_like(both)
    queries = jnp.where(is_key, both, zero)
    d_att = jnp.where(is_key, zero, both)
    blocks = (kv0, kv1, kv2, kv3)
    bands = [lax.rem(iy - i + HEADS, HEADS) for i in range(HEADS)]
    top = None
    for j, block in enumerate(blocks):
        other = jnp.bitwise_xor(c, j)
        for i in range(HEADS):
            at = j * many + i * tok
            part = contract(block[i * tok : (i + 1) * tok, :], queries, 1, 1)
            bias = jnp.concatenate(
                [
                    master[:, pl.ds(pl.multiple_of((4 * (q - bands[i]) + c - other + 15) * tok, tok), tok)]
                    for q in bands
                ],
                axis=1,
            )
            part = part + bias
            score[at : at + tok, :] = part
            peak = jnp.max(part, axis=0, keepdims=True)
            top = peak if top is None else jnp.maximum(top, peak)
    total = jnp.zeros_like(top)
    for at in range(0, 4 * many, tok):
        part = jnp.exp(score[at : at + tok, :] - top)
        score[at : at + tok, :] = part
        total = total + jnp.sum(part, axis=0, keepdims=True)
    scale = 1.0 / total
    delta = jnp.zeros_like(top)
    for j, block in enumerate(blocks):
        for i in range(HEADS):
            at = j * many + i * tok
            probs = score[at : at + tok, :] * scale
            score[at : at + tok, :] = probs
            soft[at : at + tok, :] = probs.astype(BF16)
            part = contract(block[i * tok : (i + 1) * tok, :], d_att, 1, 1)
            pull[at : at + tok, :] = part
            delta = delta + jnp.sum(part * probs, axis=0, keepdims=True)
    for at in range(0, 4 * many, tok):
        d_soft[at : at + tok, :] = (
            score[at : at + tok, :] * (pull[at : at + tok, :] - delta)
        ).astype(BF16)
    att = jnp.zeros((WIDE, many), F32)
    d_query = jnp.zeros((WIDE, many), F32)
    for j, block in enumerate(blocks):
        held = block[...]
        span = slice(j * many, (j + 1) * many)
        att = att + contract(held, soft[span, :], 0, 0)
        d_query = d_query + contract(held, d_soft[span, :], 0, 0)
        d_kv = jnp.where(
            is_key, contract(d_soft[span, :], both, 1, 0), contract(soft[span, :], both, 1, 0)
        )
        if j == 0:
            own[...] = d_kv
        elif j == 2:
            far[...] = d_kv
        else:
            give[(j // 2) * many : (j // 2 + 1) * many, :] = d_kv.astype(BF16)
    side = lax.broadcasted_iota(jnp.int32, (WIDE, 1), 0) < KEY
    mixed = jnp.where(side, d_query * KEY**-0.5, att).T.astype(BF16)
    for i, t in enumerate((t0, t1, t2, t3)):
        t[...] = mixed[i * tok : (i + 1) * tok, :]


def first_sum(own, far, got, near, send):
    many = own.shape[0]
    near[...] = own[...] + got[:many, :].astype(F32)
    send[...] = (far[...] + got[many:, :].astype(F32)).astype(BF16)


def second_sum(near, got, d0, d1, d2, d3):
    total = (near[...] + got[...].astype(F32)).astype(BF16)
    tok = d0.shape[0]
    for i, d in enumerate((d0, d1, d2, d3)):
        d[...] = total[i * tok : (i + 1) * tok, :]


def gathered(slots, parts, iy):
    for i, part in enumerate(parts):
        slots[lax.rem(iy + i, HEADS)] = part[...]


def heads_of(slots, low, high):
    return jnp.concatenate([slots[h][:, low:high] for h in range(HEADS)], axis=1)


def project(where, t0, t1, t2, t3, z, w_out, w_query, result, g_query, slots):
    gathered(slots, (t0, t1, t2, t3), where[0])
    att = heads_of(slots, KEY, WIDE)
    result[...] = (z[...].astype(F32) + contract(att, w_out[...], 1, 0)).astype(BF16)
    g_query[...] = contract(heads_of(slots, 0, KEY), w_query[...], 1, 1)


def pull_norm(held, scaled):
    s = inverse_norm(held)
    return s * scaled - held * (s * s * s) * jnp.mean(scaled * held, axis=1, keepdims=True)


def grad_top(where, d0, d1, d2, d3, g_query, z, upstream, w_key, w_value, gains, out, slots, total):
    gathered(slots, (d0, d1, d2, d3), where[0])
    total[...] = (
        g_query[...]
        + contract(heads_of(slots, 0, KEY), w_key[...], 1, 1)
        + contract(heads_of(slots, KEY, WIDE), w_value[...], 1, 1)
    )
    gain = gains[2:3, :]

    def body(r):
        at = pl.ds(r, STEP)
        grad = pull_norm(z[at, :].astype(F32), total[at, :] * gain)
        out[at, :] = (upstream[at, :].astype(F32) + grad).astype(BF16)

    loop(z.shape[0], body)


def backward(
    where, dil, left, right, grad, slope0, slope1, rows, near, taps, out, g_ext, p_ext, moved1, moved2
):
    iseq, nseq = where[1], where[2]
    tok = rows.shape[0]
    first, last = iseq == 0, iseq == nseq - 1
    g_ext[0:HALO, :] = left[...]
    g_ext[HALO : HALO + tok, :] = grad[...]
    g_ext[HALO + tok :, :] = right[...]
    gap, wide = dil[0], dil[1]
    count = tok + 2 * DMAX

    move(moved1, g_ext, wide)

    def middle(r):
        center = g_ext[pl.ds(pl.multiple_of(r + DMAX, STEP), STEP), :].astype(F32)
        mixed = tapped(taps, 3, moved1, center, r)
        at = pl.ds(r, STEP)
        held = pull_norm(near[at, :].astype(F32), mixed * slope1[at, :])
        keep = inside(r, first, last, DMAX, count)
        p_ext[at, :] = ((center + held) * keep).astype(BF16)

    loop(count, middle)
    move(moved2, p_ext, gap)

    def bottom(r):
        center = p_ext[pl.ds(pl.multiple_of(r + DMAX, STEP), STEP), :].astype(F32)
        mixed = tapped(taps, 0, moved2, center, r)
        at = pl.ds(r, STEP)
        held = pull_norm(rows[at, :].astype(F32), mixed * slope0[at, :])
        out[at, :] = (center + held).astype(BF16)

    loop(tok, bottom)


def weigh(
    where, n0, n1, n2, n3, u0, u1, u2, u3, t0, t1, t2, t3, d0, d1, d2, d3, keep, give, n_all, u_all, t_all, d_all
):
    core = where[4]
    tok = n0.shape[0]
    for i, parts in enumerate(zip((n0, n1, n2, n3), (u0, u1, u2, u3), (t0, t1, t2, t3), (d0, d1, d2, d3))):
        for all_, part in zip((n_all, u_all, t_all, d_all), parts):
            all_[i * tok : (i + 1) * tok, :] = part[...]
    half = n0.shape[1] // 2
    is_key = lax.broadcasted_iota(jnp.int32, (1, WIDE), 1) < KEY
    for out, side in ((give, 1 - core), (keep, core)):
        for low in range(0, half, 256):
            at = pl.ds(pl.multiple_of(side * half + low, 256), 256)
            left = n_all[:, at]
            first = jnp.where(
                is_key, contract(left, t_all[...], 0, 0), contract(u_all[:, at], t_all[...], 0, 0)
            )
            out[low : low + 256, :WIDE] = first.astype(out.dtype)
            out[low : low + 256, WIDE:] = contract(left, d_all[...], 0, 0).astype(out.dtype)


def fold(places, parts, *refs):
    where, keep, got = refs[0], refs[1], refs[2 : 2 + places[1]]
    own, sends, held = refs[2 + places[1]], refs[3 + places[1] : -1], refs[-1]
    total = keep[...]
    for g in got:
        total = total + g[...].astype(F32)
    held[...] = total
    size = own.shape[0]
    for i, out in enumerate((own, *sends)):
        at = parts(where, i)
        out[...] = held[pl.ds(pl.multiple_of(at * size, 8), size), :].astype(out.dtype)


def fold_call(keep, got, where, parts, count, limit=24):
    rows, width = keep.shape
    size = rows // count
    body = functools.partial(fold, (None, len(got)), parts)
    outs = [((size, width), F32)] + [((size, width), BF16)] * (count - 1)
    return call(
        body, outs, (where, keep, *got), [pltpu.VMEM((rows, width), F32)], smem=(0,), cost=0.3, limit=limit
    )


def arrange(where, g0, g1, g2, g3, out, slots):
    c = where[3]
    for i, g in enumerate((g0, g1, g2, g3)):
        slots[lax.rem(c - i + HEADS, HEADS)] = g[...]
    scale = 1.0 / where[5].astype(F32)
    keys = HEADS * KEY
    for h in range(HEADS):
        held = slots[h] * scale
        out[:, h * KEY : (h + 1) * KEY] = held[:, :KEY]
        low = 2 * keys + HEADS * VALUE + h * VALUE
        out[:, low : low + VALUE] = held[:, KEY:WIDE]
        out[:, keys + h * KEY : keys + (h + 1) * KEY] = held[:, WIDE : WIDE + KEY]
        low = 2 * keys + h * VALUE
        out[:, low : low + VALUE] = held[:, WIDE + KEY :]


def shift(array, axis, count, step):
    return lax.ppermute(array, axis, [(i, (i + step) % count) for i in range(count)])


def flip(array, axis):
    return lax.ppermute(array, axis, [(0, 1), (1, 0)])


def halo(rows, nseq):
    width = HALO
    left = lax.ppermute(rows[-width:], SEQ, [(i, i + 1) for i in range(nseq - 1)])
    right = lax.ppermute(rows[:width], SEQ, [(i + 1, i) for i in range(nseq - 1)])
    return left, right


def local(
    sizes, inputs, dilations, taps, gains, bias_table, buckets, w_query, w_key, w_value, w_out, cotangent
):
    nxh, nz, ny = sizes
    nseq = ny * 4
    rows, upstream = inputs[0], cotangent[0]
    tok, chan = rows.shape
    iy, ixl, icore = lax.axis_index("y"), lax.axis_index("xl"), lax.axis_index("core")
    ixh, iz = lax.axis_index("xh"), lax.axis_index("z")
    c = ixl * 2 + icore
    loci = inputs.shape[0] * nxh * nz
    where = jnp.stack(
        [iy, iy * 4 + c, jnp.int32(nseq), c, icore, jnp.int32(loci), ixl, ixh, iz]
    ).astype(jnp.int32)
    back_taps = taps[:, ::-1].reshape(2 * 3, chan)
    taps = taps.reshape(2 * 3, chan)
    big = (tok, chan)

    left, right = halo(rows, nseq)
    line = jnp.pad(buckets, (0, 1))[None]
    act, d_att, master = call(
        prelude,
        [(big, BF16), ((tok, HEADS * VALUE), BF16), ((128, line.shape[1]), F32)],
        (where, bias_table, line, rows, gains, upstream, w_out),
        smem=(0, 1),
        cost=3,
    )
    up = [upstream] + [shift(upstream, "y", ny, k) for k in (1, 2, 3)]
    ext = (tok + 2 * HALO, chan)
    mid = (tok + 2 * DMAX, chan)
    shifted = [pltpu.VMEM((2 * mid[0], chan), F32), pltpu.VMEM((2 * tok, chan), F32)]
    *ms, normed, z, near = call(
        forward,
        [((tok, 2 * WIDE), BF16)] * 4 + [(big, BF16), (big, BF16), (mid, BF16)],
        (where, dilations, left, right, rows, act, d_att, taps, gains, w_query, w_key, w_value),
        [pltpu.VMEM(ext, BF16), pltpu.VMEM(ext, BF16), pltpu.VMEM(mid, BF16),
         pltpu.VMEM((HEADS, tok, 2 * WIDE), BF16), *shifted],
        smem=(0, 1),
        cost=6,
    )
    ms = [ms[0]] + [shift(ms[k], "y", ny, k) for k in (1, 2, 3)]
    kv0 = jnp.concatenate([m[:, :WIDE] for m in ms], axis=0)
    kv2 = flip(kv0, "xl")
    kv1 = flip(kv0, "core")
    kv3 = flip(kv2, "core")
    slope0, slope1 = call(slopes, [(big, F32), (mid, F32)], (rows, near, gains), cost=4)
    fields = [normed] + [shift(normed, "y", ny, k) for k in (1, 2, 3)]
    many = HEADS * tok
    *ts, own, far, give = call(
        attend,
        [((tok, WIDE), BF16)] * 4 + [((many, WIDE), F32)] * 2 + [((2 * many, WIDE), BF16)],
        (where, *ms, kv1, kv2, kv3, master),
        [pltpu.VMEM((many, WIDE), BF16), pltpu.VMEM((many, WIDE), BF16),
         pltpu.VMEM((4 * many, many), F32), pltpu.VMEM((4 * many, many), F32),
         pltpu.VMEM((4 * many, many), BF16), pltpu.VMEM((4 * many, many), BF16)],
        smem=(0,),
        cost=10,
        limit=40,
    )
    got = flip(give, "core")
    back = [ts[0]] + [shift(ts[k], "y", ny, -k) for k in (1, 2, 3)]
    own, far = call(
        first_sum, [((many, WIDE), F32), ((many, WIDE), BF16)], (own, far, got), cost=0.5
    )
    got = flip(far, "xl")
    ds = call(second_sum, [((tok, WIDE), BF16)] * 4, (own, got), cost=0.5)
    back_d = [ds[0]] + [shift(ds[k], "y", ny, -k) for k in (1, 2, 3)]
    result, g_query = call(
        project,
        [(big, BF16), (big, F32)],
        (where, *back, z, w_out, w_query),
        [pltpu.VMEM((HEADS, tok, WIDE), BF16)],
        smem=(0,),
        cost=2,
    )
    half = chan // 2
    keep, give = call(
        weigh,
        [((half, 2 * WIDE), F32), ((half, 2 * WIDE), BF16)],
        (where, *fields, *up, *ts, *ds),
        [pltpu.VMEM((many, chan), BF16), pltpu.VMEM((many, chan), BF16),
         pltpu.VMEM((many, WIDE), BF16), pltpu.VMEM((many, WIDE), BF16)],
        smem=(0,),
        cost=4,
        limit=32,
    )
    (grad,) = call(
        grad_top,
        [(big, BF16)],
        (where, *back_d, g_query, z, upstream, w_key, w_value, gains),
        [pltpu.VMEM((HEADS, tok, WIDE), BF16), pltpu.VMEM(big, F32)],
        smem=(0,),
        cost=3,
    )
    left, right = halo(grad, nseq)
    got = flip(give, "core")
    (input_grad,) = call(
        backward,
        [(big, BF16)],
        (where, dilations, left, right, grad, slope0, slope1, rows, near, back_taps),
        [pltpu.VMEM(ext, BF16), pltpu.VMEM(mid, BF16), *shifted],
        smem=(0, 1),
        cost=4,
    )

    pairs = [(a, b) for b in range(nxh) for a in range(2)]

    def ring_part(where, i):
        a, b = pairs[i]
        return jnp.bitwise_xor(where[6], a) * nxh + jnp.bitwise_xor(where[7], b)

    keep, *sends = fold_call(keep, [got], where, ring_part, len(pairs))
    got = []
    for (a, b), send in zip(pairs[1:], sends):
        order = [(s, ((s // 2) ^ b) * 2 + ((s % 2) ^ a)) for s in range(2 * nxh)]
        got.append(lax.ppermute(send, ("xh", "xl"), order))

    def line_part(where, i):
        return lax.rem(where[8] + i, nz)

    keep, *sends = fold_call(keep, got, where, line_part, nz)
    got = [shift(send, "z", nz, k + 1) for k, send in enumerate(sends)]
    (keep,) = fold_call(keep, got, where, lambda where, i: jnp.int32(0), 1)
    chunks = keep.reshape(4, keep.shape[0] // 4, 2 * WIDE)
    parts = []
    for k in range(4):
        order = []
        for s in range(nxh * nz * nseq):
            core, xl, y, line = s % 2, (s // 2) % 2, (s // 4) % ny, s // nseq
            z_, xh = line % nz, line // nz
            beta = ((core * 2 + xl) * nxh + xh) * nz + z_
            order.append((s, 4 * beta + (y + k) % 4))
        chunk = lax.dynamic_index_in_dim(chunks, lax.rem(iy + k, 4), 0, keepdims=False)
        parts.append(lax.ppermute(chunk, EVERY, order))
    size = parts[0].shape[0]
    (weight_sum,) = call(
        arrange,
        [((size, 8 * WIDE), F32)],
        (where, *parts),
        [pltpu.VMEM((HEADS, size, 2 * WIDE), F32)],
        smem=(0,),
        cost=0.1,
    )
    return (result[None], input_grad[None], weight_sum)


def solution(mesh):
    nseq = mesh.shape["seq"]
    ny = nseq // 4
    ndp = mesh.shape["dp"]
    nxh = 2 if ndp % 2 == 0 else 1
    sizes = (nxh, ndp // nxh, ny)
    fine = Mesh(mesh.devices.reshape(*sizes, 2, 2), EVERY)
    cells = P(("xh", "z"), SEQ, None)
    return jax.shard_map(
        functools.partial(local, sizes),
        mesh=fine,
        in_specs=(cells, *(P() for _ in range(9)), cells),
        out_specs=(cells, cells, P(EVERY, None)),
        check_vma=False,
    )
```

```python
import functools
import math

import jax
import jax.numpy as jnp
import numpy as np
from jax import lax
from jax.experimental import pallas as pl
from jax.experimental.pallas import tpu as pltpu
from jax.sharding import Mesh, PartitionSpec as P

HEADS = 4
KEY = 64
VALUE = 192
WIDE = KEY + VALUE
BLOCKS = 2
DMAX = 16
HALO = BLOCKS * DMAX
EPS = 1e-06
STEP = 16
SEQ = ("y", "xl", "core")
EVERY = ("xh", "z", "y", "xl", "core")
F32 = jnp.float32
BF16 = jnp.bfloat16
ROOT_HALF = 0.7071067811865476
ROOT_TWO_PI = 0.3989422804014327


def contract(left, right, left_dim, right_dim):
    return lax.dot_general(
        left, right, (((left_dim,), (right_dim,)), ((), ())), preferred_element_type=F32
    )


def call(body, outs, args, scratch=(), smem=(), hbm=(), cost=1, limit=24):
    spaces = [
        pltpu.SMEM if i in smem else pltpu.HBM if i in hbm else pltpu.VMEM for i in range(len(args))
    ]
    return pl.pallas_call(
        body,
        out_shape=tuple(jax.ShapeDtypeStruct(s, d) for s, d in outs),
        in_specs=[pl.BlockSpec(memory_space=s) for s in spaces],
        out_specs=tuple(pl.BlockSpec(memory_space=pltpu.VMEM) for _ in outs),
        scratch_shapes=list(scratch),
        compiler_params=pltpu.CompilerParams(vmem_limit_bytes=limit << 20),
        cost_estimate=pl.CostEstimate(
            flops=int(cost * 1e9), bytes_accessed=int(cost * 3e6), transcendentals=0
        ),
        name=body.__name__ if hasattr(body, "__name__") else body.func.__name__,
    )(*args)


def inverse_norm(rows):
    return lax.rsqrt(jnp.mean(rows * rows, axis=1, keepdims=True) + EPS)


def activate(rows, gain):
    field = rows * inverse_norm(rows) * gain
    return 0.5 * field * (1.0 + lax.erf(field * ROOT_HALF))


def rounded(rows):
    return rows.astype(BF16).astype(F32)


def loop(count, body):
    def step(i, carry):
        body(pl.multiple_of(i * STEP, STEP))
        return carry

    lax.fori_loop(0, count // STEP, step, 0)


def inside(start, first, last, edge, count):
    out = (first & (start < edge)) | (last & (start >= count - edge))
    return jnp.where(out, 0.0, 1.0)


def move(moved, source, gap):
    count, total = moved.shape[0] // 2, source.shape[0]
    row = lax.broadcasted_iota(jnp.int32, (count, total), 0)
    col = lax.broadcasted_iota(jnp.int32, (count, total), 1)
    held = source[...]
    for i, at in enumerate((DMAX - gap, DMAX + gap)):
        pick = jnp.where(col == row + at, 1.0, 0.0).astype(BF16)
        moved[i * count : (i + 1) * count, :] = contract(pick, held, 1, 0)


def tapped(taps, first, moved, center, r, low=0, high=2):
    count = moved.shape[0] // 2
    return (
        taps[first, low : low + 1, :] * moved[pl.ds(r, STEP), :]
        + taps[first, 1:2, :] * center
        + taps[first, high : high + 1, :] * moved[pl.ds(pl.multiple_of(count + r, STEP), STEP), :]
    )


def reorder(order, source, out, start):
    unit = order.shape[1]
    row = lax.broadcasted_iota(jnp.int32, (unit, unit), 0)
    pick = jnp.where(row == order[...], 1.0, 0.0).astype(BF16)
    for low in range(0, source.shape[1], unit):
        at = slice(low, low + unit)
        out[:, start + low : start + low + unit] = contract(source[:, at], pick, 1, 0).astype(BF16)


def fetch(pairs, sems):
    copies = [pltpu.make_async_copy(a, b, sems.at[i]) for i, (a, b) in enumerate(pairs)]
    for copy in copies:
        copy.start()
    return copies


def prelude(
    where, table, buckets, rows_far, gains, upstream_far, w_out_far,
    act, d_att, master, rows, upstream, w_out, line_ref, sems,
):
    copies = fetch(((rows_far, rows), (upstream_far, upstream), (w_out_far, w_out)), sems)
    head = where[0]
    count = buckets.shape[1]
    column = lax.broadcasted_iota(jnp.int32, table.shape, 1) == head
    column = jnp.sum(jnp.where(column, table[...], 0.0), axis=1, keepdims=True)
    line_ref[...] = jnp.zeros(line_ref.shape, F32)
    bucket = lax.broadcasted_iota(jnp.int32, (table.shape[0], count), 0)
    line_ref[:, :count] = jnp.sum(
        jnp.where(buckets[...] == bucket, column, 0.0), axis=0, keepdims=True
    )
    line = line_ref[...]
    span = line.shape[1]
    for r in range(0, 128, 8):
        master[r : r + 8, :] = pltpu.roll(
            jnp.broadcast_to(line, (8, span)), (span - 127 + r) % span, 1, stride=1, stride_axis=0
        )
    gain = gains[0:1, :]
    copies[0].wait()

    def body(r):
        act[pl.ds(r, STEP), :] = activate(rows[pl.ds(r, STEP), :].astype(F32), gain).astype(BF16)

    loop(rows.shape[0], body)
    copies[1].wait()
    copies[2].wait()
    d_att[...] = contract(upstream[...], w_out[...], 1, 1).astype(BF16)


def forward(
    where, dil, left, right, rows, act, d_att, taps, gains, order, upstream, wq_far, wk_far, wv_far,
    m0, m1, m2, m3, both, z, near,
    x_ext, a_ext, b_ext, slots, moved1, moved2, normed, w_query, w_key, w_value, sems,
):
    copies = fetch(((wq_far, w_query), (wk_far, w_key), (wv_far, w_value)), sems)
    iy, iseq, nseq = where[0], where[1], where[2]
    tok = rows.shape[0]
    x_ext[0:HALO, :] = left[...]
    x_ext[HALO : HALO + tok, :] = rows[...]
    x_ext[HALO + tok :, :] = right[...]
    a_ext[HALO : HALO + tok, :] = act[...]
    gain = gains[0:1, :]
    for r in [*range(0, HALO, STEP), *range(HALO + tok, 2 * HALO + tok, STEP)]:
        a_ext[r : r + STEP, :] = activate(x_ext[r : r + STEP, :].astype(F32), gain).astype(BF16)
    gap, wide = dil[0], dil[1]
    first, last = iseq == 0, iseq == nseq - 1
    count = tok + 2 * DMAX
    gain = gains[1:2, :]
    move(moved1, a_ext, gap)

    def middle(r):
        center = pl.ds(pl.multiple_of(r + DMAX, STEP), STEP)
        mixed = tapped(taps, 0, moved1, a_ext[center, :].astype(F32), r)
        hidden = (x_ext[center, :].astype(F32) + mixed).astype(BF16)
        near[pl.ds(r, STEP), :] = hidden
        keep = inside(r, first, last, DMAX, count)
        b_ext[pl.ds(r, STEP), :] = (activate(hidden.astype(F32), gain) * keep).astype(BF16)

    loop(count, middle)
    last_gain = gains[2:3, :]
    move(moved2, b_ext, wide)

    def top(r):
        center = pl.ds(pl.multiple_of(r + DMAX, STEP), STEP)
        mixed = tapped(taps, 1, moved2, b_ext[center, :].astype(F32), r)
        hidden = (near[center, :].astype(F32) + mixed).astype(BF16)
        z[pl.ds(r, STEP), :] = hidden
        hidden = hidden.astype(F32)
        normed[pl.ds(r, STEP), :] = (hidden * inverse_norm(hidden) * last_gain).astype(BF16)

    loop(tok, top)
    field = normed[...]
    for copy in copies:
        copy.wait()
    queries = (rounded(contract(field, w_query[...], 1, 0)) * KEY**-0.5).astype(BF16)
    keys = contract(field, w_key[...], 1, 0).astype(BF16)
    values = contract(field, w_value[...], 1, 0).astype(BF16)
    for h in range(HEADS):
        k, v = slice(h * KEY, (h + 1) * KEY), slice(h * VALUE, (h + 1) * VALUE)
        slots[lax.rem(h - iy + HEADS, HEADS)] = jnp.concatenate(
            [keys[:, k], values[:, v], queries[:, k], d_att[:, v]], axis=1
        )
    for i, out in enumerate((m0, m1, m2, m3)):
        out[...] = slots[i]
    reorder(order, normed, both, 0)
    reorder(order, upstream, both, normed.shape[1])


def slopes(rows, near, gains, slope0, slope1):
    def fill(source, gain, out):
        def body(r):
            held = source[pl.ds(r, STEP), :].astype(F32)
            field = held * inverse_norm(held) * gain
            below = 0.5 * (1.0 + lax.erf(field * ROOT_HALF))
            out[pl.ds(r, STEP), :] = (
                below + field * (ROOT_TWO_PI * jnp.exp(-0.5 * field * field))
            ) * gain

        loop(source.shape[0], body)

    fill(near, gains[1:2, :], slope1)
    fill(rows, gains[0:1, :], slope0)


def attend(
    where, m0, m1, m2, m3, kv1, kv2, kv3, master,
    t0, t1, t2, t3, own, far, give, ask, kv0, score, pull, soft, d_soft,
):
    iy, c = where[0], where[3]
    tok = m0.shape[0]
    many = HEADS * tok
    for i, m in enumerate((m0, m1, m2, m3)):
        kv0[i * tok : (i + 1) * tok, :] = m[:, :WIDE]
        ask[i * tok : (i + 1) * tok, :] = m[:, WIDE:]
    both = ask[...]
    lane = lax.broadcasted_iota(jnp.int32, (1, WIDE), 1)
    is_key = lane < KEY
    zero = jnp.zeros_like(both)
    queries = jnp.where(is_key, both, zero)
    d_att = jnp.where(is_key, zero, both)
    blocks = (kv0, kv1, kv2, kv3)
    bands = [lax.rem(iy - i + HEADS, HEADS) for i in range(HEADS)]
    top = None
    for j, block in enumerate(blocks):
        other = jnp.bitwise_xor(c, j)
        for i in range(HEADS):
            at = j * many + i * tok
            part = contract(block[i * tok : (i + 1) * tok, :], queries, 1, 1)
            bias = jnp.concatenate(
                [
                    master[:, pl.ds(pl.multiple_of((4 * (q - bands[i]) + c - other + 15) * tok, tok), tok)]
                    for q in bands
                ],
                axis=1,
            )
            part = part + bias
            score[at : at + tok, :] = part
            peak = jnp.max(part, axis=0, keepdims=True)
            top = peak if top is None else jnp.maximum(top, peak)
    total = jnp.zeros_like(top)
    for at in range(0, 4 * many, tok):
        part = jnp.exp(score[at : at + tok, :] - top)
        score[at : at + tok, :] = part
        total = total + jnp.sum(part, axis=0, keepdims=True)
    scale = 1.0 / total
    delta = jnp.zeros_like(top)
    for j, block in enumerate(blocks):
        for i in range(HEADS):
            at = j * many + i * tok
            probs = score[at : at + tok, :] * scale
            score[at : at + tok, :] = probs
            soft[at : at + tok, :] = probs.astype(BF16)
            part = contract(block[i * tok : (i + 1) * tok, :], d_att, 1, 1)
            pull[at : at + tok, :] = part
            delta = delta + jnp.sum(part * probs, axis=0, keepdims=True)
    for at in range(0, 4 * many, tok):
        d_soft[at : at + tok, :] = (
            score[at : at + tok, :] * (pull[at : at + tok, :] - delta)
        ).astype(BF16)
    att = jnp.zeros((WIDE, many), F32)
    d_query = jnp.zeros((WIDE, many), F32)
    for j, block in enumerate(blocks):
        held = block[...]
        span = slice(j * many, (j + 1) * many)
        att = att + contract(held, soft[span, :], 0, 0)
        d_query = d_query + contract(held, d_soft[span, :], 0, 0)
        d_kv = jnp.where(
            is_key, contract(d_soft[span, :], both, 1, 0), contract(soft[span, :], both, 1, 0)
        )
        if j == 0:
            own[...] = d_kv
        elif j == 2:
            far[...] = d_kv
        else:
            give[(j // 2) * many : (j // 2 + 1) * many, :] = d_kv.astype(BF16)
    side = lax.broadcasted_iota(jnp.int32, (WIDE, 1), 0) < KEY
    mixed = jnp.where(side, d_query * KEY**-0.5, att).T.astype(BF16)
    for i, t in enumerate((t0, t1, t2, t3)):
        t[...] = mixed[i * tok : (i + 1) * tok, :]


def first_sum(own, far, got, near, send):
    many = own.shape[0]
    near[...] = own[...] + got[:many, :].astype(F32)
    send[...] = (far[...] + got[many:, :].astype(F32)).astype(BF16)


def second_sum(near, got, d0, d1, d2, d3):
    total = (near[...] + got[...].astype(F32)).astype(BF16)
    tok = d0.shape[0]
    for i, d in enumerate((d0, d1, d2, d3)):
        d[...] = total[i * tok : (i + 1) * tok, :]


def gathered(slots, parts, iy):
    for i, part in enumerate(parts):
        slots[lax.rem(iy + i, HEADS)] = part[...]


def heads_of(slots, low, high):
    return jnp.concatenate([slots[h][:, low:high] for h in range(HEADS)], axis=1)


def project(where, t0, t1, t2, t3, z, w_out, w_query, result, g_query, slots):
    gathered(slots, (t0, t1, t2, t3), where[0])
    att = heads_of(slots, KEY, WIDE)
    result[...] = (z[...].astype(F32) + contract(att, w_out[...], 1, 0)).astype(BF16)
    g_query[...] = contract(heads_of(slots, 0, KEY), w_query[...], 1, 1)


def pull_norm(held, scaled):
    s = inverse_norm(held)
    return s * scaled - held * (s * s * s) * jnp.mean(scaled * held, axis=1, keepdims=True)


def grad_top(where, d0, d1, d2, d3, g_query, z, upstream, w_key, w_value, gains, out, slots, total):
    gathered(slots, (d0, d1, d2, d3), where[0])
    total[...] = (
        g_query[...]
        + contract(heads_of(slots, 0, KEY), w_key[...], 1, 1)
        + contract(heads_of(slots, KEY, WIDE), w_value[...], 1, 1)
    )
    gain = gains[2:3, :]

    def body(r):
        at = pl.ds(r, STEP)
        grad = pull_norm(z[at, :].astype(F32), total[at, :] * gain)
        out[at, :] = (upstream[at, :].astype(F32) + grad).astype(BF16)

    loop(z.shape[0], body)


def backward(
    where, dil, left, right, grad, slope0, slope1, rows, near, taps, out, g_ext, p_ext, moved1, moved2
):
    iseq, nseq = where[1], where[2]
    tok = rows.shape[0]
    first, last = iseq == 0, iseq == nseq - 1
    g_ext[0:HALO, :] = left[...]
    g_ext[HALO : HALO + tok, :] = grad[...]
    g_ext[HALO + tok :, :] = right[...]
    gap, wide = dil[0], dil[1]
    count = tok + 2 * DMAX

    move(moved1, g_ext, wide)

    def middle(r):
        center = g_ext[pl.ds(pl.multiple_of(r + DMAX, STEP), STEP), :].astype(F32)
        mixed = tapped(taps, 1, moved1, center, r, 2, 0)
        at = pl.ds(r, STEP)
        held = pull_norm(near[at, :].astype(F32), mixed * slope1[at, :])
        keep = inside(r, first, last, DMAX, count)
        p_ext[at, :] = ((center + held) * keep).astype(BF16)

    loop(count, middle)
    move(moved2, p_ext, gap)

    def bottom(r):
        center = p_ext[pl.ds(pl.multiple_of(r + DMAX, STEP), STEP), :].astype(F32)
        mixed = tapped(taps, 0, moved2, center, r, 2, 0)
        at = pl.ds(r, STEP)
        held = pull_norm(rows[at, :].astype(F32), mixed * slope0[at, :])
        out[at, :] = (center + held).astype(BF16)

    loop(tok, bottom)


def weigh(
    sizes, where, fields, t0, t1, t2, t3, d0, d1, d2, d3, keep, give, t_all, d_all, halves
):
    iy, core = where[0], where[4]
    nxh, nz, unit = sizes
    tok = t0.shape[0]
    for i, (t, d) in enumerate(zip((t0, t1, t2, t3), (d0, d1, d2, d3))):
        at = pl.ds(pl.multiple_of(lax.rem(iy - i + HEADS, HEADS) * tok, tok), tok)
        t_all[at, :] = t[...]
        d_all[at, :] = d[...]
    is_key = lax.broadcasted_iota(jnp.int32, (1, WIDE), 1) < KEY
    chan = fields.shape[1] // 2
    size = chan // (4 * nxh * nz)
    for low in range(0, chan, unit):
        left = fields[:, low : low + unit]
        first = jnp.where(
            is_key,
            contract(left, t_all[...], 0, 0),
            contract(fields[:, chan + low : chan + low + unit], t_all[...], 0, 0),
        )
        second = contract(left, d_all[...], 0, 0)
        for block in range(unit // size):
            place = low // size + block
            line, xl, side = place // 4, place // 2 % 2, place % 2
            xh, z = line // nz, line % nz
            to = ((xl * nxh + xh) * nz + z) * size
            rows = slice(block * size, (block + 1) * size)
            halves[side, to : to + size, :WIDE] = first[rows, :]
            halves[side, to : to + size, WIDE:] = second[rows, :]
    keep[...] = halves[core]
    give[...] = halves[1 - core].astype(BF16)


def fold(places, parts, *refs):
    where, keep, got = refs[0], refs[1], refs[2 : 2 + places[1]]
    own, sends, held = refs[2 + places[1]], refs[3 + places[1] : -1], refs[-1]
    total = keep[...]
    for g in got:
        total = total + g[...].astype(F32)
    held[...] = total
    size = own.shape[0]
    for i, out in enumerate((own, *sends)):
        at = parts(where, i)
        out[...] = held[pl.ds(pl.multiple_of(at * size, 8), size), :].astype(out.dtype)


def fold_call(keep, got, where, parts, count, limit=24):
    rows, width = keep.shape
    size = rows // count
    body = functools.partial(fold, (None, len(got)), parts)
    outs = [((size, width), F32)] + [((size, width), BF16)] * (count - 1)
    return call(
        body, outs, (where, keep, *got), [pltpu.VMEM((rows, width), F32)], smem=(0,), cost=0.3, limit=limit
    )


def last_fold(where, keep, *refs):
    got, outs, slots = refs[:-5], refs[-5:-1], refs[-1]
    total = keep[...]
    for g in got:
        total = total + g[...].astype(F32)
    size = total.shape[0] // 4
    for i in range(4):
        slots[i] = total[i * size : (i + 1) * size, :]
    for i, out in enumerate(outs):
        out[...] = slots[lax.rem(where[0] + i, 4)]


def arrange(where, g0, g1, g2, g3, out, slots):
    iy = where[0]
    for i, g in enumerate((g0, g1, g2, g3)):
        slots[lax.rem(iy - i + HEADS, HEADS)] = g[...]
    scale = 1.0 / where[5].astype(F32)
    keys = HEADS * KEY
    for h in range(HEADS):
        held = slots[h] * scale
        out[:, h * KEY : (h + 1) * KEY] = held[:, :KEY]
        low = 2 * keys + HEADS * VALUE + h * VALUE
        out[:, low : low + VALUE] = held[:, KEY:WIDE]
        out[:, keys + h * KEY : keys + (h + 1) * KEY] = held[:, WIDE : WIDE + KEY]
        low = 2 * keys + h * VALUE
        out[:, low : low + VALUE] = held[:, WIDE + KEY :]


def column_order(unit, size):
    place = np.arange(unit)
    group, rest = place // (16 * size), place % (16 * size)
    c, y, j = rest // (4 * size), rest // size % 4, rest % size
    return (group * 16 * size + y * 4 * size + c * size + j).astype(np.int32)[None]


def shift(array, axis, count, step):
    return lax.ppermute(array, axis, [(i, (i + step) % count) for i in range(count)])


def flip(array, axis):
    return lax.ppermute(array, axis, [(0, 1), (1, 0)])


def halo(rows, nseq):
    width = HALO
    left = lax.ppermute(rows[-width:], SEQ, [(i, i + 1) for i in range(nseq - 1)])
    right = lax.ppermute(rows[:width], SEQ, [(i + 1, i) for i in range(nseq - 1)])
    return left, right


def local(
    sizes, inputs, dilations, taps, gains, bias_table, buckets, w_query, w_key, w_value, w_out, cotangent
):
    nxh, nz, ny = sizes
    nseq = ny * 4
    rows, upstream = inputs[0], cotangent[0]
    tok, chan = rows.shape
    iy, ixl, icore = lax.axis_index("y"), lax.axis_index("xl"), lax.axis_index("core")
    ixh, iz = lax.axis_index("xh"), lax.axis_index("z")
    c = ixl * 2 + icore
    loci = inputs.shape[0] * nxh * nz
    where = jnp.stack(
        [iy, iy * 4 + c, jnp.int32(nseq), c, icore, jnp.int32(loci), ixl, ixh, iz]
    ).astype(jnp.int32)
    big = (tok, chan)

    left, right = halo(rows, nseq)
    unit = math.lcm(16 * (chan // (nxh * nz * nseq)), 128)
    order = jnp.asarray(column_order(unit, chan // (nxh * nz * nseq)))
    size = buckets.shape[0]
    act, d_att, master = call(
        prelude,
        [(big, BF16), ((tok, HEADS * VALUE), BF16), ((128, size + 1), F32)],
        (where, bias_table, buckets[None], rows, gains, upstream, w_out),
        [pltpu.VMEM(big, BF16), pltpu.VMEM(big, BF16), pltpu.VMEM(w_out.shape, BF16),
         pltpu.VMEM((1, size + 1), F32), pltpu.SemaphoreType.DMA((3,))],
        smem=(0,),
        hbm=(3, 5, 6),
        cost=3,
    )
    ext = (tok + 2 * HALO, chan)
    mid = (tok + 2 * DMAX, chan)
    shifted = [pltpu.VMEM((2 * mid[0], chan), F32), pltpu.VMEM((2 * tok, chan), F32)]
    *ms, fields, z, near = call(
        forward,
        [((tok, 2 * WIDE), BF16)] * 4 + [((tok, 2 * chan), BF16), (big, BF16), (mid, BF16)],
        (where, dilations, left, right, rows, act, d_att, taps, gains, order, upstream, w_query, w_key, w_value),
        [pltpu.VMEM(ext, BF16), pltpu.VMEM(ext, BF16), pltpu.VMEM(mid, BF16),
         pltpu.VMEM((HEADS, tok, 2 * WIDE), BF16), *shifted, pltpu.VMEM(big, BF16),
         *(pltpu.VMEM(w.shape, BF16) for w in (w_query, w_key, w_value)), pltpu.SemaphoreType.DMA((3,))],
        smem=(0, 1),
        hbm=(11, 12, 13),
        cost=6,
    )
    ms = [ms[0]] + [shift(ms[k], "y", ny, k) for k in (1, 2, 3)]
    kv0 = jnp.concatenate([m[:, :WIDE] for m in ms], axis=0)
    kv2 = flip(kv0, "xl")
    kv1 = flip(kv0, "core")
    kv3 = flip(kv2, "core")
    slope0, slope1 = call(slopes, [(big, F32), (mid, F32)], (rows, near, gains), cost=4)
    kv3, slope0, slope1 = lax.optimization_barrier((kv3, slope0, slope1))
    fields = lax.all_gather(fields, "y", axis=0, tiled=True)
    many = HEADS * tok
    *ts, own, far, give = call(
        attend,
        [((tok, WIDE), BF16)] * 4 + [((many, WIDE), F32)] * 2 + [((2 * many, WIDE), BF16)],
        (where, *ms, kv1, kv2, kv3, master),
        [pltpu.VMEM((many, WIDE), BF16), pltpu.VMEM((many, WIDE), BF16),
         pltpu.VMEM((4 * many, many), F32), pltpu.VMEM((4 * many, many), F32),
         pltpu.VMEM((4 * many, many), BF16), pltpu.VMEM((4 * many, many), BF16)],
        smem=(0,),
        cost=10,
        limit=24,
    )
    got = flip(give, "core")
    back = [ts[0]] + [shift(ts[k], "y", ny, -k) for k in (1, 2, 3)]
    own, far = call(
        first_sum, [((many, WIDE), F32), ((many, WIDE), BF16)], (own, far, got), cost=0.5
    )
    got = flip(far, "xl")
    got, *back = lax.optimization_barrier((got, *back))
    ds = call(second_sum, [((tok, WIDE), BF16)] * 4, (own, got), cost=0.5)
    back_d = [ds[0]] + [shift(ds[k], "y", ny, -k) for k in (1, 2, 3)]
    result, g_query = call(
        project,
        [(big, BF16), (big, F32)],
        (where, *back, z, w_out, w_query),
        [pltpu.VMEM((HEADS, tok, WIDE), BF16)],
        smem=(0,),
        cost=2,
    )
    half = chan // 2
    keep, give = call(
        functools.partial(weigh, (nxh, nz, unit)),
        [((half, 2 * WIDE), F32), ((half, 2 * WIDE), BF16)],
        (where, fields, *ts, *ds),
        [pltpu.VMEM((many, WIDE), BF16), pltpu.VMEM((many, WIDE), BF16),
         pltpu.VMEM((2, half, 2 * WIDE), F32)],
        smem=(0,),
        cost=4,
        limit=32,
    )
    (grad,) = call(
        grad_top,
        [(big, BF16)],
        (where, *back_d, g_query, z, upstream, w_key, w_value, gains),
        [pltpu.VMEM((HEADS, tok, WIDE), BF16), pltpu.VMEM(big, F32)],
        smem=(0,),
        cost=3,
    )
    left, right = halo(grad, nseq)
    got = flip(give, "core")
    got, grad = lax.optimization_barrier((got, grad))
    (input_grad,) = call(
        backward,
        [(big, BF16)],
        (where, dilations, left, right, grad, slope0, slope1, rows, near, taps),
        [pltpu.VMEM(ext, BF16), pltpu.VMEM(mid, BF16), *shifted],
        smem=(0, 1),
        cost=4,
    )

    pairs = [(a, b) for b in range(nxh) for a in range(2)]

    def ring_part(where, i):
        a, b = pairs[i]
        return jnp.bitwise_xor(where[6], a) * nxh + jnp.bitwise_xor(where[7], b)

    keep, *sends = fold_call(keep, [got], where, ring_part, len(pairs))
    got = []
    for (a, b), send in zip(pairs[1:], sends):
        order = [(s, ((s // 2) ^ b) * 2 + ((s % 2) ^ a)) for s in range(2 * nxh)]
        got.append(lax.ppermute(send, ("xh", "xl"), order))
    result, *got = lax.optimization_barrier((result, *got))

    def line_part(where, i):
        return lax.rem(where[8] + i, nz)

    keep, *sends = fold_call(keep, got, where, line_part, nz)
    input_grad, *sends = lax.optimization_barrier((input_grad, *sends))
    got = [shift(send, "z", nz, k + 1) for k, send in enumerate(sends)]
    size = keep.shape[0] // 4
    parts = call(
        last_fold,
        [((size, 2 * WIDE), F32)] * 4,
        (where, keep, *got),
        [pltpu.VMEM((4, size, 2 * WIDE), F32)],
        smem=(0,),
        cost=0.3,
    )
    parts = [parts[0]] + [shift(parts[k], "y", ny, k) for k in (1, 2, 3)]
    (weight_sum,) = call(
        arrange,
        [((size, 8 * WIDE), F32)],
        (where, *parts),
        [pltpu.VMEM((HEADS, size, 2 * WIDE), F32)],
        smem=(0,),
        cost=0.1,
    )
    return (result[None], input_grad[None], weight_sum)


def solution(mesh):
    nseq = mesh.shape["seq"]
    ny = nseq // 4
    ndp = mesh.shape["dp"]
    nxh = 2 if ndp % 2 == 0 else 1
    sizes = (nxh, ndp // nxh, ny)
    fine = Mesh(mesh.devices.reshape(*sizes, 2, 2), EVERY)
    cells = P(("xh", "z"), SEQ, None)
    return jax.shard_map(
        functools.partial(local, sizes),
        mesh=fine,
        in_specs=(cells, *(P() for _ in range(9)), cells),
        out_specs=(cells, cells, P(EVERY, None)),
        check_vma=False,
    )
```

```python
import functools

import jax
import jax.numpy as jnp
import numpy as np
from jax import lax
from jax.experimental import pallas as pl
from jax.experimental.pallas import tpu as pltpu
from jax.sharding import Mesh, PartitionSpec as P

HEADS = 4
KEY = 64
VALUE = 192
WIDE = KEY + VALUE
BLOCKS = 2
DMAX = 16
HALO = BLOCKS * DMAX
EPS = 1e-06
STEP = 16
LARGE = 60
SEQ = ("y", "xl", "core")
EVERY = ("xh", "z", "y", "xl", "core")
F32 = jnp.float32
BF16 = jnp.bfloat16
ROOT_HALF = 0.7071067811865476
ROOT_TWO_PI = 0.3989422804014327


def contract(left, right, left_dim, right_dim):
    return lax.dot_general(
        left, right, (((left_dim,), (right_dim,)), ((), ())), preferred_element_type=F32
    )


def call(body, outs, args, scratch=(), smem=(), hbm=(), us=1.0, limit=24):
    spaces = [
        pltpu.SMEM if i in smem else pltpu.HBM if i in hbm else pltpu.VMEM for i in range(len(args))
    ]
    return pl.pallas_call(
        body,
        out_shape=tuple(jax.ShapeDtypeStruct(s, d) for s, d in outs),
        in_specs=[pl.BlockSpec(memory_space=s) for s in spaces],
        out_specs=tuple(pl.BlockSpec(memory_space=pltpu.VMEM) for _ in outs),
        scratch_shapes=list(scratch),
        compiler_params=pltpu.CompilerParams(vmem_limit_bytes=limit << 20),
        cost_estimate=pl.CostEstimate(
            flops=1000, bytes_accessed=int(us * 3.6e6), transcendentals=0
        ),
        name=body.__name__ if hasattr(body, "__name__") else body.func.__name__,
    )(*args)


def inverse_norm(rows):
    return lax.rsqrt(jnp.mean(rows * rows, axis=1, keepdims=True) + EPS)


def activate(rows, gain):
    field = rows * inverse_norm(rows) * gain
    return 0.5 * field * (1.0 + lax.erf(field * ROOT_HALF))


def rounded(rows):
    return rows.astype(BF16).astype(F32)


def loop(count, body):
    def step(i, carry):
        body(pl.multiple_of(i * STEP, STEP))
        return carry

    lax.fori_loop(0, count // STEP, step, 0)


def inside(start, first, last, edge, count):
    out = (first & (start < edge)) | (last & (start >= count - edge))
    return jnp.where(out, 0.0, 1.0)


def move(moved, source, gap):
    count, total = moved.shape[0] // 2, source.shape[0]
    row = lax.broadcasted_iota(jnp.int32, (count, total), 0)
    col = lax.broadcasted_iota(jnp.int32, (count, total), 1)
    held = source[...]
    for i, at in enumerate((DMAX - gap, DMAX + gap)):
        pick = jnp.where(col == row + at, 1.0, 0.0).astype(BF16)
        moved[i * count : (i + 1) * count, :] = contract(pick, held, 1, 0)


def tapped(taps, first, moved, center, r, low=0, high=2):
    count = moved.shape[0] // 2
    return (
        taps[low, first : first + 1, :] * moved[pl.ds(r, STEP), :]
        + taps[1, first : first + 1, :] * center
        + taps[high, first : first + 1, :] * moved[pl.ds(pl.multiple_of(count + r, STEP), STEP), :]
    )


def shuffle(where, order, normed, upstream, f0, f1, f2, f3, slots):
    unit = order.shape[1]
    chan = normed.shape[1]
    row = lax.broadcasted_iota(jnp.int32, (unit, unit), 0)
    pick = jnp.where(row == order[...], 1.0, 0.0).astype(BF16)
    share = unit // 4
    to = 0
    for source in (normed, upstream):
        for low in range(0, chan, unit):
            mixed = contract(source[:, low : low + unit], pick, 1, 0).astype(BF16)
            for y in range(4):
                slots[lax.rem(y - where[0] + 4, 4), :, to : to + share] = mixed[
                    :, y * share : (y + 1) * share
                ]
            to += share
    for i, out in enumerate((f0, f1, f2, f3)):
        out[...] = slots[i]


def fetch(pairs, sems):
    copies = [pltpu.make_async_copy(a, b, sems.at[i]) for i, (a, b) in enumerate(pairs)]
    for copy in copies:
        copy.start()
    return copies


def prelude(
    where, table, buckets, rows_far, gains, upstream_far, w_out_far,
    act, d_att, master, rows, upstream, w_out, line_ref, sems,
):
    copies = fetch(((rows_far, rows), (upstream_far, upstream), (w_out_far, w_out)), sems)
    head = where[0]
    count = buckets.shape[1]
    bucket = lax.broadcasted_iota(jnp.int32, (table.shape[1], count), 0)
    line = lax.dot_general(
        table[...],
        jnp.where(buckets[...] == bucket, 1.0, 0.0),
        (((1,), (0,)), ((), ())),
        precision=lax.Precision.HIGHEST,
        preferred_element_type=F32,
    )
    chosen = lax.broadcasted_iota(jnp.int32, line.shape, 0) == head
    line_ref[...] = jnp.zeros(line_ref.shape, F32)
    line_ref[:, :count] = jnp.sum(jnp.where(chosen, line, 0.0), axis=0, keepdims=True)
    line = line_ref[...]
    span = line.shape[1]
    for r in range(0, 128, 8):
        master[r : r + 8, :] = pltpu.roll(
            jnp.broadcast_to(line, (8, span)), (span - 127 + r) % span, 1, stride=1, stride_axis=0
        )
    gain = gains[0:1, :]
    copies[0].wait()

    def body(r):
        act[pl.ds(r, STEP), :] = activate(rows[pl.ds(r, STEP), :].astype(F32), gain).astype(BF16)

    loop(rows.shape[0], body)
    copies[1].wait()
    copies[2].wait()
    d_att[...] = contract(upstream[...], w_out[...], 1, 1).astype(BF16)


def forward(
    where, dil, left, right, rows, act, d_att, taps, gains, wq_far, wk_far, wv_far,
    m0, m1, m2, m3, normed, z, near,
    x_ext, a_ext, b_ext, slots, moved1, moved2, w_query, w_key, w_value, sems,
):
    copies = fetch(((wq_far, w_query), (wk_far, w_key), (wv_far, w_value)), sems)
    iy, iseq, nseq = where[0], where[1], where[2]
    tok = rows.shape[0]
    x_ext[0:HALO, :] = left[...]
    x_ext[HALO : HALO + tok, :] = rows[...]
    x_ext[HALO + tok :, :] = right[...]
    a_ext[HALO : HALO + tok, :] = act[...]
    gain = gains[0:1, :]
    for r in [*range(0, HALO, STEP), *range(HALO + tok, 2 * HALO + tok, STEP)]:
        a_ext[r : r + STEP, :] = activate(x_ext[r : r + STEP, :].astype(F32), gain).astype(BF16)
    gap, wide = dil[0], dil[1]
    first, last = iseq == 0, iseq == nseq - 1
    count = tok + 2 * DMAX
    gain = gains[1:2, :]
    move(moved1, a_ext, gap)

    def middle(r):
        center = pl.ds(pl.multiple_of(r + DMAX, STEP), STEP)
        mixed = tapped(taps, 0, moved1, a_ext[center, :].astype(F32), r)
        hidden = (x_ext[center, :].astype(F32) + mixed).astype(BF16)
        near[pl.ds(r, STEP), :] = hidden
        keep = inside(r, first, last, DMAX, count)
        b_ext[pl.ds(r, STEP), :] = (activate(hidden.astype(F32), gain) * keep).astype(BF16)

    loop(count, middle)
    last_gain = gains[2:3, :]
    move(moved2, b_ext, wide)

    def top(r):
        center = pl.ds(pl.multiple_of(r + DMAX, STEP), STEP)
        mixed = tapped(taps, 1, moved2, b_ext[center, :].astype(F32), r)
        hidden = (near[center, :].astype(F32) + mixed).astype(BF16)
        z[pl.ds(r, STEP), :] = hidden
        hidden = hidden.astype(F32)
        normed[pl.ds(r, STEP), :] = (hidden * inverse_norm(hidden) * last_gain).astype(BF16)

    loop(tok, top)
    field = normed[...]
    for copy in copies:
        copy.wait()
    queries = (rounded(contract(field, w_query[...], 1, 0)) * KEY**-0.5).astype(BF16)
    keys = contract(field, w_key[...], 1, 0).astype(BF16)
    values = contract(field, w_value[...], 1, 0).astype(BF16)
    for h in range(HEADS):
        k, v = slice(h * KEY, (h + 1) * KEY), slice(h * VALUE, (h + 1) * VALUE)
        slots[lax.rem(h - iy + HEADS, HEADS)] = jnp.concatenate(
            [keys[:, k], values[:, v], queries[:, k], d_att[:, v]], axis=1
        )
    for i, out in enumerate((m0, m1, m2, m3)):
        out[...] = slots[i]


def slopes(rows, near, gains, slope0, slope1):
    def fill(source, gain, out):
        def body(r):
            held = source[pl.ds(r, STEP), :].astype(F32)
            field = held * inverse_norm(held) * gain
            below = 0.5 * (1.0 + lax.erf(field * ROOT_HALF))
            out[pl.ds(r, STEP), :] = (
                below + field * (ROOT_TWO_PI * jnp.exp(-0.5 * field * field))
            ) * gain

        loop(source.shape[0], body)

    fill(near, gains[1:2, :], slope1)
    fill(rows, gains[0:1, :], slope0)


def attend(
    where, m0, m1, m2, m3, kv1, kv2, kv3, master,
    t, own, far, give, ask, kv0, score, pull, soft, d_soft,
):
    iy, c = where[0], where[3]
    tok = m0.shape[0]
    many = HEADS * tok
    for i, m in enumerate((m0, m1, m2, m3)):
        kv0[i * tok : (i + 1) * tok, :] = m[:, :WIDE]
        ask[i * tok : (i + 1) * tok, :] = m[:, WIDE:]
    both = ask[...]
    lane = lax.broadcasted_iota(jnp.int32, (1, WIDE), 1)
    is_key = lane < KEY
    zero = jnp.zeros_like(both)
    queries = jnp.where(is_key, both, zero)
    d_att = jnp.where(is_key, zero, both)
    blocks = (kv0, kv1, kv2, kv3)
    bands = [lax.rem(iy - i + HEADS, HEADS) for i in range(HEADS)]
    top = None
    for j, block in enumerate(blocks):
        other = jnp.bitwise_xor(c, j)
        for i in range(HEADS):
            at = j * many + i * tok
            part = contract(block[i * tok : (i + 1) * tok, :], queries, 1, 1)
            bias = jnp.concatenate(
                [
                    master[:, pl.ds(pl.multiple_of((4 * (q - bands[i]) + c - other + 15) * tok, tok), tok)]
                    for q in bands
                ],
                axis=1,
            )
            part = part + bias
            score[at : at + tok, :] = part
            peak = jnp.max(part, axis=0, keepdims=True)
            top = peak if top is None else jnp.maximum(top, peak)
    total = jnp.zeros_like(top)
    for at in range(0, 4 * many, tok):
        part = jnp.exp(score[at : at + tok, :] - top)
        score[at : at + tok, :] = part
        total = total + jnp.sum(part, axis=0, keepdims=True)
    scale = 1.0 / total
    delta = jnp.zeros_like(top)
    for j, block in enumerate(blocks):
        for i in range(HEADS):
            at = j * many + i * tok
            probs = score[at : at + tok, :] * scale
            score[at : at + tok, :] = probs
            soft[at : at + tok, :] = probs.astype(BF16)
            part = contract(block[i * tok : (i + 1) * tok, :], d_att, 1, 1)
            pull[at : at + tok, :] = part
            delta = delta + jnp.sum(part * probs, axis=0, keepdims=True)
    for at in range(0, 4 * many, tok):
        d_soft[at : at + tok, :] = (
            score[at : at + tok, :] * (pull[at : at + tok, :] - delta)
        ).astype(BF16)
    att = jnp.zeros((WIDE, many), F32)
    d_query = jnp.zeros((WIDE, many), F32)
    for j, block in enumerate(blocks):
        held = block[...]
        span = slice(j * many, (j + 1) * many)
        att = att + contract(held, soft[span, :], 0, 0)
        d_query = d_query + contract(held, d_soft[span, :], 0, 0)
        d_kv = jnp.where(
            is_key, contract(d_soft[span, :], both, 1, 0), contract(soft[span, :], both, 1, 0)
        )
        if j == 0:
            own[...] = d_kv
        elif j == 2:
            far[...] = d_kv
        else:
            give[(j // 2) * many : (j // 2 + 1) * many, :] = d_kv.astype(BF16)
    side = lax.broadcasted_iota(jnp.int32, (WIDE, 1), 0) < KEY
    mixed = jnp.where(side, d_query * KEY**-0.5, att).T.astype(BF16)
    for i, band in enumerate(bands):
        t[pl.ds(pl.multiple_of(band * tok, tok), tok), :] = mixed[i * tok : (i + 1) * tok, :]


def first_sum(own, far, got, near, send):
    many = own.shape[0]
    near[...] = own[...] + got[:many, :].astype(F32)
    send[...] = (far[...] + got[many:, :].astype(F32)).astype(BF16)


def second_sum(where, near, got, total):
    held = (near[...] + got[...].astype(F32)).astype(BF16)
    tok = held.shape[0] // HEADS
    for i in range(HEADS):
        band = lax.rem(where[0] - i + HEADS, HEADS)
        total[pl.ds(pl.multiple_of(band * tok, tok), tok), :] = held[i * tok : (i + 1) * tok, :]


def gathered(slots, parts, iy):
    tok = slots.shape[1]
    for i, part in enumerate(parts):
        held = part[pl.ds(pl.multiple_of(iy * tok, tok), tok), :]
        slots[lax.rem(iy - i + HEADS, HEADS)] = held


def heads_of(slots, low, high):
    return jnp.concatenate([slots[h][:, low:high] for h in range(HEADS)], axis=1)


def project(where, t0, t1, t2, t3, z, w_out, w_query, result, g_query, slots):
    gathered(slots, (t0, t1, t2, t3), where[0])
    att = heads_of(slots, KEY, WIDE)
    result[...] = (z[...].astype(F32) + contract(att, w_out[...], 1, 0)).astype(BF16)
    g_query[...] = contract(heads_of(slots, 0, KEY), w_query[...], 1, 1)


def pull_norm(held, scaled):
    s = inverse_norm(held)
    return s * scaled - held * (s * s * s) * jnp.mean(scaled * held, axis=1, keepdims=True)


def grad_top(where, d0, d1, d2, d3, g_query, z, upstream, w_key, w_value, gains, out, slots, total):
    gathered(slots, (d0, d1, d2, d3), where[0])
    total[...] = (
        g_query[...]
        + contract(heads_of(slots, 0, KEY), w_key[...], 1, 1)
        + contract(heads_of(slots, KEY, WIDE), w_value[...], 1, 1)
    )
    gain = gains[2:3, :]

    def body(r):
        at = pl.ds(r, STEP)
        grad = pull_norm(z[at, :].astype(F32), total[at, :] * gain)
        out[at, :] = (upstream[at, :].astype(F32) + grad).astype(BF16)

    loop(z.shape[0], body)


def backward(
    where, dil, left, right, grad, slope0, slope1, rows, near, taps, out, g_ext, p_ext, moved1, moved2
):
    iseq, nseq = where[1], where[2]
    tok = rows.shape[0]
    first, last = iseq == 0, iseq == nseq - 1
    g_ext[0:HALO, :] = left[...]
    g_ext[HALO : HALO + tok, :] = grad[...]
    g_ext[HALO + tok :, :] = right[...]
    gap, wide = dil[0], dil[1]
    count = tok + 2 * DMAX

    move(moved1, g_ext, wide)

    def middle(r):
        center = g_ext[pl.ds(pl.multiple_of(r + DMAX, STEP), STEP), :].astype(F32)
        mixed = tapped(taps, 1, moved1, center, r, 2, 0)
        at = pl.ds(r, STEP)
        held = pull_norm(near[at, :].astype(F32), mixed * slope1[at, :])
        keep = inside(r, first, last, DMAX, count)
        p_ext[at, :] = ((center + held) * keep).astype(BF16)

    loop(count, middle)
    move(moved2, p_ext, gap)

    def bottom(r):
        center = p_ext[pl.ds(pl.multiple_of(r + DMAX, STEP), STEP), :].astype(F32)
        mixed = tapped(taps, 0, moved2, center, r, 2, 0)
        at = pl.ds(r, STEP)
        held = pull_norm(rows[at, :].astype(F32), mixed * slope0[at, :])
        out[at, :] = (center + held).astype(BF16)

    loop(tok, bottom)


def placed(out, cuts, head, held):
    nxh, nz0, size = cuts
    at = 0
    for xh in range(nxh):
        for core in range(2):
            for xl in range(2):
                for z0 in range(nz0):
                    to = ((xl * nxh + xh) * nz0 + z0) * size
                    out[core, head, to : to + size, :] = held[at : at + size, :]
                    at += size


def naturally(parts, out, low, iy):
    tok, width = parts[0].shape[0], out.shape[1]
    for i, part in enumerate(parts):
        band = lax.rem(iy - i + HEADS, HEADS)
        out[pl.ds(pl.multiple_of(band * tok, tok), tok), :] = part[:, low : low + width]


def weigh_first(cuts, where, f0, f1, f2, f3, t0, t1, t2, t3, out, n_all, u_all):
    iy = where[0]
    parts = (f0, f1, f2, f3)
    naturally(parts, n_all, 0, iy)
    naturally(parts, u_all, n_all.shape[1], iy)
    is_key = lax.broadcasted_iota(jnp.int32, (1, WIDE), 1) < KEY
    for i, t in enumerate((t0, t1, t2, t3)):
        held = t[...]
        first = jnp.where(
            is_key, contract(n_all[...], held, 0, 0), contract(u_all[...], held, 0, 0)
        )
        placed(out, cuts, lax.rem(iy - i + HEADS, HEADS), first)


def weigh_second(
    cuts, where, f0, f1, f2, f3, d0, d1, d2, d3, before, keep, give, n_all, out
):
    iy, core = where[0], where[4]
    naturally((f0, f1, f2, f3), n_all, 0, iy)
    for i, d in enumerate((d0, d1, d2, d3)):
        placed(out, cuts, lax.rem(iy - i + HEADS, HEADS), contract(n_all[...], d[...], 0, 0))
    keep[:, :, :WIDE] = before[core]
    keep[:, :, WIDE:] = out[core]
    give[:, :, :WIDE] = before[1 - core].astype(BF16)
    give[:, :, WIDE:] = out[1 - core].astype(BF16)


def fold(count, part_of, where, keep, *refs):
    got, outs, held = refs[:count], refs[count:-1], refs[-1]
    total = keep[...]
    for g in got:
        total = total + g[...].astype(F32)
    held[...] = total
    size = outs[0].shape[1]
    for i, out in enumerate(outs):
        at = part_of(where, i)
        out[...] = held[:, pl.ds(pl.multiple_of(at * size, 8), size), :].astype(out.dtype)


def fold_call(keep, got, where, part_of, count):
    heads, rows, width = keep.shape
    shape = (heads, rows // count, width)
    return call(
        functools.partial(fold, len(got), part_of),
        [(shape, F32)] + [(shape, BF16)] * (count - 1),
        (where, keep, *got),
        [pltpu.VMEM(keep.shape, F32)],
        smem=(0,),
        us=0.7,
    )


def last_fold(where, keep, got, *refs):
    outs, slots = refs[:-1], refs[-1]
    count = len(outs)
    total = keep[...] + got[...].astype(F32)
    size = total.shape[1] // count
    for i in range(count):
        slots[i] = total[:, i * size : (i + 1) * size, :]
    for i, out in enumerate(outs):
        out[...] = slots[lax.rem(where[9] + i, count)]


def arrange(where, *refs):
    held, out = refs[0][...], refs[-1]
    for g in refs[1:-1]:
        held = held + g[...]
    held = held * (1.0 / where[5].astype(F32))
    keys = HEADS * KEY
    for h in range(HEADS):
        part = held[h]
        out[:, h * KEY : (h + 1) * KEY] = part[:, :KEY]
        low = 2 * keys + HEADS * VALUE + h * VALUE
        out[:, low : low + VALUE] = part[:, KEY:WIDE]
        out[:, keys + h * KEY : keys + (h + 1) * KEY] = part[:, WIDE : WIDE + KEY]
        low = 2 * keys + h * VALUE
        out[:, low : low + VALUE] = part[:, WIDE + KEY :]


def column_order(nz0, nzh, size):
    y, core, xl, z0, zh, j = np.meshgrid(
        *(np.arange(n) for n in (4, 2, 2, nz0, nzh, size)), indexing="ij"
    )
    column = ((((zh * nz0 + z0) * 4 + y) * 2 + xl) * 2 + core) * size + j
    return column.reshape(1, -1).astype(np.int32)


def shift(array, axis, count, step):
    return lax.ppermute(array, axis, [(i, (i + step) % count) for i in range(count)])


def flip(array, axis):
    return lax.ppermute(array, axis, [(0, 1), (1, 0)])


def halo(rows, nseq):
    width = HALO
    left = lax.ppermute(rows[-width:], SEQ, [(i, i + 1) for i in range(nseq - 1)])
    right = lax.ppermute(rows[:width], SEQ, [(i + 1, i) for i in range(nseq - 1)])
    return left, right


def local(
    sizes, inputs, dilations, taps, gains, bias_table, buckets, w_query, w_key, w_value, w_out, cotangent
):
    nxh, nz, ny = sizes
    nz0 = 2 if nz % 2 == 0 else 1
    nzh = nz // nz0
    nseq = ny * 4
    rows, upstream = inputs[0], cotangent[0]
    tok, chan = rows.shape
    iy, ixl, icore = lax.axis_index("y"), lax.axis_index("xl"), lax.axis_index("core")
    ixh, iz = lax.axis_index("xh"), lax.axis_index("z")
    c = ixl * 2 + icore
    loci = inputs.shape[0] * nxh * nz
    where = jnp.stack(
        [iy, iy * 4 + c, jnp.int32(nseq), c, icore, jnp.int32(loci), ixl, ixh, iz % nz0, iz // nz0]
    ).astype(jnp.int32)
    taps = taps.transpose(1, 0, 2)
    big = (tok, chan)

    left, right = halo(rows, nseq)
    share = chan // (nxh * nz * nseq)
    order = jnp.asarray(column_order(nz0, nzh, share))
    size = buckets.shape[0]
    act, d_att, master = call(
        prelude,
        [(big, BF16), ((tok, HEADS * VALUE), BF16), ((128, size + 1), F32)],
        (where, bias_table.T, buckets[None], rows, gains, upstream, w_out),
        [pltpu.VMEM(big, BF16), pltpu.VMEM(big, BF16), pltpu.VMEM(w_out.shape, BF16),
         pltpu.VMEM((1, size + 1), F32), pltpu.SemaphoreType.DMA((3,))],
        smem=(0,),
        hbm=(3, 5, 6),
        us=3.6,
        limit=LARGE,
    )
    ext = (tok + 2 * HALO, chan)
    mid = (tok + 2 * DMAX, chan)
    shifted = [pltpu.VMEM((2 * mid[0], chan), F32), pltpu.VMEM((2 * tok, chan), F32)]
    *ms, normed, z, near = call(
        forward,
        [((tok, 2 * WIDE), BF16)] * 4 + [(big, BF16), (big, BF16), (mid, BF16)],
        (where, dilations, left, right, rows, act, d_att, taps, gains, w_query, w_key, w_value),
        [pltpu.VMEM(ext, BF16), pltpu.VMEM(ext, BF16), pltpu.VMEM(mid, BF16),
         pltpu.VMEM((HEADS, tok, 2 * WIDE), BF16), *shifted,
         *(pltpu.VMEM(w.shape, BF16) for w in (w_query, w_key, w_value)), pltpu.SemaphoreType.DMA((3,))],
        smem=(0, 1),
        hbm=(9, 10, 11),
        us=5.0,
        limit=LARGE,
    )
    ms = [ms[0]] + [shift(ms[k], "y", ny, k) for k in (1, 2, 3)]
    unit = order.shape[1]
    fs = call(
        shuffle,
        [((tok, 2 * nxh * unit // 4), BF16)] * 4,
        (where, order, normed, upstream),
        [pltpu.VMEM((4, tok, 2 * nxh * unit // 4), BF16)],
        smem=(0,),
        us=1.6,
    )
    ms, fs = lax.optimization_barrier((ms, fs))
    kv0 = jnp.concatenate([m[:, :WIDE] for m in ms], axis=0)
    kv2 = flip(kv0, "xl")
    kv1 = flip(kv0, "core")
    fs = [fs[0]] + [shift(fs[k], "y", ny, k) for k in (1, 2, 3)]
    kv2, fs = lax.optimization_barrier((kv2, fs))
    kv3 = flip(kv2, "core")
    many = HEADS * tok
    t, own, far, give = call(
        attend,
        [((many, WIDE), BF16)] + [((many, WIDE), F32)] * 2 + [((2 * many, WIDE), BF16)],
        (where, *ms, kv1, kv2, kv3, master),
        [pltpu.VMEM((many, WIDE), BF16), pltpu.VMEM((many, WIDE), BF16),
         pltpu.VMEM((4 * many, many), F32), pltpu.VMEM((4 * many, many), F32),
         pltpu.VMEM((4 * many, many), BF16), pltpu.VMEM((4 * many, many), BF16)],
        smem=(0,),
        us=7.0,
        limit=24,
    )
    got = flip(give, "core")
    own, far = call(
        first_sum, [((many, WIDE), F32), ((many, WIDE), BF16)], (own, far, got), us=0.5
    )
    far, t = lax.optimization_barrier((far, t))
    got = flip(far, "xl")
    ts = [t] + [shift(t, "y", ny, k) for k in (1, 2, 3)]
    (d,) = call(second_sum, [((many, WIDE), BF16)], (where, own, got), smem=(0,), us=0.5)
    d, near, held, ts = lax.optimization_barrier((d, near, rows, ts))
    ds = [d] + [shift(d, "y", ny, k) for k in (1, 2, 3)]
    fields = ((many, nxh * unit // 4), BF16)
    cuts = (nxh, nz0, nzh * share)
    half = nxh * nz * 2 * share
    (before,) = call(
        functools.partial(weigh_first, cuts),
        [((2, HEADS, half, WIDE), F32)],
        (where, *fs, *ts),
        [pltpu.VMEM(*fields), pltpu.VMEM(*fields)],
        smem=(0,),
        us=2.0,
    )
    result, g_query = call(
        project,
        [(big, BF16), (big, F32)],
        (where, *ts, z, w_out, w_query),
        [pltpu.VMEM((HEADS, tok, WIDE), BF16)],
        smem=(0,),
        us=2.0,
    )
    slope0, slope1 = call(slopes, [(big, F32), (mid, F32)], (held, near, gains), us=2.6)
    ds, before, result, g_query, slope0, slope1 = lax.optimization_barrier(
        (ds, before, result, g_query, slope0, slope1)
    )
    keep, give = call(
        functools.partial(weigh_second, cuts),
        [((HEADS, half, 2 * WIDE), F32), ((HEADS, half, 2 * WIDE), BF16)],
        (where, *fs, *ds, before),
        [pltpu.VMEM(*fields), pltpu.VMEM((2, HEADS, half, WIDE), F32)],
        smem=(0,),
        us=1.5,
    )
    got = flip(give, "core")
    (grad,) = call(
        grad_top,
        [(big, BF16)],
        (where, *ds, g_query, z, upstream, w_key, w_value, gains),
        [pltpu.VMEM((HEADS, tok, WIDE), BF16), pltpu.VMEM(big, F32)],
        smem=(0,),
        us=3.0,
    )
    left, right = halo(grad, nseq)

    pairs = [(a, b) for b in range(nxh) for a in range(2)]

    def ring_part(where, i):
        a, b = pairs[i]
        return jnp.bitwise_xor(where[6], a) * nxh + jnp.bitwise_xor(where[7], b)

    keep, *sends = fold_call(keep, [got], where, ring_part, len(pairs))
    got = []
    for (a, b), send in zip(pairs[1:], sends):
        way = [(s, ((s // 2) ^ b) * 2 + ((s % 2) ^ a)) for s in range(2 * nxh)]
        got.append(lax.ppermute(send, ("xh", "xl"), way))
    left, right, got = lax.optimization_barrier((left, right, got))
    if nz0 == 2:
        keep, send = fold_call(
            keep, got, where, lambda where, i: jnp.bitwise_xor(where[8], i), 2
        )
        got = [lax.ppermute(send, "z", [(s, s ^ 1) for s in range(nz)])]
    (input_grad,) = call(
        backward,
        [(big, BF16)],
        (where, dilations, left, right, grad, slope0, slope1, rows, near, taps),
        [pltpu.VMEM(ext, BF16), pltpu.VMEM(mid, BF16), *shifted],
        smem=(0, 1),
        us=4.6,
    )
    input_grad, got = lax.optimization_barrier((input_grad, got))
    part = ((HEADS, share, 2 * WIDE), F32)
    parts = call(
        last_fold,
        [part] * nzh,
        (where, keep, got[0]),
        [pltpu.VMEM((nzh, *part[0]), F32)],
        smem=(0,),
        us=0.6,
    )
    parts = [parts[0]] + [shift(parts[k], "z", nz, k * nz0) for k in range(1, nzh)]
    (weight_sum,) = call(
        arrange, [((share, 8 * WIDE), F32)], (where, *parts), smem=(0,), us=1.0
    )
    return (result[None], input_grad[None], weight_sum)


def solution(mesh):
    nseq = mesh.shape["seq"]
    ny = nseq // 4
    ndp = mesh.shape["dp"]
    nxh = 2 if ndp % 2 == 0 else 1
    sizes = (nxh, ndp // nxh, ny)
    fine = Mesh(mesh.devices.reshape(*sizes, 2, 2), EVERY)
    cells = P(("xh", "z"), SEQ, None)
    return jax.shard_map(
        functools.partial(local, sizes),
        mesh=fine,
        in_specs=(cells, *(P() for _ in range(9)), cells),
        out_specs=(cells, cells, P(EVERY, None)),
        check_vma=False,
    )
```

```python
import functools

import jax
import jax.numpy as jnp
import numpy as np
from jax import lax
from jax.experimental import pallas as pl
from jax.experimental.pallas import tpu as pltpu
from jax.sharding import Mesh, PartitionSpec as P

HEADS = 4
KEY = 64
VALUE = 192
WIDE = KEY + VALUE
BLOCKS = 2
DMAX = 16
HALO = BLOCKS * DMAX
EPS = 1e-06
STEP = 16
LARGE = 60
SEQ = ("y", "xl", "core")
EVERY = ("xh", "z", "y", "xl", "core")
F32 = jnp.float32
BF16 = jnp.bfloat16
ROOT_HALF = 0.7071067811865476
ROOT_TWO_PI = 0.3989422804014327


def contract(left, right, left_dim, right_dim):
    return lax.dot_general(
        left, right, (((left_dim,), (right_dim,)), ((), ())), preferred_element_type=F32
    )


def call(body, outs, args, scratch=(), smem=(), hbm=(), us=1.0, limit=24):
    spaces = [
        pltpu.SMEM if i in smem else pltpu.HBM if i in hbm else pltpu.VMEM for i in range(len(args))
    ]
    return pl.pallas_call(
        body,
        out_shape=tuple(jax.ShapeDtypeStruct(s, d) for s, d in outs),
        in_specs=[pl.BlockSpec(memory_space=s) for s in spaces],
        out_specs=tuple(pl.BlockSpec(memory_space=pltpu.VMEM) for _ in outs),
        scratch_shapes=list(scratch),
        compiler_params=pltpu.CompilerParams(vmem_limit_bytes=limit << 20),
        cost_estimate=pl.CostEstimate(
            flops=1000, bytes_accessed=int(us * 3.6e6), transcendentals=0
        ),
        name=body.__name__ if hasattr(body, "__name__") else body.func.__name__,
    )(*args)


def inverse_norm(rows):
    return lax.rsqrt(jnp.mean(rows * rows, axis=1, keepdims=True) + EPS)


def activate(rows, gain):
    field = rows * inverse_norm(rows) * gain
    return 0.5 * field * (1.0 + lax.erf(field * ROOT_HALF))


def rounded(rows):
    return rows.astype(BF16).astype(F32)


def loop(count, body):
    def step(i, carry):
        body(pl.multiple_of(i * STEP, STEP))
        return carry

    lax.fori_loop(0, count // STEP, step, 0)


def inside(start, first, last, edge, count):
    out = (first & (start < edge)) | (last & (start >= count - edge))
    return jnp.where(out, 0.0, 1.0)


def move(moved, source, gap):
    count, total = moved.shape[0] // 2, source.shape[0]
    row = lax.broadcasted_iota(jnp.int32, (count, total), 0)
    col = lax.broadcasted_iota(jnp.int32, (count, total), 1)
    held = source[...]
    for i, at in enumerate((DMAX - gap, DMAX + gap)):
        pick = jnp.where(col == row + at, 1.0, 0.0).astype(BF16)
        moved[i * count : (i + 1) * count, :] = contract(pick, held, 1, 0)


def tapped(taps, first, moved, center, r, low=0, high=2):
    count = moved.shape[0] // 2
    return (
        taps[low, first : first + 1, :] * moved[pl.ds(r, STEP), :]
        + taps[1, first : first + 1, :] * center
        + taps[high, first : first + 1, :] * moved[pl.ds(pl.multiple_of(count + r, STEP), STEP), :]
    )


def shuffle(where, order, normed, upstream, f0, f1, f2, f3, slots):
    unit = order.shape[1]
    chan = normed.shape[1]
    row = lax.broadcasted_iota(jnp.int32, (unit, unit), 0)
    pick = jnp.where(row == order[...], 1.0, 0.0).astype(BF16)
    share = unit // 4
    to = 0
    for source in (normed, upstream):
        for low in range(0, chan, unit):
            mixed = contract(source[:, low : low + unit], pick, 1, 0).astype(BF16)
            for y in range(4):
                slots[lax.rem(y - where[0] + 4, 4), :, to : to + share] = mixed[
                    :, y * share : (y + 1) * share
                ]
            to += share
    for i, out in enumerate((f0, f1, f2, f3)):
        out[...] = slots[i]


def fetch(pairs, sems):
    copies = [pltpu.make_async_copy(a, b, sems.at[i]) for i, (a, b) in enumerate(pairs)]
    for copy in copies:
        copy.start()
    return copies


def prelude(
    where, table, buckets, rows_far, gains, upstream_far, w_out_far,
    act, d_att, master, rows, upstream, w_out, line_ref, sems,
):
    copies = fetch(((rows_far, rows), (upstream_far, upstream), (w_out_far, w_out)), sems)
    head = where[0]
    count = buckets.shape[1]
    bucket = lax.broadcasted_iota(jnp.int32, (table.shape[1], count), 0)
    line = lax.dot_general(
        table[...],
        jnp.where(buckets[...] == bucket, 1.0, 0.0),
        (((1,), (0,)), ((), ())),
        precision=lax.Precision.HIGHEST,
        preferred_element_type=F32,
    )
    chosen = lax.broadcasted_iota(jnp.int32, line.shape, 0) == head
    line_ref[...] = jnp.zeros(line_ref.shape, F32)
    line_ref[:, :count] = jnp.sum(jnp.where(chosen, line, 0.0), axis=0, keepdims=True)
    line = line_ref[...]
    span = line.shape[1]
    for r in range(0, 128, 8):
        master[r : r + 8, :] = pltpu.roll(
            jnp.broadcast_to(line, (8, span)), (span - 127 + r) % span, 1, stride=1, stride_axis=0
        )
    gain = gains[0:1, :]
    copies[0].wait()

    def body(r):
        act[pl.ds(r, STEP), :] = activate(rows[pl.ds(r, STEP), :].astype(F32), gain).astype(BF16)

    loop(rows.shape[0], body)
    copies[1].wait()
    copies[2].wait()
    d_att[...] = contract(upstream[...], w_out[...], 1, 1).astype(BF16)


def forward(
    where, dil, left, right, rows, act, d_att, taps, gains, wq_far, wk_far, wv_far,
    m0, m1, m2, m3, normed, z, near,
    x_ext, a_ext, b_ext, slots, moved1, moved2, w_query, w_key, w_value, sems,
):
    copies = fetch(((wq_far, w_query), (wk_far, w_key), (wv_far, w_value)), sems)
    iy, iseq, nseq = where[0], where[1], where[2]
    tok = rows.shape[0]
    x_ext[0:HALO, :] = left[...]
    x_ext[HALO : HALO + tok, :] = rows[...]
    x_ext[HALO + tok :, :] = right[...]
    a_ext[HALO : HALO + tok, :] = act[...]
    gain = gains[0:1, :]
    for r in [*range(0, HALO, STEP), *range(HALO + tok, 2 * HALO + tok, STEP)]:
        a_ext[r : r + STEP, :] = activate(x_ext[r : r + STEP, :].astype(F32), gain).astype(BF16)
    gap, wide = dil[0], dil[1]
    first, last = iseq == 0, iseq == nseq - 1
    count = tok + 2 * DMAX
    gain = gains[1:2, :]
    move(moved1, a_ext, gap)

    def middle(r):
        center = pl.ds(pl.multiple_of(r + DMAX, STEP), STEP)
        mixed = tapped(taps, 0, moved1, a_ext[center, :].astype(F32), r)
        hidden = (x_ext[center, :].astype(F32) + mixed).astype(BF16)
        near[pl.ds(r, STEP), :] = hidden
        keep = inside(r, first, last, DMAX, count)
        b_ext[pl.ds(r, STEP), :] = (activate(hidden.astype(F32), gain) * keep).astype(BF16)

    loop(count, middle)
    last_gain = gains[2:3, :]
    move(moved2, b_ext, wide)

    def top(r):
        center = pl.ds(pl.multiple_of(r + DMAX, STEP), STEP)
        mixed = tapped(taps, 1, moved2, b_ext[center, :].astype(F32), r)
        hidden = (near[center, :].astype(F32) + mixed).astype(BF16)
        z[pl.ds(r, STEP), :] = hidden
        hidden = hidden.astype(F32)
        normed[pl.ds(r, STEP), :] = (hidden * inverse_norm(hidden) * last_gain).astype(BF16)

    loop(tok, top)
    field = normed[...]
    for copy in copies:
        copy.wait()
    queries = (rounded(contract(field, w_query[...], 1, 0)) * KEY**-0.5).astype(BF16)
    keys = contract(field, w_key[...], 1, 0).astype(BF16)
    values = contract(field, w_value[...], 1, 0).astype(BF16)
    for h in range(HEADS):
        k, v = slice(h * KEY, (h + 1) * KEY), slice(h * VALUE, (h + 1) * VALUE)
        slots[lax.rem(h - iy + HEADS, HEADS)] = jnp.concatenate(
            [keys[:, k], values[:, v], queries[:, k], d_att[:, v]], axis=1
        )
    for i, out in enumerate((m0, m1, m2, m3)):
        out[...] = slots[i]


def slopes(rows, near, gains, slope0, slope1):
    def fill(source, gain, out):
        def body(r):
            held = source[pl.ds(r, STEP), :].astype(F32)
            field = held * inverse_norm(held) * gain
            below = 0.5 * (1.0 + lax.erf(field * ROOT_HALF))
            out[pl.ds(r, STEP), :] = (
                below + field * (ROOT_TWO_PI * jnp.exp(-0.5 * field * field))
            ) * gain

        loop(source.shape[0], body)

    fill(near, gains[1:2, :], slope1)
    fill(rows, gains[0:1, :], slope0)


def attend(
    where, m0, m1, m2, m3, kv1, kv2, kv3, master,
    t, own, far, give, ask, kv0, score, pull, soft, d_soft,
):
    iy, c = where[0], where[3]
    tok = m0.shape[0]
    many = HEADS * tok
    for i, m in enumerate((m0, m1, m2, m3)):
        kv0[i * tok : (i + 1) * tok, :] = m[:, :WIDE]
        ask[i * tok : (i + 1) * tok, :] = m[:, WIDE:]
    both = ask[...]
    lane = lax.broadcasted_iota(jnp.int32, (1, WIDE), 1)
    is_key = lane < KEY
    zero = jnp.zeros_like(both)
    queries = jnp.where(is_key, both, zero)
    d_att = jnp.where(is_key, zero, both)
    blocks = (kv0, kv1, kv2, kv3)
    bands = [lax.rem(iy - i + HEADS, HEADS) for i in range(HEADS)]
    top = None
    for j, block in enumerate(blocks):
        other = jnp.bitwise_xor(c, j)
        for i in range(HEADS):
            at = j * many + i * tok
            part = contract(block[i * tok : (i + 1) * tok, :], queries, 1, 1)
            bias = jnp.concatenate(
                [
                    master[:, pl.ds(pl.multiple_of((4 * (q - bands[i]) + c - other + 15) * tok, tok), tok)]
                    for q in bands
                ],
                axis=1,
            )
            part = part + bias
            score[at : at + tok, :] = part
            peak = jnp.max(part, axis=0, keepdims=True)
            top = peak if top is None else jnp.maximum(top, peak)
    total = jnp.zeros_like(top)
    for at in range(0, 4 * many, tok):
        part = jnp.exp(score[at : at + tok, :] - top)
        score[at : at + tok, :] = part
        total = total + jnp.sum(part, axis=0, keepdims=True)
    scale = 1.0 / total
    delta = jnp.zeros_like(top)
    for j, block in enumerate(blocks):
        for i in range(HEADS):
            at = j * many + i * tok
            probs = score[at : at + tok, :] * scale
            score[at : at + tok, :] = probs
            soft[at : at + tok, :] = probs.astype(BF16)
            part = contract(block[i * tok : (i + 1) * tok, :], d_att, 1, 1)
            pull[at : at + tok, :] = part
            delta = delta + jnp.sum(part * probs, axis=0, keepdims=True)
    for at in range(0, 4 * many, tok):
        d_soft[at : at + tok, :] = (
            score[at : at + tok, :] * (pull[at : at + tok, :] - delta)
        ).astype(BF16)
    att = jnp.zeros((WIDE, many), F32)
    d_query = jnp.zeros((WIDE, many), F32)
    for j, block in enumerate(blocks):
        held = block[...]
        span = slice(j * many, (j + 1) * many)
        att = att + contract(held, soft[span, :], 0, 0)
        d_query = d_query + contract(held, d_soft[span, :], 0, 0)
        d_kv = jnp.where(
            is_key, contract(d_soft[span, :], both, 1, 0), contract(soft[span, :], both, 1, 0)
        )
        if j == 0:
            own[...] = d_kv
        elif j == 2:
            far[...] = d_kv
        else:
            give[(j // 2) * many : (j // 2 + 1) * many, :] = d_kv.astype(BF16)
    side = lax.broadcasted_iota(jnp.int32, (WIDE, 1), 0) < KEY
    mixed = jnp.where(side, d_query * KEY**-0.5, att).T.astype(BF16)
    for i, band in enumerate(bands):
        t[pl.ds(pl.multiple_of(band * tok, tok), tok), :] = mixed[i * tok : (i + 1) * tok, :]


def first_sum(own, far, got, near, send):
    many = own.shape[0]
    near[...] = own[...] + got[:many, :].astype(F32)
    send[...] = (far[...] + got[many:, :].astype(F32)).astype(BF16)


def second_sum(where, near, got, total):
    held = (near[...] + got[...].astype(F32)).astype(BF16)
    tok = held.shape[0] // HEADS
    for i in range(HEADS):
        band = lax.rem(where[0] - i + HEADS, HEADS)
        total[pl.ds(pl.multiple_of(band * tok, tok), tok), :] = held[i * tok : (i + 1) * tok, :]


def gathered(slots, parts, iy):
    tok = slots.shape[1]
    for i, part in enumerate(parts):
        held = part[pl.ds(pl.multiple_of(iy * tok, tok), tok), :]
        slots[lax.rem(iy - i + HEADS, HEADS)] = held


def heads_of(slots, low, high):
    return jnp.concatenate([slots[h][:, low:high] for h in range(HEADS)], axis=1)


def project(where, t0, t1, t2, t3, z, w_out, w_query, result, g_query, slots):
    gathered(slots, (t0, t1, t2, t3), where[0])
    att = heads_of(slots, KEY, WIDE)
    result[...] = (z[...].astype(F32) + contract(att, w_out[...], 1, 0)).astype(BF16)
    g_query[...] = contract(heads_of(slots, 0, KEY), w_query[...], 1, 1)


def pull_norm(held, scaled):
    s = inverse_norm(held)
    return s * scaled - held * (s * s * s) * jnp.mean(scaled * held, axis=1, keepdims=True)


def grad_top(where, d0, d1, d2, d3, g_query, z, upstream, w_key, w_value, gains, out, slots, total):
    gathered(slots, (d0, d1, d2, d3), where[0])
    total[...] = (
        g_query[...]
        + contract(heads_of(slots, 0, KEY), w_key[...], 1, 1)
        + contract(heads_of(slots, KEY, WIDE), w_value[...], 1, 1)
    )
    gain = gains[2:3, :]

    def body(r):
        at = pl.ds(r, STEP)
        grad = pull_norm(z[at, :].astype(F32), total[at, :] * gain)
        out[at, :] = (upstream[at, :].astype(F32) + grad).astype(BF16)

    loop(z.shape[0], body)


def backward(
    where, dil, left, right, grad, slope0, slope1, rows, near, taps, out, g_ext, p_ext, moved1, moved2
):
    iseq, nseq = where[1], where[2]
    tok = rows.shape[0]
    first, last = iseq == 0, iseq == nseq - 1
    g_ext[0:HALO, :] = left[...]
    g_ext[HALO : HALO + tok, :] = grad[...]
    g_ext[HALO + tok :, :] = right[...]
    gap, wide = dil[0], dil[1]
    count = tok + 2 * DMAX

    move(moved1, g_ext, wide)

    def middle(r):
        center = g_ext[pl.ds(pl.multiple_of(r + DMAX, STEP), STEP), :].astype(F32)
        mixed = tapped(taps, 1, moved1, center, r, 2, 0)
        at = pl.ds(r, STEP)
        held = pull_norm(near[at, :].astype(F32), mixed * slope1[at, :])
        keep = inside(r, first, last, DMAX, count)
        p_ext[at, :] = ((center + held) * keep).astype(BF16)

    loop(count, middle)
    move(moved2, p_ext, gap)

    def bottom(r):
        center = p_ext[pl.ds(pl.multiple_of(r + DMAX, STEP), STEP), :].astype(F32)
        mixed = tapped(taps, 0, moved2, center, r, 2, 0)
        at = pl.ds(r, STEP)
        held = pull_norm(rows[at, :].astype(F32), mixed * slope0[at, :])
        out[at, :] = (center + held).astype(BF16)

    loop(tok, bottom)


def placed(out, cuts, head, held):
    nxh, nz0, size = cuts
    at = 0
    for xh in range(nxh):
        for core in range(2):
            for xl in range(2):
                for z0 in range(nz0):
                    to = ((xl * nxh + xh) * nz0 + z0) * size
                    out[core, head, to : to + size, :] = held[at : at + size, :]
                    at += size


def naturally(parts, out, low, iy):
    tok, width = parts[0].shape[0], out.shape[1]
    for i, part in enumerate(parts):
        band = lax.rem(iy - i + HEADS, HEADS)
        out[pl.ds(pl.multiple_of(band * tok, tok), tok), :] = part[:, low : low + width]


def weigh_first(cuts, where, f0, f1, f2, f3, t0, t1, t2, t3, out, n_all, u_all):
    iy = where[0]
    parts = (f0, f1, f2, f3)
    naturally(parts, n_all, 0, iy)
    naturally(parts, u_all, n_all.shape[1], iy)
    is_key = lax.broadcasted_iota(jnp.int32, (1, WIDE), 1) < KEY
    for i, t in enumerate((t0, t1, t2, t3)):
        held = t[...]
        first = jnp.where(
            is_key, contract(n_all[...], held, 0, 0), contract(u_all[...], held, 0, 0)
        )
        placed(out, cuts, lax.rem(iy - i + HEADS, HEADS), first)


def weigh_second(
    cuts, where, f0, f1, f2, f3, d0, d1, d2, d3, before, keep, give, n_all, out
):
    iy, core = where[0], where[4]
    naturally((f0, f1, f2, f3), n_all, 0, iy)
    for i, d in enumerate((d0, d1, d2, d3)):
        placed(out, cuts, lax.rem(iy - i + HEADS, HEADS), contract(n_all[...], d[...], 0, 0))
    keep[:, :, :WIDE] = before[core]
    keep[:, :, WIDE:] = out[core]
    give[:, :, :WIDE] = before[1 - core].astype(BF16)
    give[:, :, WIDE:] = out[1 - core].astype(BF16)


def fold(count, part_of, where, keep, *refs):
    got, outs, held = refs[:count], refs[count:-1], refs[-1]
    total = keep[...]
    for g in got:
        total = total + g[...].astype(F32)
    held[...] = total
    size = outs[0].shape[1]
    for i, out in enumerate(outs):
        at = part_of(where, i)
        out[...] = held[:, pl.ds(pl.multiple_of(at * size, 8), size), :].astype(out.dtype)


def fold_call(keep, got, where, part_of, count):
    heads, rows, width = keep.shape
    shape = (heads, rows // count, width)
    return call(
        functools.partial(fold, len(got), part_of),
        [(shape, F32)] + [(shape, BF16)] * (count - 1),
        (where, keep, *got),
        [pltpu.VMEM(keep.shape, F32)],
        smem=(0,),
        us=0.7,
    )


def last_fold(where, keep, got, *refs):
    outs, slots = refs[:-1], refs[-1]
    count = len(outs)
    total = keep[...] + got[...].astype(F32)
    size = total.shape[1] // count
    for i in range(count):
        slots[i] = total[:, i * size : (i + 1) * size, :]
    for i, out in enumerate(outs):
        out[...] = slots[lax.rem(where[9] + i, count)]


def arrange(where, *refs):
    held, out = refs[0][...], refs[-1]
    for g in refs[1:-1]:
        held = held + g[...]
    held = held * (1.0 / where[5].astype(F32))
    keys = HEADS * KEY
    for h in range(HEADS):
        part = held[h]
        out[:, h * KEY : (h + 1) * KEY] = part[:, :KEY]
        low = 2 * keys + HEADS * VALUE + h * VALUE
        out[:, low : low + VALUE] = part[:, KEY:WIDE]
        out[:, keys + h * KEY : keys + (h + 1) * KEY] = part[:, WIDE : WIDE + KEY]
        low = 2 * keys + h * VALUE
        out[:, low : low + VALUE] = part[:, WIDE + KEY :]


def column_order(nz0, nzh, size):
    y, core, xl, z0, zh, j = np.meshgrid(
        *(np.arange(n) for n in (4, 2, 2, nz0, nzh, size)), indexing="ij"
    )
    column = ((((zh * nz0 + z0) * 4 + y) * 2 + xl) * 2 + core) * size + j
    return column.reshape(1, -1).astype(np.int32)


def shift(array, axis, count, step):
    return lax.ppermute(array, axis, [(i, (i + step) % count) for i in range(count)])


def flip(array, axis):
    return lax.ppermute(array, axis, [(0, 1), (1, 0)])


def halo(rows, nseq):
    width = HALO
    left = lax.ppermute(rows[-width:], SEQ, [(i, i + 1) for i in range(nseq - 1)])
    right = lax.ppermute(rows[:width], SEQ, [(i + 1, i) for i in range(nseq - 1)])
    return left, right


def local(
    sizes, inputs, dilations, taps, gains, bias_table, buckets, w_query, w_key, w_value, w_out, cotangent
):
    nxh, nz, ny = sizes
    nz0 = 2 if nz % 2 == 0 else 1
    nzh = nz // nz0
    nseq = ny * 4
    rows, upstream = inputs[0], cotangent[0]
    tok, chan = rows.shape
    iy, ixl, icore = lax.axis_index("y"), lax.axis_index("xl"), lax.axis_index("core")
    ixh, iz = lax.axis_index("xh"), lax.axis_index("z")
    c = ixl * 2 + icore
    loci = inputs.shape[0] * nxh * nz
    where = jnp.stack(
        [iy, iy * 4 + c, jnp.int32(nseq), c, icore, jnp.int32(loci), ixl, ixh, iz % nz0, iz // nz0]
    ).astype(jnp.int32)
    taps = taps.transpose(1, 0, 2)
    big = (tok, chan)

    left, right = halo(rows, nseq)
    share = chan // (nxh * nz * nseq)
    order = jnp.asarray(column_order(nz0, nzh, share))
    size = buckets.shape[0]
    act, d_att, master = call(
        prelude,
        [(big, BF16), ((tok, HEADS * VALUE), BF16), ((128, size + 1), F32)],
        (iy.reshape(1), bias_table.T, buckets[None], rows, gains, upstream, w_out),
        [pltpu.VMEM(big, BF16), pltpu.VMEM(big, BF16), pltpu.VMEM(w_out.shape, BF16),
         pltpu.VMEM((1, size + 1), F32), pltpu.SemaphoreType.DMA((3,))],
        smem=(0,),
        hbm=(3, 5, 6),
        us=3.6,
        limit=LARGE,
    )
    ext = (tok + 2 * HALO, chan)
    mid = (tok + 2 * DMAX, chan)
    shifted = [pltpu.VMEM((2 * mid[0], chan), F32), pltpu.VMEM((2 * tok, chan), F32)]
    *ms, normed, z, near = call(
        forward,
        [((tok, 2 * WIDE), BF16)] * 4 + [(big, BF16), (big, BF16), (mid, BF16)],
        (where, dilations, left, right, rows, act, d_att, taps, gains, w_query, w_key, w_value),
        [pltpu.VMEM(ext, BF16), pltpu.VMEM(ext, BF16), pltpu.VMEM(mid, BF16),
         pltpu.VMEM((HEADS, tok, 2 * WIDE), BF16), *shifted,
         *(pltpu.VMEM(w.shape, BF16) for w in (w_query, w_key, w_value)), pltpu.SemaphoreType.DMA((3,))],
        smem=(0, 1),
        hbm=(9, 10, 11),
        us=5.0,
        limit=LARGE,
    )
    ms = [ms[0]] + [shift(ms[k], "y", ny, k) for k in (1, 2, 3)]
    unit = order.shape[1]
    fs = call(
        shuffle,
        [((tok, 2 * nxh * unit // 4), BF16)] * 4,
        (where, order, normed, upstream),
        [pltpu.VMEM((4, tok, 2 * nxh * unit // 4), BF16)],
        smem=(0,),
        us=1.6,
    )
    ms, fs = lax.optimization_barrier((ms, fs))
    kv0 = jnp.concatenate([m[:, :WIDE] for m in ms], axis=0)
    kv2 = flip(kv0, "xl")
    kv1 = flip(kv0, "core")
    fs = [fs[0]] + [shift(fs[k], "y", ny, k) for k in (1, 2, 3)]
    kv3 = flip(kv2, "core")
    many = HEADS * tok
    t, own, far, give = call(
        attend,
        [((many, WIDE), BF16)] + [((many, WIDE), F32)] * 2 + [((2 * many, WIDE), BF16)],
        (where, *ms, kv1, kv2, kv3, master),
        [pltpu.VMEM((many, WIDE), BF16), pltpu.VMEM((many, WIDE), BF16),
         pltpu.VMEM((4 * many, many), F32), pltpu.VMEM((4 * many, many), F32),
         pltpu.VMEM((4 * many, many), BF16), pltpu.VMEM((4 * many, many), BF16)],
        smem=(0,),
        us=7.0,
        limit=24,
    )
    give, fs = lax.optimization_barrier((give, fs))
    got = flip(give, "core")
    own, far = call(
        first_sum, [((many, WIDE), F32), ((many, WIDE), BF16)], (own, far, got), us=0.5
    )
    far, t = lax.optimization_barrier((far, t))
    got = flip(far, "xl")
    ts = [t] + [shift(t, "y", ny, k) for k in (1, 2, 3)]
    (d,) = call(second_sum, [((many, WIDE), BF16)], (where, own, got), smem=(0,), us=0.5)
    d, near, held = lax.optimization_barrier((d, near, rows))
    ds = [d] + [shift(d, "y", ny, k) for k in (1, 2, 3)]
    fields = ((many, nxh * unit // 4), BF16)
    cuts = (nxh, nz0, nzh * share)
    half = nxh * nz * 2 * share
    (before,) = call(
        functools.partial(weigh_first, cuts),
        [((2, HEADS, half, WIDE), F32)],
        (where, *fs, *ts),
        [pltpu.VMEM(*fields), pltpu.VMEM(*fields)],
        smem=(0,),
        us=2.0,
    )
    result, g_query = call(
        project,
        [(big, BF16), (big, F32)],
        (where, *ts, z, w_out, w_query),
        [pltpu.VMEM((HEADS, tok, WIDE), BF16)],
        smem=(0,),
        us=2.0,
    )
    slope0, slope1 = call(slopes, [(big, F32), (mid, F32)], (held, near, gains), us=2.6)
    ds, before, result, g_query, slope0, slope1 = lax.optimization_barrier(
        (ds, before, result, g_query, slope0, slope1)
    )
    keep, give = call(
        functools.partial(weigh_second, cuts),
        [((HEADS, half, 2 * WIDE), F32), ((HEADS, half, 2 * WIDE), BF16)],
        (where, *fs, *ds, before),
        [pltpu.VMEM(*fields), pltpu.VMEM((2, HEADS, half, WIDE), F32)],
        smem=(0,),
        us=1.5,
    )
    got = flip(give, "core")
    (grad,) = call(
        grad_top,
        [(big, BF16)],
        (where, *ds, g_query, z, upstream, w_key, w_value, gains),
        [pltpu.VMEM((HEADS, tok, WIDE), BF16), pltpu.VMEM(big, F32)],
        smem=(0,),
        us=3.0,
    )
    left, right = halo(grad, nseq)

    pairs = [(a, b) for b in range(nxh) for a in range(2)]

    def ring_part(where, i):
        a, b = pairs[i]
        return jnp.bitwise_xor(where[6], a) * nxh + jnp.bitwise_xor(where[7], b)

    keep, *sends = fold_call(keep, [got], where, ring_part, len(pairs))
    got = []
    for (a, b), send in zip(pairs[1:], sends):
        way = [(s, ((s // 2) ^ b) * 2 + ((s % 2) ^ a)) for s in range(2 * nxh)]
        got.append(lax.ppermute(send, ("xh", "xl"), way))
    left, right, got = lax.optimization_barrier((left, right, got))
    if nz0 == 2:
        keep, send = fold_call(
            keep, got, where, lambda where, i: jnp.bitwise_xor(where[8], i), 2
        )
        got = [lax.ppermute(send, "z", [(s, s ^ 1) for s in range(nz)])]
    (input_grad,) = call(
        backward,
        [(big, BF16)],
        (where, dilations, left, right, grad, slope0, slope1, rows, near, taps),
        [pltpu.VMEM(ext, BF16), pltpu.VMEM(mid, BF16), *shifted],
        smem=(0, 1),
        us=4.6,
    )
    input_grad, got = lax.optimization_barrier((input_grad, got))
    part = ((HEADS, share, 2 * WIDE), F32)
    parts = call(
        last_fold,
        [part] * nzh,
        (where, keep, got[0]),
        [pltpu.VMEM((nzh, *part[0]), F32)],
        smem=(0,),
        us=0.6,
    )
    parts = [parts[0]] + [shift(parts[k], "z", nz, k * nz0) for k in range(1, nzh)]
    (weight_sum,) = call(
        arrange, [((share, 8 * WIDE), F32)], (where, *parts), smem=(0,), us=1.0
    )
    return (result[None], input_grad[None], weight_sum)


def solution(mesh):
    nseq = mesh.shape["seq"]
    ny = nseq // 4
    ndp = mesh.shape["dp"]
    nxh = 2 if ndp % 2 == 0 else 1
    sizes = (nxh, ndp // nxh, ny)
    fine = Mesh(mesh.devices.reshape(*sizes, 2, 2), EVERY)
    cells = P(("xh", "z"), SEQ, None)
    return jax.shard_map(
        functools.partial(local, sizes),
        mesh=fine,
        in_specs=(cells, *(P() for _ in range(9)), cells),
        out_specs=(cells, cells, P(EVERY, None)),
        check_vma=False,
    )
```

```python
import functools

import jax
import jax.numpy as jnp
import numpy as np
from jax import lax
from jax.experimental import pallas as pl
from jax.experimental.pallas import tpu as pltpu
from jax.sharding import Mesh, PartitionSpec as P

HEADS = 4
KEY = 64
VALUE = 192
WIDE = KEY + VALUE
BLOCKS = 2
DMAX = 16
HALO = BLOCKS * DMAX
EPS = 1e-06
STEP = 16
LARGE = 60
SEQ = ("y", "xl", "core")
EVERY = ("xh", "z", "y", "xl", "core")
F32 = jnp.float32
BF16 = jnp.bfloat16
ROOT_HALF = 0.7071067811865476
ROOT_TWO_PI = 0.3989422804014327


def contract(left, right, left_dim, right_dim):
    return lax.dot_general(
        left, right, (((left_dim,), (right_dim,)), ((), ())), preferred_element_type=F32
    )


def call(body, outs, args, scratch=(), smem=(), hbm=(), us=1.0, limit=24):
    spaces = [
        pltpu.SMEM if i in smem else pltpu.HBM if i in hbm else pltpu.VMEM for i in range(len(args))
    ]
    return pl.pallas_call(
        body,
        out_shape=tuple(jax.ShapeDtypeStruct(s, d) for s, d in outs),
        in_specs=[pl.BlockSpec(memory_space=s) for s in spaces],
        out_specs=tuple(pl.BlockSpec(memory_space=pltpu.VMEM) for _ in outs),
        scratch_shapes=list(scratch),
        compiler_params=pltpu.CompilerParams(vmem_limit_bytes=limit << 20),
        cost_estimate=pl.CostEstimate(
            flops=1000, bytes_accessed=int(us * 3.6e6), transcendentals=0
        ),
        name=body.__name__ if hasattr(body, "__name__") else body.func.__name__,
    )(*args)


def inverse_norm(rows):
    return lax.rsqrt(jnp.mean(rows * rows, axis=1, keepdims=True) + EPS)


def activate(rows, gain):
    field = rows * inverse_norm(rows) * gain
    return 0.5 * field * (1.0 + lax.erf(field * ROOT_HALF))


def rounded(rows):
    return rows.astype(BF16).astype(F32)


def loop(count, body):
    def step(i, carry):
        body(pl.multiple_of(i * STEP, STEP))
        return carry

    lax.fori_loop(0, count // STEP, step, 0, unroll=2)


def inside(start, first, last, edge, count):
    out = (first & (start < edge)) | (last & (start >= count - edge))
    return jnp.where(out, 0.0, 1.0)


def move(moved, source, gap):
    count, total = moved.shape[0] // 2, source.shape[0]
    row = lax.broadcasted_iota(jnp.int32, (count, total), 0)
    col = lax.broadcasted_iota(jnp.int32, (count, total), 1)
    held = source[...]
    for i, at in enumerate((DMAX - gap, DMAX + gap)):
        pick = jnp.where(col == row + at, 1.0, 0.0).astype(BF16)
        moved[i * count : (i + 1) * count, :] = contract(pick, held, 1, 0)


def tapped(taps, first, moved, center, r, low=0, high=2):
    count = moved.shape[0] // 2
    return (
        taps[low, first : first + 1, :] * moved[pl.ds(r, STEP), :]
        + taps[1, first : first + 1, :] * center
        + taps[high, first : first + 1, :] * moved[pl.ds(pl.multiple_of(count + r, STEP), STEP), :]
    )


def shuffle(where, order, normed, upstream, f0, f1, f2, f3, slots):
    unit = order.shape[1]
    chan = normed.shape[1]
    row = lax.broadcasted_iota(jnp.int32, (unit, unit), 0)
    pick = jnp.where(row == order[...], 1.0, 0.0).astype(BF16)
    share = unit // 4
    to = 0
    for source in (normed, upstream):
        for low in range(0, chan, unit):
            mixed = contract(source[:, low : low + unit], pick, 1, 0).astype(BF16)
            for y in range(4):
                slots[lax.rem(y - where[0] + 4, 4), :, to : to + share] = mixed[
                    :, y * share : (y + 1) * share
                ]
            to += share
    for i, out in enumerate((f0, f1, f2, f3)):
        out[...] = slots[i]


def fetch(pairs, sems):
    copies = [pltpu.make_async_copy(a, b, sems.at[i]) for i, (a, b) in enumerate(pairs)]
    for copy in copies:
        copy.start()
    return copies


def expand(where, table, buckets, master, line_ref):
    head = where[0]
    count = buckets.shape[1]
    bucket = lax.broadcasted_iota(jnp.int32, (table.shape[1], count), 0)
    line = lax.dot_general(
        table[...],
        jnp.where(buckets[...] == bucket, 1.0, 0.0),
        (((1,), (0,)), ((), ())),
        precision=lax.Precision.HIGHEST,
        preferred_element_type=F32,
    )
    chosen = lax.broadcasted_iota(jnp.int32, line.shape, 0) == head
    line_ref[...] = jnp.zeros(line_ref.shape, F32)
    line_ref[:, :count] = jnp.sum(jnp.where(chosen, line, 0.0), axis=0, keepdims=True)
    line = line_ref[...]
    span = line.shape[1]
    for r in range(0, 128, 8):
        master[r : r + 8, :] = pltpu.roll(
            jnp.broadcast_to(line, (8, span)), (span - 127 + r) % span, 1, stride=1, stride_axis=0
        )


def prelude(
    rows_far, gains, upstream_far, w_out_far,
    act, d_att, rows, upstream, w_out, sems,
):
    copies = fetch(((rows_far, rows), (upstream_far, upstream), (w_out_far, w_out)), sems)
    gain = gains[0:1, :]
    copies[0].wait()

    def body(r):
        act[pl.ds(r, STEP), :] = activate(rows[pl.ds(r, STEP), :].astype(F32), gain).astype(BF16)

    loop(rows.shape[0], body)
    copies[1].wait()
    copies[2].wait()
    d_att[...] = contract(upstream[...], w_out[...], 1, 1).astype(BF16)


def forward(
    where, dil, left, right, rows, act, d_att, taps, gains, wq_far, wk_far, wv_far,
    m0, m1, m2, m3, normed, z, near,
    x_ext, a_ext, b_ext, slots, moved1, moved2, w_query, w_key, w_value, sems,
):
    copies = fetch(((wq_far, w_query), (wk_far, w_key), (wv_far, w_value)), sems)
    iy, iseq, nseq = where[0], where[1], where[2]
    tok = rows.shape[0]
    x_ext[0:HALO, :] = left[...]
    x_ext[HALO : HALO + tok, :] = rows[...]
    x_ext[HALO + tok :, :] = right[...]
    a_ext[HALO : HALO + tok, :] = act[...]
    gain = gains[0:1, :]
    for r in [*range(0, HALO, STEP), *range(HALO + tok, 2 * HALO + tok, STEP)]:
        a_ext[r : r + STEP, :] = activate(x_ext[r : r + STEP, :].astype(F32), gain).astype(BF16)
    gap, wide = dil[0], dil[1]
    first, last = iseq == 0, iseq == nseq - 1
    count = tok + 2 * DMAX
    gain = gains[1:2, :]
    move(moved1, a_ext, gap)

    def middle(r):
        center = pl.ds(pl.multiple_of(r + DMAX, STEP), STEP)
        mixed = tapped(taps, 0, moved1, a_ext[center, :].astype(F32), r)
        hidden = (x_ext[center, :].astype(F32) + mixed).astype(BF16)
        near[pl.ds(r, STEP), :] = hidden
        keep = inside(r, first, last, DMAX, count)
        b_ext[pl.ds(r, STEP), :] = (activate(hidden.astype(F32), gain) * keep).astype(BF16)

    loop(count, middle)
    last_gain = gains[2:3, :]
    move(moved2, b_ext, wide)

    def top(r):
        center = pl.ds(pl.multiple_of(r + DMAX, STEP), STEP)
        mixed = tapped(taps, 1, moved2, b_ext[center, :].astype(F32), r)
        hidden = (near[center, :].astype(F32) + mixed).astype(BF16)
        z[pl.ds(r, STEP), :] = hidden
        hidden = hidden.astype(F32)
        normed[pl.ds(r, STEP), :] = (hidden * inverse_norm(hidden) * last_gain).astype(BF16)

    loop(tok, top)
    field = normed[...]
    for copy in copies:
        copy.wait()
    queries = (rounded(contract(field, w_query[...], 1, 0)) * KEY**-0.5).astype(BF16)
    keys = contract(field, w_key[...], 1, 0).astype(BF16)
    values = contract(field, w_value[...], 1, 0).astype(BF16)
    for h in range(HEADS):
        k, v = slice(h * KEY, (h + 1) * KEY), slice(h * VALUE, (h + 1) * VALUE)
        slots[lax.rem(h - iy + HEADS, HEADS)] = jnp.concatenate(
            [keys[:, k], values[:, v], queries[:, k], d_att[:, v]], axis=1
        )
    for i, out in enumerate((m0, m1, m2, m3)):
        out[...] = slots[i]


def slopes(rows, near, gains, slope0, slope1):
    def fill(source, gain, out):
        def body(r):
            held = source[pl.ds(r, STEP), :].astype(F32)
            field = held * inverse_norm(held) * gain
            below = 0.5 * (1.0 + lax.erf(field * ROOT_HALF))
            out[pl.ds(r, STEP), :] = (
                below + field * (ROOT_TWO_PI * jnp.exp(-0.5 * field * field))
            ) * gain

        loop(source.shape[0], body)

    fill(near, gains[1:2, :], slope1)
    fill(rows, gains[0:1, :], slope0)


def attend(
    where, m0, m1, m2, m3, kv1, kv2, kv3, master,
    t, own, far, give, ask, kv0, score, pull, soft, d_soft,
):
    iy, c = where[0], where[3]
    tok = m0.shape[0]
    many = HEADS * tok
    for i, m in enumerate((m0, m1, m2, m3)):
        kv0[i * tok : (i + 1) * tok, :] = m[:, :WIDE]
        ask[i * tok : (i + 1) * tok, :] = m[:, WIDE:]
    both = ask[...]
    lane = lax.broadcasted_iota(jnp.int32, (1, WIDE), 1)
    is_key = lane < KEY
    zero = jnp.zeros_like(both)
    queries = jnp.where(is_key, both, zero)
    d_att = jnp.where(is_key, zero, both)
    blocks = (kv0, kv1, kv2, kv3)
    bands = [lax.rem(iy - i + HEADS, HEADS) for i in range(HEADS)]
    top = None
    for j, block in enumerate(blocks):
        other = jnp.bitwise_xor(c, j)
        for i in range(HEADS):
            at = j * many + i * tok
            part = contract(block[i * tok : (i + 1) * tok, :], queries, 1, 1)
            bias = jnp.concatenate(
                [
                    master[:, pl.ds(pl.multiple_of((4 * (q - bands[i]) + c - other + 15) * tok, tok), tok)]
                    for q in bands
                ],
                axis=1,
            )
            part = part + bias
            score[at : at + tok, :] = part
            peak = jnp.max(part, axis=0, keepdims=True)
            top = peak if top is None else jnp.maximum(top, peak)
    total = jnp.zeros_like(top)
    for at in range(0, 4 * many, tok):
        part = jnp.exp(score[at : at + tok, :] - top)
        score[at : at + tok, :] = part
        total = total + jnp.sum(part, axis=0, keepdims=True)
    scale = 1.0 / total
    delta = jnp.zeros_like(top)
    for j, block in enumerate(blocks):
        for i in range(HEADS):
            at = j * many + i * tok
            probs = score[at : at + tok, :] * scale
            score[at : at + tok, :] = probs
            soft[at : at + tok, :] = probs.astype(BF16)
            part = contract(block[i * tok : (i + 1) * tok, :], d_att, 1, 1)
            pull[at : at + tok, :] = part
            delta = delta + jnp.sum(part * probs, axis=0, keepdims=True)
    for at in range(0, 4 * many, tok):
        d_soft[at : at + tok, :] = (
            score[at : at + tok, :] * (pull[at : at + tok, :] - delta)
        ).astype(BF16)
    att = jnp.zeros((WIDE, many), F32)
    d_query = jnp.zeros((WIDE, many), F32)
    for j, block in enumerate(blocks):
        held = block[...]
        span = slice(j * many, (j + 1) * many)
        att = att + contract(held, soft[span, :], 0, 0)
        d_query = d_query + contract(held, d_soft[span, :], 0, 0)
        d_kv = jnp.where(
            is_key, contract(d_soft[span, :], both, 1, 0), contract(soft[span, :], both, 1, 0)
        )
        if j == 0:
            own[...] = d_kv
        elif j == 2:
            far[...] = d_kv
        else:
            give[(j // 2) * many : (j // 2 + 1) * many, :] = d_kv.astype(BF16)
    side = lax.broadcasted_iota(jnp.int32, (WIDE, 1), 0) < KEY
    mixed = jnp.where(side, d_query * KEY**-0.5, att).T.astype(BF16)
    for i, band in enumerate(bands):
        t[pl.ds(pl.multiple_of(band * tok, tok), tok), :] = mixed[i * tok : (i + 1) * tok, :]


def first_sum(own, far, got, near, send):
    many = own.shape[0]
    near[...] = own[...] + got[:many, :].astype(F32)
    send[...] = (far[...] + got[many:, :].astype(F32)).astype(BF16)


def second_sum(where, near, got, total):
    held = (near[...] + got[...].astype(F32)).astype(BF16)
    tok = held.shape[0] // HEADS
    for i in range(HEADS):
        band = lax.rem(where[0] - i + HEADS, HEADS)
        total[pl.ds(pl.multiple_of(band * tok, tok), tok), :] = held[i * tok : (i + 1) * tok, :]


def joined(parts, whole):
    half = parts[2].shape[0]
    whole[:half, :] = parts[2][...]
    whole[half:, :] = parts[3][...]
    return parts[0], parts[1], whole, parts[4]


def gathered(slots, parts, whole, iy):
    tok = slots.shape[1]
    for i, part in enumerate(joined(parts, whole)):
        held = part[pl.ds(pl.multiple_of(iy * tok, tok), tok), :]
        slots[lax.rem(iy - i + HEADS, HEADS)] = held


def heads_of(slots, low, high):
    return jnp.concatenate([slots[h][:, low:high] for h in range(HEADS)], axis=1)


def project(where, t0, t1, t2, t3, t4, z, w_out, w_query, result, g_query, slots, whole):
    gathered(slots, (t0, t1, t2, t3, t4), whole, where[0])
    att = heads_of(slots, KEY, WIDE)
    result[...] = (z[...].astype(F32) + contract(att, w_out[...], 1, 0)).astype(BF16)
    g_query[...] = contract(heads_of(slots, 0, KEY), w_query[...], 1, 1)


def pull_norm(held, scaled):
    s = inverse_norm(held)
    return s * scaled - held * (s * s * s) * jnp.mean(scaled * held, axis=1, keepdims=True)


def grad_top(
    where, d0, d1, d2, d3, d4, g_query, z, upstream, w_key, w_value, gains, out, slots, total, whole
):
    gathered(slots, (d0, d1, d2, d3, d4), whole, where[0])
    total[...] = (
        g_query[...]
        + contract(heads_of(slots, 0, KEY), w_key[...], 1, 1)
        + contract(heads_of(slots, KEY, WIDE), w_value[...], 1, 1)
    )
    gain = gains[2:3, :]

    def body(r):
        at = pl.ds(r, STEP)
        grad = pull_norm(z[at, :].astype(F32), total[at, :] * gain)
        out[at, :] = (upstream[at, :].astype(F32) + grad).astype(BF16)

    loop(z.shape[0], body)


def backward(
    where, dil, left, right, grad, slope0, slope1, rows, near, taps, out, g_ext, p_ext, moved1, moved2
):
    iseq, nseq = where[1], where[2]
    tok = rows.shape[0]
    first, last = iseq == 0, iseq == nseq - 1
    g_ext[0:HALO, :] = left[...]
    g_ext[HALO : HALO + tok, :] = grad[...]
    g_ext[HALO + tok :, :] = right[...]
    gap, wide = dil[0], dil[1]
    count = tok + 2 * DMAX

    move(moved1, g_ext, wide)

    def middle(r):
        center = g_ext[pl.ds(pl.multiple_of(r + DMAX, STEP), STEP), :].astype(F32)
        mixed = tapped(taps, 1, moved1, center, r, 2, 0)
        at = pl.ds(r, STEP)
        held = pull_norm(near[at, :].astype(F32), mixed * slope1[at, :])
        keep = inside(r, first, last, DMAX, count)
        p_ext[at, :] = ((center + held) * keep).astype(BF16)

    loop(count, middle)
    move(moved2, p_ext, gap)

    def bottom(r):
        center = p_ext[pl.ds(pl.multiple_of(r + DMAX, STEP), STEP), :].astype(F32)
        mixed = tapped(taps, 0, moved2, center, r, 2, 0)
        at = pl.ds(r, STEP)
        held = pull_norm(rows[at, :].astype(F32), mixed * slope0[at, :])
        out[at, :] = (center + held).astype(BF16)

    loop(tok, bottom)


def placed(out, cuts, head, held):
    nxh, nz0, size = cuts
    at = 0
    for xh in range(nxh):
        for core in range(2):
            for xl in range(2):
                for z0 in range(nz0):
                    to = ((xl * nxh + xh) * nz0 + z0) * size
                    out[core, head, to : to + size, :] = held[at : at + size, :]
                    at += size


def naturally(parts, out, low, iy):
    tok, width = parts[0].shape[0], out.shape[1]
    for i, part in enumerate(parts):
        band = lax.rem(iy - i + HEADS, HEADS)
        out[pl.ds(pl.multiple_of(band * tok, tok), tok), :] = part[:, low : low + width]


def weigh_first(cuts, where, f0, f1, f2, f3, t0, t1, t2, t3, t4, out, n_all, u_all, whole):
    iy = where[0]
    parts = (f0, f1, f2, f3)
    naturally(parts, n_all, 0, iy)
    naturally(parts, u_all, n_all.shape[1], iy)
    is_key = lax.broadcasted_iota(jnp.int32, (1, WIDE), 1) < KEY
    for i, t in enumerate(joined((t0, t1, t2, t3, t4), whole)):
        held = t[...]
        first = jnp.where(
            is_key, contract(n_all[...], held, 0, 0), contract(u_all[...], held, 0, 0)
        )
        placed(out, cuts, lax.rem(iy - i + HEADS, HEADS), first)


def weigh_second(
    cuts, where, f0, f1, f2, f3, d0, d1, d2, d3, d4, before, keep, give, n_all, out, whole
):
    iy, core = where[0], where[4]
    naturally((f0, f1, f2, f3), n_all, 0, iy)
    for i, d in enumerate(joined((d0, d1, d2, d3, d4), whole)):
        placed(out, cuts, lax.rem(iy - i + HEADS, HEADS), contract(n_all[...], d[...], 0, 0))
    keep[:, :, :WIDE] = before[core]
    keep[:, :, WIDE:] = out[core]
    give[:, :, :WIDE] = before[1 - core].astype(BF16)
    give[:, :, WIDE:] = out[1 - core].astype(BF16)


def fold(count, part_of, where, keep, *refs):
    got, outs, held = refs[:count], refs[count:-1], refs[-1]
    total = keep[...]
    for g in got:
        total = total + g[...].astype(F32)
    held[...] = total
    size = outs[0].shape[1]
    for i, out in enumerate(outs):
        at = part_of(where, i)
        out[...] = held[:, pl.ds(pl.multiple_of(at * size, 8), size), :].astype(out.dtype)


def fold_call(keep, got, where, part_of, count):
    heads, rows, width = keep.shape
    shape = (heads, rows // count, width)
    return call(
        functools.partial(fold, len(got), part_of),
        [(shape, F32)] + [(shape, BF16)] * (count - 1),
        (where, keep, *got),
        [pltpu.VMEM(keep.shape, F32)],
        smem=(0,),
        us=0.7,
    )


def last_fold(where, keep, got, *refs):
    outs, slots = refs[:-1], refs[-1]
    count = len(outs)
    total = keep[...] + got[...].astype(F32)
    size = total.shape[1] // count
    for i in range(count):
        slots[i] = total[:, i * size : (i + 1) * size, :]
    for i, out in enumerate(outs):
        out[...] = slots[lax.rem(where[9] + i, count)]


def arrange(where, *refs):
    held, out = refs[0][...], refs[-1]
    for g in refs[1:-1]:
        held = held + g[...]
    held = held * (1.0 / where[5].astype(F32))
    keys = HEADS * KEY
    for h in range(HEADS):
        part = held[h]
        out[:, h * KEY : (h + 1) * KEY] = part[:, :KEY]
        low = 2 * keys + HEADS * VALUE + h * VALUE
        out[:, low : low + VALUE] = part[:, KEY:WIDE]
        out[:, keys + h * KEY : keys + (h + 1) * KEY] = part[:, WIDE : WIDE + KEY]
        low = 2 * keys + h * VALUE
        out[:, low : low + VALUE] = part[:, WIDE + KEY :]


def column_order(nz0, nzh, size):
    y, core, xl, z0, zh, j = np.meshgrid(
        *(np.arange(n) for n in (4, 2, 2, nz0, nzh, size)), indexing="ij"
    )
    column = ((((zh * nz0 + z0) * 4 + y) * 2 + xl) * 2 + core) * size + j
    return column.reshape(1, -1).astype(np.int32)


def shift(array, axis, count, step):
    return lax.ppermute(array, axis, [(i, (i + step) % count) for i in range(count)])


def ring(array, axis, count):
    half = array.shape[0] // 2
    before, after = shift(array, axis, count, 1), shift(array, axis, count, -1)
    low = shift(before[:half], axis, count, 1)
    high = shift(after[half:], axis, count, -1)
    return [array, before, low, high, after]


def flip(array, axis):
    return lax.ppermute(array, axis, [(0, 1), (1, 0)])


def halo(rows, nseq):
    width = HALO
    left = lax.ppermute(rows[-width:], SEQ, [(i, i + 1) for i in range(nseq - 1)])
    right = lax.ppermute(rows[:width], SEQ, [(i + 1, i) for i in range(nseq - 1)])
    return left, right


def local(
    sizes, inputs, dilations, taps, gains, bias_table, buckets, w_query, w_key, w_value, w_out, cotangent
):
    nxh, nz, ny = sizes
    nz0 = 2 if nz % 2 == 0 else 1
    nzh = nz // nz0
    nseq = ny * 4
    rows, upstream = inputs[0], cotangent[0]
    tok, chan = rows.shape
    iy, ixl, icore = lax.axis_index("y"), lax.axis_index("xl"), lax.axis_index("core")
    ixh, iz = lax.axis_index("xh"), lax.axis_index("z")
    c = ixl * 2 + icore
    loci = inputs.shape[0] * nxh * nz
    where = jnp.stack(
        [iy, iy * 4 + c, jnp.int32(nseq), c, icore, jnp.int32(loci), ixl, ixh, iz % nz0, iz // nz0]
    ).astype(jnp.int32)
    taps = taps.transpose(1, 0, 2)
    big = (tok, chan)

    left, right = halo(rows, nseq)
    share = chan // (nxh * nz * nseq)
    order = jnp.asarray(column_order(nz0, nzh, share))
    act, d_att = call(
        prelude,
        [(big, BF16), ((tok, HEADS * VALUE), BF16)],
        (rows, gains, upstream, w_out),
        [pltpu.VMEM(big, BF16), pltpu.VMEM(big, BF16), pltpu.VMEM(w_out.shape, BF16),
         pltpu.SemaphoreType.DMA((3,))],
        hbm=(0, 2, 3),
        us=3.0,
        limit=LARGE,
    )
    ext = (tok + 2 * HALO, chan)
    mid = (tok + 2 * DMAX, chan)
    shifted = [pltpu.VMEM((2 * mid[0], chan), F32), pltpu.VMEM((2 * tok, chan), F32)]
    *ms, normed, z, near = call(
        forward,
        [((tok, 2 * WIDE), BF16)] * 4 + [(big, BF16), (big, BF16), (mid, BF16)],
        (where, dilations, left, right, rows, act, d_att, taps, gains, w_query, w_key, w_value),
        [pltpu.VMEM(ext, BF16), pltpu.VMEM(ext, BF16), pltpu.VMEM(mid, BF16),
         pltpu.VMEM((HEADS, tok, 2 * WIDE), BF16), *shifted,
         *(pltpu.VMEM(w.shape, BF16) for w in (w_query, w_key, w_value)), pltpu.SemaphoreType.DMA((3,))],
        smem=(0, 1),
        hbm=(9, 10, 11),
        us=5.0,
        limit=LARGE,
    )
    ms = [ms[0]] + [shift(ms[k], "y", ny, k) for k in (1, 2, 3)]
    unit = order.shape[1]
    fs = call(
        shuffle,
        [((tok, 2 * nxh * unit // 4), BF16)] * 4,
        (where, order, normed, upstream),
        [pltpu.VMEM((4, tok, 2 * nxh * unit // 4), BF16)],
        smem=(0,),
        us=1.6,
    )
    ms, fs, table = lax.optimization_barrier((ms, fs, bias_table.T))
    size = buckets.shape[0]
    (master,) = call(
        expand,
        [((128, size + 1), F32)],
        (where, table, buckets[None]),
        [pltpu.VMEM((1, size + 1), F32)],
        smem=(0,),
        us=1.5,
    )
    kv0 = jnp.concatenate([m[:, :WIDE] for m in ms], axis=0)
    kv2 = flip(kv0, "xl")
    kv1 = flip(kv0, "core")
    fs = [fs[0]] + [shift(fs[k], "y", ny, k) for k in (1, 2, 3)]
    kv2, fs[1], fs[3], master = lax.optimization_barrier((kv2, fs[1], fs[3], master))
    kv3 = flip(kv2, "core")
    many = HEADS * tok
    t, own, far, give = call(
        attend,
        [((many, WIDE), BF16)] + [((many, WIDE), F32)] * 2 + [((2 * many, WIDE), BF16)],
        (where, *ms, kv1, kv2, kv3, master),
        [pltpu.VMEM((many, WIDE), BF16), pltpu.VMEM((many, WIDE), BF16),
         pltpu.VMEM((4 * many, many), F32), pltpu.VMEM((4 * many, many), F32),
         pltpu.VMEM((4 * many, many), BF16), pltpu.VMEM((4 * many, many), BF16)],
        smem=(0,),
        us=7.0,
        limit=24,
    )
    give, fs = lax.optimization_barrier((give, fs))
    got = flip(give, "core")
    own, far = call(
        first_sum, [((many, WIDE), F32), ((many, WIDE), BF16)], (own, far, got), us=0.5
    )
    far, t = lax.optimization_barrier((far, t))
    got = flip(far, "xl")
    ts = ring(t, "y", ny)
    (d,) = call(second_sum, [((many, WIDE), BF16)], (where, own, got), smem=(0,), us=0.5)
    d, near, held = lax.optimization_barrier((d, near, rows))
    ds = ring(d, "y", ny)
    fields = ((many, nxh * unit // 4), BF16)
    cuts = (nxh, nz0, nzh * share)
    half = nxh * nz * 2 * share
    whole = pltpu.VMEM((many, WIDE), BF16)
    (before,) = call(
        functools.partial(weigh_first, cuts),
        [((2, HEADS, half, WIDE), F32)],
        (where, *fs, *ts),
        [pltpu.VMEM(*fields), pltpu.VMEM(*fields), whole],
        smem=(0,),
        us=2.0,
    )
    result, g_query = call(
        project,
        [(big, BF16), (big, F32)],
        (where, *ts, z, w_out, w_query),
        [pltpu.VMEM((HEADS, tok, WIDE), BF16), whole],
        smem=(0,),
        us=2.0,
    )
    slope0, slope1 = call(slopes, [(big, F32), (mid, F32)], (held, near, gains), us=2.6)
    ds, before, result, g_query, slope0, slope1 = lax.optimization_barrier(
        (ds, before, result, g_query, slope0, slope1)
    )
    keep, give = call(
        functools.partial(weigh_second, cuts),
        [((HEADS, half, 2 * WIDE), F32), ((HEADS, half, 2 * WIDE), BF16)],
        (where, *fs, *ds, before),
        [pltpu.VMEM(*fields), pltpu.VMEM((2, HEADS, half, WIDE), F32), whole],
        smem=(0,),
        us=1.5,
    )
    got = flip(give, "core")
    (grad,) = call(
        grad_top,
        [(big, BF16)],
        (where, *ds, g_query, z, upstream, w_key, w_value, gains),
        [pltpu.VMEM((HEADS, tok, WIDE), BF16), pltpu.VMEM(big, F32), whole],
        smem=(0,),
        us=3.0,
    )
    left, right = halo(grad, nseq)

    pairs = [(a, b) for b in range(nxh) for a in range(2)]

    def ring_part(where, i):
        a, b = pairs[i]
        return jnp.bitwise_xor(where[6], a) * nxh + jnp.bitwise_xor(where[7], b)

    keep, *sends = fold_call(keep, [got], where, ring_part, len(pairs))
    got = []
    for (a, b), send in zip(pairs[1:], sends):
        way = [(s, ((s // 2) ^ b) * 2 + ((s % 2) ^ a)) for s in range(2 * nxh)]
        got.append(lax.ppermute(send, ("xh", "xl"), way))
    left, right, got = lax.optimization_barrier((left, right, got))
    if nz0 == 2:
        keep, send = fold_call(
            keep, got, where, lambda where, i: jnp.bitwise_xor(where[8], i), 2
        )
        got = [lax.ppermute(send, "z", [(s, s ^ 1) for s in range(nz)])]
    (input_grad,) = call(
        backward,
        [(big, BF16)],
        (where, dilations, left, right, grad, slope0, slope1, rows, near, taps),
        [pltpu.VMEM(ext, BF16), pltpu.VMEM(mid, BF16), *shifted],
        smem=(0, 1),
        us=4.6,
    )
    input_grad, got = lax.optimization_barrier((input_grad, got))
    part = ((HEADS, share, 2 * WIDE), F32)
    parts = call(
        last_fold,
        [part] * nzh,
        (where, keep, got[0]),
        [pltpu.VMEM((nzh, *part[0]), F32)],
        smem=(0,),
        us=0.6,
    )
    parts = [parts[0]] + [shift(parts[k], "z", nz, k * nz0) for k in range(1, nzh)]
    (weight_sum,) = call(
        arrange, [((share, 8 * WIDE), F32)], (where, *parts), smem=(0,), us=1.0
    )
    return (result[None], input_grad[None], weight_sum)


def solution(mesh):
    nseq = mesh.shape["seq"]
    ny = nseq // 4
    ndp = mesh.shape["dp"]
    nxh = 2 if ndp % 2 == 0 else 1
    sizes = (nxh, ndp // nxh, ny)
    fine = Mesh(mesh.devices.reshape(*sizes, 2, 2), EVERY)
    cells = P(("xh", "z"), SEQ, None)
    return jax.shard_map(
        functools.partial(local, sizes),
        mesh=fine,
        in_specs=(cells, *(P() for _ in range(9)), cells),
        out_specs=(cells, cells, P(EVERY, None)),
        check_vma=False,
    )
```

```python
import functools

import jax
import jax.numpy as jnp
import numpy as np
from jax import lax
from jax.experimental import pallas as pl
from jax.experimental.pallas import tpu as pltpu
from jax.sharding import Mesh, PartitionSpec as P

HEADS = 4
KEY = 64
VALUE = 192
WIDE = KEY + VALUE
BLOCKS = 2
DMAX = 16
HALO = BLOCKS * DMAX
EPS = 1e-06
STEP = 16
LARGE = 60
SEQ = ("y", "xl", "core")
EVERY = ("xh", "z", "y", "xl", "core")
F32 = jnp.float32
BF16 = jnp.bfloat16
ROOT_HALF = 0.7071067811865476
ROOT_TWO_PI = 0.3989422804014327


def contract(left, right, left_dim, right_dim):
    return lax.dot_general(
        left, right, (((left_dim,), (right_dim,)), ((), ())), preferred_element_type=F32
    )


def call(body, outs, args, scratch=(), smem=(), hbm=(), us=1.0, limit=24):
    spaces = [
        pltpu.SMEM if i in smem else pltpu.HBM if i in hbm else pltpu.VMEM for i in range(len(args))
    ]
    return pl.pallas_call(
        body,
        out_shape=tuple(jax.ShapeDtypeStruct(s, d) for s, d in outs),
        in_specs=[pl.BlockSpec(memory_space=s) for s in spaces],
        out_specs=tuple(pl.BlockSpec(memory_space=pltpu.VMEM) for _ in outs),
        scratch_shapes=list(scratch),
        compiler_params=pltpu.CompilerParams(vmem_limit_bytes=limit << 20),
        cost_estimate=pl.CostEstimate(
            flops=1000, bytes_accessed=int(us * 3.6e6), transcendentals=0
        ),
        name=body.__name__ if hasattr(body, "__name__") else body.func.__name__,
    )(*args)


def inverse_norm(rows):
    return lax.rsqrt(jnp.mean(rows * rows, axis=1, keepdims=True) + EPS)


def activate(rows, gain):
    field = rows * inverse_norm(rows) * gain
    return 0.5 * field * (1.0 + lax.erf(field * ROOT_HALF))


def rounded(rows):
    return rows.astype(BF16).astype(F32)


def loop(count, body):
    def step(i, carry):
        body(pl.multiple_of(i * STEP, STEP))
        return carry

    steps = count // STEP
    lax.fori_loop(0, steps, step, 0, unroll=next(u for u in (4, 5, 2, 1) if steps % u == 0))


def inside(start, first, last, edge, count):
    out = (first & (start < edge)) | (last & (start >= count - edge))
    return jnp.where(out, 0.0, 1.0)


def move(moved, source, gap):
    count, total = moved.shape[0] // 2, source.shape[0]
    row = lax.broadcasted_iota(jnp.int32, (count, total), 0)
    col = lax.broadcasted_iota(jnp.int32, (count, total), 1)
    held = source[...]
    for i, at in enumerate((DMAX - gap, DMAX + gap)):
        pick = jnp.where(col == row + at, 1.0, 0.0).astype(BF16)
        moved[i * count : (i + 1) * count, :] = contract(pick, held, 1, 0)


def tapped(taps, first, moved, center, r, low=0, high=2):
    count = moved.shape[0] // 2
    return (
        taps[low, first : first + 1, :] * moved[pl.ds(r, STEP), :]
        + taps[1, first : first + 1, :] * center
        + taps[high, first : first + 1, :] * moved[pl.ds(pl.multiple_of(count + r, STEP), STEP), :]
    )


def shuffle(where, order, normed, upstream, f0, f1, f2, f3, slots):
    unit = order.shape[1]
    chan = normed.shape[1]
    row = lax.broadcasted_iota(jnp.int32, (unit, unit), 0)
    pick = jnp.where(row == order[...], 1.0, 0.0).astype(BF16)
    share = unit // 4
    to = 0
    for source in (normed, upstream):
        for low in range(0, chan, unit):
            mixed = contract(source[:, low : low + unit], pick, 1, 0).astype(BF16)
            for y in range(4):
                slots[lax.rem(y - where[0] + 4, 4), :, to : to + share] = mixed[
                    :, y * share : (y + 1) * share
                ]
            to += share
    for i, out in enumerate((f0, f1, f2, f3)):
        out[...] = slots[i]


def fetch(pairs, sems):
    copies = [pltpu.make_async_copy(a, b, sems.at[i]) for i, (a, b) in enumerate(pairs)]
    for copy in copies:
        copy.start()
    return copies


def expand(where, table, buckets, master, line_ref):
    head = where[0]
    count = buckets.shape[1]
    bucket = lax.broadcasted_iota(jnp.int32, (table.shape[1], count), 0)
    line = lax.dot_general(
        table[...],
        jnp.where(buckets[...] == bucket, 1.0, 0.0),
        (((1,), (0,)), ((), ())),
        precision=lax.Precision.HIGHEST,
        preferred_element_type=F32,
    )
    chosen = lax.broadcasted_iota(jnp.int32, line.shape, 0) == head
    line_ref[...] = jnp.zeros(line_ref.shape, F32)
    line_ref[:, :count] = jnp.sum(jnp.where(chosen, line, 0.0), axis=0, keepdims=True)
    line = line_ref[...]
    span = line.shape[1]
    for r in range(0, 128, 8):
        master[r : r + 8, :] = pltpu.roll(
            jnp.broadcast_to(line, (8, span)), (span - 127 + r) % span, 1, stride=1, stride_axis=0
        )


def prelude(
    rows_far, gains, upstream_far, w_out_far,
    act, d_att, rows, upstream, w_out, sems,
):
    copies = fetch(((rows_far, rows), (upstream_far, upstream), (w_out_far, w_out)), sems)
    gain = gains[0:1, :]
    copies[0].wait()

    def body(r):
        act[pl.ds(r, STEP), :] = activate(rows[pl.ds(r, STEP), :].astype(F32), gain).astype(BF16)

    loop(rows.shape[0], body)
    copies[1].wait()
    copies[2].wait()
    d_att[...] = contract(upstream[...], w_out[...], 1, 1).astype(BF16)


def forward(
    dil, left, right, rows, act, d_att, taps, gains, wq_far, wk_far, wv_far,
    m0, m1, m2, m3, normed, z, near,
    x_ext, a_ext, b_ext, slots, moved1, moved2, w_query, w_key, w_value, sems,
):
    copies = fetch(((wq_far, w_query), (wk_far, w_key), (wv_far, w_value)), sems)
    iy = lax.axis_index("y")
    first = (iy == 0) & (lax.axis_index("xl") == 0) & (lax.axis_index("core") == 0)
    last = (iy == HEADS - 1) & (lax.axis_index("xl") == 1) & (lax.axis_index("core") == 1)
    tok = rows.shape[0]
    x_ext[0:HALO, :] = left[...]
    x_ext[HALO : HALO + tok, :] = rows[...]
    x_ext[HALO + tok :, :] = right[...]
    a_ext[HALO : HALO + tok, :] = act[...]
    gain = gains[0:1, :]
    for r in [*range(0, HALO, STEP), *range(HALO + tok, 2 * HALO + tok, STEP)]:
        a_ext[r : r + STEP, :] = activate(x_ext[r : r + STEP, :].astype(F32), gain).astype(BF16)
    gap, wide = dil[0], dil[1]
    count = tok + 2 * DMAX
    gain = gains[1:2, :]
    move(moved1, a_ext, gap)

    def middle(r):
        center = pl.ds(pl.multiple_of(r + DMAX, STEP), STEP)
        mixed = tapped(taps, 0, moved1, a_ext[center, :].astype(F32), r)
        hidden = (x_ext[center, :].astype(F32) + mixed).astype(BF16)
        near[pl.ds(r, STEP), :] = hidden
        keep = inside(r, first, last, DMAX, count)
        b_ext[pl.ds(r, STEP), :] = (activate(hidden.astype(F32), gain) * keep).astype(BF16)

    loop(count, middle)
    last_gain = gains[2:3, :]
    move(moved2, b_ext, wide)

    def top(r):
        center = pl.ds(pl.multiple_of(r + DMAX, STEP), STEP)
        mixed = tapped(taps, 1, moved2, b_ext[center, :].astype(F32), r)
        hidden = (near[center, :].astype(F32) + mixed).astype(BF16)
        z[pl.ds(r, STEP), :] = hidden
        hidden = hidden.astype(F32)
        normed[pl.ds(r, STEP), :] = (hidden * inverse_norm(hidden) * last_gain).astype(BF16)

    loop(tok, top)
    field = normed[...]
    for copy in copies:
        copy.wait()
    queries = (rounded(contract(field, w_query[...], 1, 0)) * KEY**-0.5).astype(BF16)
    keys = contract(field, w_key[...], 1, 0).astype(BF16)
    values = contract(field, w_value[...], 1, 0).astype(BF16)
    for h in range(HEADS):
        k, v = slice(h * KEY, (h + 1) * KEY), slice(h * VALUE, (h + 1) * VALUE)
        slots[lax.rem(h - iy + HEADS, HEADS)] = jnp.concatenate(
            [keys[:, k], values[:, v], queries[:, k], d_att[:, v]], axis=1
        )
    for i, out in enumerate((m0, m1, m2, m3)):
        out[...] = slots[i]


def slopes(rows, near, gains, slope0, slope1):
    def fill(source, gain, out):
        def body(r):
            held = source[pl.ds(r, STEP), :].astype(F32)
            field = held * inverse_norm(held) * gain
            below = 0.5 * (1.0 + lax.erf(field * ROOT_HALF))
            out[pl.ds(r, STEP), :] = (
                below + field * (ROOT_TWO_PI * jnp.exp(-0.5 * field * field))
            ) * gain

        loop(source.shape[0], body)

    fill(near, gains[1:2, :], slope1)
    fill(rows, gains[0:1, :], slope0)


def attend(
    where, m0, m1, m2, m3, kv1, kv2, kv3, master,
    t, own, far, give, ask, kv0, score, pull, soft, d_soft,
):
    iy, c = where[0], where[3]
    tok = m0.shape[0]
    many = HEADS * tok
    for i, m in enumerate((m0, m1, m2, m3)):
        kv0[i * tok : (i + 1) * tok, :] = m[:, :WIDE]
        ask[i * tok : (i + 1) * tok, :] = m[:, WIDE:]
    both = ask[...]
    lane = lax.broadcasted_iota(jnp.int32, (1, WIDE), 1)
    is_key = lane < KEY
    zero = jnp.zeros_like(both)
    queries = jnp.where(is_key, both, zero)
    d_att = jnp.where(is_key, zero, both)
    blocks = (kv0, kv1, kv2, kv3)
    bands = [lax.rem(iy - i + HEADS, HEADS) for i in range(HEADS)]
    top = None
    for j, block in enumerate(blocks):
        other = jnp.bitwise_xor(c, j)
        for i in range(HEADS):
            at = j * many + i * tok
            part = contract(block[i * tok : (i + 1) * tok, :], queries, 1, 1)
            bias = jnp.concatenate(
                [
                    master[:, pl.ds(pl.multiple_of((4 * (q - bands[i]) + c - other + 15) * tok, tok), tok)]
                    for q in bands
                ],
                axis=1,
            )
            part = part + bias
            score[at : at + tok, :] = part
            peak = jnp.max(part, axis=0, keepdims=True)
            top = peak if top is None else jnp.maximum(top, peak)
    total = jnp.zeros_like(top)
    for at in range(0, 4 * many, tok):
        part = jnp.exp(score[at : at + tok, :] - top)
        score[at : at + tok, :] = part
        total = total + jnp.sum(part, axis=0, keepdims=True)
    scale = 1.0 / total
    delta = jnp.zeros_like(top)
    for j, block in enumerate(blocks):
        for i in range(HEADS):
            at = j * many + i * tok
            probs = score[at : at + tok, :] * scale
            score[at : at + tok, :] = probs
            soft[at : at + tok, :] = probs.astype(BF16)
            part = contract(block[i * tok : (i + 1) * tok, :], d_att, 1, 1)
            pull[at : at + tok, :] = part
            delta = delta + jnp.sum(part * probs, axis=0, keepdims=True)
    for at in range(0, 4 * many, tok):
        d_soft[at : at + tok, :] = (
            score[at : at + tok, :] * (pull[at : at + tok, :] - delta)
        ).astype(BF16)
    att = jnp.zeros((WIDE, many), F32)
    d_query = jnp.zeros((WIDE, many), F32)
    for j, block in enumerate(blocks):
        held = block[...]
        span = slice(j * many, (j + 1) * many)
        att = att + contract(held, soft[span, :], 0, 0)
        d_query = d_query + contract(held, d_soft[span, :], 0, 0)
        d_kv = jnp.where(
            is_key, contract(d_soft[span, :], both, 1, 0), contract(soft[span, :], both, 1, 0)
        )
        if j == 0:
            own[...] = d_kv
        elif j == 2:
            far[...] = d_kv
        else:
            give[(j // 2) * many : (j // 2 + 1) * many, :] = d_kv.astype(BF16)
    side = lax.broadcasted_iota(jnp.int32, (WIDE, 1), 0) < KEY
    mixed = jnp.where(side, d_query * KEY**-0.5, att).T.astype(BF16)
    for i, band in enumerate(bands):
        t[pl.ds(pl.multiple_of(band * tok, tok), tok), :] = mixed[i * tok : (i + 1) * tok, :]


def first_sum(own, far, got, near, send):
    many = own.shape[0]
    near[...] = own[...] + got[:many, :].astype(F32)
    send[...] = (far[...] + got[many:, :].astype(F32)).astype(BF16)


def second_sum(where, near, got, total):
    held = (near[...] + got[...].astype(F32)).astype(BF16)
    tok = held.shape[0] // HEADS
    for i in range(HEADS):
        band = lax.rem(where[0] - i + HEADS, HEADS)
        total[pl.ds(pl.multiple_of(band * tok, tok), tok), :] = held[i * tok : (i + 1) * tok, :]


def joined(parts, whole):
    half = parts[2].shape[0]
    whole[:half, :] = parts[2][...]
    whole[half:, :] = parts[3][...]
    return parts[0], parts[1], whole, parts[4]


def gathered(slots, parts, whole, iy):
    tok = slots.shape[1]
    for i, part in enumerate(joined(parts, whole)):
        held = part[pl.ds(pl.multiple_of(iy * tok, tok), tok), :]
        slots[lax.rem(iy - i + HEADS, HEADS)] = held


def heads_of(slots, low, high):
    return jnp.concatenate([slots[h][:, low:high] for h in range(HEADS)], axis=1)


def project(where, t0, t1, t2, t3, t4, z, w_out, w_query, result, g_query, slots, whole):
    gathered(slots, (t0, t1, t2, t3, t4), whole, where[0])
    att = heads_of(slots, KEY, WIDE)
    result[...] = (z[...].astype(F32) + contract(att, w_out[...], 1, 0)).astype(BF16)
    g_query[...] = contract(heads_of(slots, 0, KEY), w_query[...], 1, 1)


def pull_norm(held, scaled):
    s = inverse_norm(held)
    return s * scaled - held * (s * s * s) * jnp.mean(scaled * held, axis=1, keepdims=True)


def grad_top(
    where, d0, d1, d2, d3, d4, g_query, z, upstream, w_key, w_value, gains, out, slots, total, whole
):
    gathered(slots, (d0, d1, d2, d3, d4), whole, where[0])
    total[...] = (
        g_query[...]
        + contract(heads_of(slots, 0, KEY), w_key[...], 1, 1)
        + contract(heads_of(slots, KEY, WIDE), w_value[...], 1, 1)
    )
    gain = gains[2:3, :]

    def body(r):
        at = pl.ds(r, STEP)
        grad = pull_norm(z[at, :].astype(F32), total[at, :] * gain)
        out[at, :] = (upstream[at, :].astype(F32) + grad).astype(BF16)

    loop(z.shape[0], body)


def backward(
    where, dil, left, right, grad, slope0, slope1, rows, near, taps, out, g_ext, p_ext, moved1, moved2
):
    iseq, nseq = where[1], where[2]
    tok = rows.shape[0]
    first, last = iseq == 0, iseq == nseq - 1
    g_ext[0:HALO, :] = left[...]
    g_ext[HALO : HALO + tok, :] = grad[...]
    g_ext[HALO + tok :, :] = right[...]
    gap, wide = dil[0], dil[1]
    count = tok + 2 * DMAX

    move(moved1, g_ext, wide)

    def middle(r):
        center = g_ext[pl.ds(pl.multiple_of(r + DMAX, STEP), STEP), :].astype(F32)
        mixed = tapped(taps, 1, moved1, center, r, 2, 0)
        at = pl.ds(r, STEP)
        held = pull_norm(near[at, :].astype(F32), mixed * slope1[at, :])
        keep = inside(r, first, last, DMAX, count)
        p_ext[at, :] = ((center + held) * keep).astype(BF16)

    loop(count, middle)
    move(moved2, p_ext, gap)

    def bottom(r):
        center = p_ext[pl.ds(pl.multiple_of(r + DMAX, STEP), STEP), :].astype(F32)
        mixed = tapped(taps, 0, moved2, center, r, 2, 0)
        at = pl.ds(r, STEP)
        held = pull_norm(rows[at, :].astype(F32), mixed * slope0[at, :])
        out[at, :] = (center + held).astype(BF16)

    loop(tok, bottom)


def placed(out, cuts, head, held):
    nxh, nz0, size = cuts
    at = 0
    for xh in range(nxh):
        for core in range(2):
            for xl in range(2):
                for z0 in range(nz0):
                    to = ((xl * nxh + xh) * nz0 + z0) * size
                    out[core, head, to : to + size, :] = held[at : at + size, :]
                    at += size


def naturally(parts, out, low, iy):
    tok, width = parts[0].shape[0], out.shape[1]
    for i, part in enumerate(parts):
        band = lax.rem(iy - i + HEADS, HEADS)
        out[pl.ds(pl.multiple_of(band * tok, tok), tok), :] = part[:, low : low + width]


def weigh_first(cuts, where, f0, f1, f2, f3, t0, t1, t2, t3, t4, out, n_all, u_all, whole):
    iy = where[0]
    parts = (f0, f1, f2, f3)
    naturally(parts, n_all, 0, iy)
    naturally(parts, u_all, n_all.shape[1], iy)
    is_key = lax.broadcasted_iota(jnp.int32, (1, WIDE), 1) < KEY
    for i, t in enumerate(joined((t0, t1, t2, t3, t4), whole)):
        held = t[...]
        first = jnp.where(
            is_key, contract(n_all[...], held, 0, 0), contract(u_all[...], held, 0, 0)
        )
        placed(out, cuts, lax.rem(iy - i + HEADS, HEADS), first)


def weigh_second(
    cuts, where, f0, f1, f2, f3, d0, d1, d2, d3, d4, before, keep, give, n_all, out, whole
):
    iy, core = where[0], where[4]
    naturally((f0, f1, f2, f3), n_all, 0, iy)
    for i, d in enumerate(joined((d0, d1, d2, d3, d4), whole)):
        placed(out, cuts, lax.rem(iy - i + HEADS, HEADS), contract(n_all[...], d[...], 0, 0))
    keep[:, :, :WIDE] = before[core]
    keep[:, :, WIDE:] = out[core]
    give[:, :, :WIDE] = before[1 - core].astype(BF16)
    give[:, :, WIDE:] = out[1 - core].astype(BF16)


def fold(count, part_of, where, keep, *refs):
    got, outs, held = refs[:count], refs[count:-1], refs[-1]
    total = keep[...]
    for g in got:
        total = total + g[...].astype(F32)
    held[...] = total
    size = outs[0].shape[1]
    for i, out in enumerate(outs):
        at = part_of(where, i)
        out[...] = held[:, pl.ds(pl.multiple_of(at * size, 8), size), :].astype(out.dtype)


def fold_call(keep, got, where, part_of, count):
    heads, rows, width = keep.shape
    shape = (heads, rows // count, width)
    return call(
        functools.partial(fold, len(got), part_of),
        [(shape, F32)] + [(shape, BF16)] * (count - 1),
        (where, keep, *got),
        [pltpu.VMEM(keep.shape, F32)],
        smem=(0,),
        us=0.7,
    )


def last_fold(where, keep, got, *refs):
    outs, slots = refs[:-1], refs[-1]
    count = len(outs)
    total = keep[...] + got[...].astype(F32)
    size = total.shape[1] // count
    for i in range(count):
        slots[i] = total[:, i * size : (i + 1) * size, :]
    for i, out in enumerate(outs):
        out[...] = slots[lax.rem(where[9] + i, count)]


def arrange(where, *refs):
    held, out = refs[0][...], refs[-1]
    for g in refs[1:-1]:
        held = held + g[...]
    held = held * (1.0 / where[5].astype(F32))
    keys = HEADS * KEY
    for h in range(HEADS):
        part = held[h]
        out[:, h * KEY : (h + 1) * KEY] = part[:, :KEY]
        low = 2 * keys + HEADS * VALUE + h * VALUE
        out[:, low : low + VALUE] = part[:, KEY:WIDE]
        out[:, keys + h * KEY : keys + (h + 1) * KEY] = part[:, WIDE : WIDE + KEY]
        low = 2 * keys + h * VALUE
        out[:, low : low + VALUE] = part[:, WIDE + KEY :]


def column_order(nz0, nzh, size):
    y, core, xl, z0, zh, j = np.meshgrid(
        *(np.arange(n) for n in (4, 2, 2, nz0, nzh, size)), indexing="ij"
    )
    column = ((((zh * nz0 + z0) * 4 + y) * 2 + xl) * 2 + core) * size + j
    return column.reshape(1, -1).astype(np.int32)


def shift(array, axis, count, step):
    return lax.ppermute(array, axis, [(i, (i + step) % count) for i in range(count)])


def ring(array, axis, count):
    half = array.shape[0] // 2
    before, after = shift(array, axis, count, 1), shift(array, axis, count, -1)
    low = shift(before[:half], axis, count, 1)
    high = shift(after[half:], axis, count, -1)
    return [array, before, low, high, after]


def flip(array, axis):
    return lax.ppermute(array, axis, [(0, 1), (1, 0)])


def halo(rows, nseq):
    width = HALO
    left = lax.ppermute(rows[-width:], SEQ, [(i, i + 1) for i in range(nseq - 1)])
    right = lax.ppermute(rows[:width], SEQ, [(i + 1, i) for i in range(nseq - 1)])
    return left, right


def local(
    sizes, inputs, dilations, taps, gains, bias_table, buckets, w_query, w_key, w_value, w_out, cotangent
):
    nxh, nz, ny = sizes
    nz0 = 2 if nz % 2 == 0 else 1
    nzh = nz // nz0
    nseq = ny * 4
    rows, upstream = inputs[0], cotangent[0]
    tok, chan = rows.shape
    iy, ixl, icore = lax.axis_index("y"), lax.axis_index("xl"), lax.axis_index("core")
    ixh, iz = lax.axis_index("xh"), lax.axis_index("z")
    c = ixl * 2 + icore
    loci = inputs.shape[0] * nxh * nz
    where = jnp.stack(
        [iy, iy * 4 + c, jnp.int32(nseq), c, icore, jnp.int32(loci), ixl, ixh, iz % nz0, iz // nz0]
    ).astype(jnp.int32)
    taps = taps.transpose(1, 0, 2)
    big = (tok, chan)

    left, right = halo(rows, nseq)
    share = chan // (nxh * nz * nseq)
    order = jnp.asarray(column_order(nz0, nzh, share))
    act, d_att = call(
        prelude,
        [(big, BF16), ((tok, HEADS * VALUE), BF16)],
        (rows, gains, upstream, w_out),
        [pltpu.VMEM(big, BF16), pltpu.VMEM(big, BF16), pltpu.VMEM(w_out.shape, BF16),
         pltpu.SemaphoreType.DMA((3,))],
        hbm=(0, 2, 3),
        us=3.0,
        limit=LARGE,
    )
    ext = (tok + 2 * HALO, chan)
    mid = (tok + 2 * DMAX, chan)
    shifted = [pltpu.VMEM((2 * mid[0], chan), F32), pltpu.VMEM((2 * tok, chan), F32)]
    *ms, normed, z, near = call(
        forward,
        [((tok, 2 * WIDE), BF16)] * 4 + [(big, BF16), (big, BF16), (mid, BF16)],
        (dilations, left, right, rows, act, d_att, taps, gains, w_query, w_key, w_value),
        [pltpu.VMEM(ext, BF16), pltpu.VMEM(ext, BF16), pltpu.VMEM(mid, BF16),
         pltpu.VMEM((HEADS, tok, 2 * WIDE), BF16), *shifted,
         *(pltpu.VMEM(w.shape, BF16) for w in (w_query, w_key, w_value)), pltpu.SemaphoreType.DMA((3,))],
        smem=(0,),
        hbm=(8, 9, 10),
        us=5.0,
        limit=LARGE,
    )
    ms = [ms[0]] + [shift(ms[k], "y", ny, k) for k in (1, 2, 3)]
    unit = order.shape[1]
    fs = call(
        shuffle,
        [((tok, 2 * nxh * unit // 4), BF16)] * 4,
        (where, order, normed, upstream),
        [pltpu.VMEM((4, tok, 2 * nxh * unit // 4), BF16)],
        smem=(0,),
        us=1.6,
    )
    ms, fs, table = lax.optimization_barrier((ms, fs, bias_table.T))
    size = buckets.shape[0]
    (master,) = call(
        expand,
        [((128, size + 1), F32)],
        (where, table, buckets[None]),
        [pltpu.VMEM((1, size + 1), F32)],
        smem=(0,),
        us=1.5,
    )
    kv0 = jnp.concatenate([m[:, :WIDE] for m in ms], axis=0)
    kv2 = flip(kv0, "xl")
    kv1 = flip(kv0, "core")
    fs = [fs[0]] + [shift(fs[k], "y", ny, k) for k in (1, 2, 3)]
    kv2, fs[1], fs[3], master = lax.optimization_barrier((kv2, fs[1], fs[3], master))
    kv3 = flip(kv2, "core")
    many = HEADS * tok
    t, own, far, give = call(
        attend,
        [((many, WIDE), BF16)] + [((many, WIDE), F32)] * 2 + [((2 * many, WIDE), BF16)],
        (where, *ms, kv1, kv2, kv3, master),
        [pltpu.VMEM((many, WIDE), BF16), pltpu.VMEM((many, WIDE), BF16),
         pltpu.VMEM((4 * many, many), F32), pltpu.VMEM((4 * many, many), F32),
         pltpu.VMEM((4 * many, many), BF16), pltpu.VMEM((4 * many, many), BF16)],
        smem=(0,),
        us=7.0,
        limit=24,
    )
    give, fs = lax.optimization_barrier((give, fs))
    got = flip(give, "core")
    own, far = call(
        first_sum, [((many, WIDE), F32), ((many, WIDE), BF16)], (own, far, got), us=0.5
    )
    far, t, near, held = lax.optimization_barrier((far, t, near, rows))
    got = flip(far, "xl")
    slope0, slope1 = call(slopes, [(big, F32), (mid, F32)], (held, near, gains), us=0.01)
    got, slope0, slope1 = lax.optimization_barrier((got, slope0, slope1))
    ts = ring(t, "y", ny)
    (d,) = call(second_sum, [((many, WIDE), BF16)], (where, own, got), smem=(0,), us=0.5)
    ds = ring(d, "y", ny)
    fields = ((many, nxh * unit // 4), BF16)
    cuts = (nxh, nz0, nzh * share)
    half = nxh * nz * 2 * share
    whole = pltpu.VMEM((many, WIDE), BF16)
    (before,) = call(
        functools.partial(weigh_first, cuts),
        [((2, HEADS, half, WIDE), F32)],
        (where, *fs, *ts),
        [pltpu.VMEM(*fields), pltpu.VMEM(*fields), whole],
        smem=(0,),
        us=2.0,
    )
    result, g_query = call(
        project,
        [(big, BF16), (big, F32)],
        (where, *ts, z, w_out, w_query),
        [pltpu.VMEM((HEADS, tok, WIDE), BF16), whole],
        smem=(0,),
        us=2.0,
    )
    ds, before, result, g_query = lax.optimization_barrier((ds, before, result, g_query))
    keep, give = call(
        functools.partial(weigh_second, cuts),
        [((HEADS, half, 2 * WIDE), F32), ((HEADS, half, 2 * WIDE), BF16)],
        (where, *fs, *ds, before),
        [pltpu.VMEM(*fields), pltpu.VMEM((2, HEADS, half, WIDE), F32), whole],
        smem=(0,),
        us=1.5,
    )
    got = flip(give, "core")
    (grad,) = call(
        grad_top,
        [(big, BF16)],
        (where, *ds, g_query, z, upstream, w_key, w_value, gains),
        [pltpu.VMEM((HEADS, tok, WIDE), BF16), pltpu.VMEM(big, F32), whole],
        smem=(0,),
        us=3.0,
    )
    left, right = halo(grad, nseq)

    pairs = [(a, b) for b in range(nxh) for a in range(2)]

    def ring_part(where, i):
        a, b = pairs[i]
        return jnp.bitwise_xor(where[6], a) * nxh + jnp.bitwise_xor(where[7], b)

    keep, *sends = fold_call(keep, [got], where, ring_part, len(pairs))
    got = []
    for (a, b), send in zip(pairs[1:], sends):
        way = [(s, ((s // 2) ^ b) * 2 + ((s % 2) ^ a)) for s in range(2 * nxh)]
        got.append(lax.ppermute(send, ("xh", "xl"), way))
    left, right, got = lax.optimization_barrier((left, right, got))
    if nz0 == 2:
        keep, send = fold_call(
            keep, got, where, lambda where, i: jnp.bitwise_xor(where[8], i), 2
        )
        got = [lax.ppermute(send, "z", [(s, s ^ 1) for s in range(nz)])]
    (input_grad,) = call(
        backward,
        [(big, BF16)],
        (where, dilations, left, right, grad, slope0, slope1, rows, near, taps),
        [pltpu.VMEM(ext, BF16), pltpu.VMEM(mid, BF16), *shifted],
        smem=(0, 1),
        us=4.6,
    )
    input_grad, got = lax.optimization_barrier((input_grad, got))
    part = ((HEADS, share, 2 * WIDE), F32)
    parts = call(
        last_fold,
        [part] * nzh,
        (where, keep, got[0]),
        [pltpu.VMEM((nzh, *part[0]), F32)],
        smem=(0,),
        us=0.6,
    )
    away = sorted(range(1, nzh), key=lambda k: -min(k, nzh - k))
    parts = [parts[0]] + [shift(parts[k], "z", nz, k * nz0) for k in away]
    (weight_sum,) = call(
        arrange, [((share, 8 * WIDE), F32)], (where, *parts), smem=(0,), us=1.0
    )
    return (result[None], input_grad[None], weight_sum)


def solution(mesh):
    nseq = mesh.shape["seq"]
    ny = nseq // 4
    ndp = mesh.shape["dp"]
    nxh = 2 if ndp % 2 == 0 else 1
    sizes = (nxh, ndp // nxh, ny)
    fine = Mesh(mesh.devices.reshape(*sizes, 2, 2), EVERY)
    cells = P(("xh", "z"), SEQ, None)
    return jax.shard_map(
        functools.partial(local, sizes),
        mesh=fine,
        in_specs=(cells, *(P() for _ in range(9)), cells),
        out_specs=(cells, cells, P(EVERY, None)),
        check_vma=False,
    )
```

```python
import functools

import jax
import jax.numpy as jnp
import numpy as np
from jax import lax
from jax.experimental import pallas as pl
from jax.experimental.pallas import tpu as pltpu
from jax.sharding import Mesh, PartitionSpec as P

HEADS = 4
KEY = 64
VALUE = 192
WIDE = KEY + VALUE
BLOCKS = 2
DMAX = 16
HALO = BLOCKS * DMAX
EPS = 1e-06
STEP = 16
LARGE = 60
SEQ = ("y", "xl", "core")
EVERY = ("xh", "z", "y", "xl", "core")
F32 = jnp.float32
BF16 = jnp.bfloat16
ROOT_HALF = 0.7071067811865476
ROOT_TWO_PI = 0.3989422804014327


def contract(left, right, left_dim, right_dim):
    return lax.dot_general(
        left, right, (((left_dim,), (right_dim,)), ((), ())), preferred_element_type=F32
    )


def call(body, outs, args, scratch=(), smem=(), hbm=(), anywhere=(), us=1.0, limit=24):
    spaces = [
        pltpu.SMEM if i in smem
        else pltpu.HBM if i in hbm
        else pl.ANY if i in anywhere
        else pltpu.VMEM
        for i in range(len(args))
    ]
    return pl.pallas_call(
        body,
        out_shape=tuple(jax.ShapeDtypeStruct(s, d) for s, d in outs),
        in_specs=[pl.BlockSpec(memory_space=s) for s in spaces],
        out_specs=tuple(pl.BlockSpec(memory_space=pltpu.VMEM) for _ in outs),
        scratch_shapes=list(scratch),
        compiler_params=pltpu.CompilerParams(vmem_limit_bytes=limit << 20),
        cost_estimate=pl.CostEstimate(
            flops=1000, bytes_accessed=int(us * 3.6e6), transcendentals=0
        ),
        name=body.__name__ if hasattr(body, "__name__") else body.func.__name__,
    )(*args)


def inverse_norm(rows):
    return lax.rsqrt(jnp.mean(rows * rows, axis=1, keepdims=True) + EPS)


def activate(rows, gain):
    field = rows * inverse_norm(rows) * gain
    return 0.5 * field * (1.0 + lax.erf(field * ROOT_HALF))


def rounded(rows):
    return rows.astype(BF16).astype(F32)


def loop(count, body):
    def step(i, carry):
        body(pl.multiple_of(i * STEP, STEP))
        return carry

    steps = count // STEP
    lax.fori_loop(0, steps, step, 0, unroll=True)


def inside(start, first, last, edge, count):
    out = (first & (start < edge)) | (last & (start >= count - edge))
    return jnp.where(out, 0.0, 1.0)


def move(moved, source, gap):
    count, total = moved.shape[0] // 2, source.shape[0]
    row = lax.broadcasted_iota(jnp.int32, (count, total), 0)
    col = lax.broadcasted_iota(jnp.int32, (count, total), 1)
    held = source[...]
    for i, at in enumerate((DMAX - gap, DMAX + gap)):
        pick = jnp.where(col == row + at, 1.0, 0.0).astype(BF16)
        moved[i * count : (i + 1) * count, :] = contract(pick, held, 1, 0)


def tapped(taps, first, moved, center, r, low=0, high=2):
    count = moved.shape[0] // 2
    return (
        taps[low, first : first + 1, :] * moved[pl.ds(r, STEP), :]
        + taps[1, first : first + 1, :] * center
        + taps[high, first : first + 1, :] * moved[pl.ds(pl.multiple_of(count + r, STEP), STEP), :]
    )


def shuffle(where, order, normed, upstream, f0, f1, f2, f3, slots):
    unit = order.shape[1]
    chan = normed.shape[1]
    row = lax.broadcasted_iota(jnp.int32, (unit, unit), 0)
    pick = jnp.where(row == order[...], 1.0, 0.0).astype(BF16)
    share = unit // 4
    to = 0
    for source in (normed, upstream):
        for low in range(0, chan, unit):
            mixed = contract(source[:, low : low + unit], pick, 1, 0).astype(BF16)
            for y in range(4):
                slots[lax.rem(y - where[0] + 4, 4), :, to : to + share] = mixed[
                    :, y * share : (y + 1) * share
                ]
            to += share
    for i, out in enumerate((f0, f1, f2, f3)):
        out[...] = slots[i]


def fetch(pairs, sems):
    copies = [pltpu.make_async_copy(a, b, sems.at[i]) for i, (a, b) in enumerate(pairs)]
    for copy in copies:
        copy.start()
    return copies


def expand(where, table, buckets, master, line_ref):
    head = where[0]
    count = buckets.shape[1]
    bucket = lax.broadcasted_iota(jnp.int32, (table.shape[1], count), 0)
    line = lax.dot_general(
        table[...],
        jnp.where(buckets[...] == bucket, 1.0, 0.0),
        (((1,), (0,)), ((), ())),
        precision=lax.Precision.HIGHEST,
        preferred_element_type=F32,
    )
    chosen = lax.broadcasted_iota(jnp.int32, line.shape, 0) == head
    line_ref[...] = jnp.zeros(line_ref.shape, F32)
    line_ref[:, :count] = jnp.sum(jnp.where(chosen, line, 0.0), axis=0, keepdims=True)
    line = line_ref[...]
    span = line.shape[1]
    for r in range(0, 128, 8):
        master[r : r + 8, :] = pltpu.roll(
            jnp.broadcast_to(line, (8, span)), (span - 127 + r) % span, 1, stride=1, stride_axis=0
        )


def prelude(
    rows_far, gains, upstream_far, w_out_far,
    act, d_att, rows, upstream, w_out, sems,
):
    copies = fetch(((rows_far, rows), (upstream_far, upstream), (w_out_far, w_out)), sems)
    gain = gains[0:1, :]
    copies[0].wait()

    def body(r):
        act[pl.ds(r, STEP), :] = activate(rows[pl.ds(r, STEP), :].astype(F32), gain).astype(BF16)

    loop(rows.shape[0], body)
    copies[1].wait()
    copies[2].wait()
    d_att[...] = contract(upstream[...], w_out[...], 1, 1).astype(BF16)


def forward(
    dil, left, right, rows, act, d_att_far, taps, gains, wq_far, wk_far, wv_far,
    m0, m1, m2, m3, normed, z, near,
    x_ext, a_ext, b_ext, slots, moved1, moved2, w_query, w_key, w_value, d_att, sems,
):
    tok = rows.shape[0]
    own = slice(HALO, HALO + tok)
    after = slice(HALO + tok, 2 * HALO + tok)
    copies = fetch(
        (
            (left, x_ext.at[0:HALO]),
            (right, x_ext.at[after]),
            (rows, x_ext.at[own]),
            (act, a_ext.at[own]),
            (d_att_far, d_att),
            (wq_far, w_query),
            (wk_far, w_key),
            (wv_far, w_value),
        ),
        sems,
    )
    iy = lax.axis_index("y")
    first = (iy == 0) & (lax.axis_index("xl") == 0) & (lax.axis_index("core") == 0)
    last = (iy == HEADS - 1) & (lax.axis_index("xl") == 1) & (lax.axis_index("core") == 1)
    copies[0].wait()
    copies[1].wait()
    gain = gains[0:1, :]
    for r in [*range(0, HALO, STEP), *range(HALO + tok, 2 * HALO + tok, STEP)]:
        a_ext[r : r + STEP, :] = activate(x_ext[r : r + STEP, :].astype(F32), gain).astype(BF16)
    gap, wide = dil[0], dil[1]
    count = tok + 2 * DMAX
    gain = gains[1:2, :]
    copies[2].wait()
    copies[3].wait()
    move(moved1, a_ext, gap)

    def middle(r):
        center = pl.ds(pl.multiple_of(r + DMAX, STEP), STEP)
        mixed = tapped(taps, 0, moved1, a_ext[center, :].astype(F32), r)
        hidden = (x_ext[center, :].astype(F32) + mixed).astype(BF16)
        near[pl.ds(r, STEP), :] = hidden
        keep = inside(r, first, last, DMAX, count)
        b_ext[pl.ds(r, STEP), :] = (activate(hidden.astype(F32), gain) * keep).astype(BF16)

    loop(count, middle)
    last_gain = gains[2:3, :]
    move(moved2, b_ext, wide)

    def top(r):
        center = pl.ds(pl.multiple_of(r + DMAX, STEP), STEP)
        mixed = tapped(taps, 1, moved2, b_ext[center, :].astype(F32), r)
        hidden = (near[center, :].astype(F32) + mixed).astype(BF16)
        z[pl.ds(r, STEP), :] = hidden
        hidden = hidden.astype(F32)
        normed[pl.ds(r, STEP), :] = (hidden * inverse_norm(hidden) * last_gain).astype(BF16)

    loop(tok, top)
    field = normed[...]
    for copy in copies[4:]:
        copy.wait()
    queries = (rounded(contract(field, w_query[...], 1, 0)) * KEY**-0.5).astype(BF16)
    keys = contract(field, w_key[...], 1, 0).astype(BF16)
    values = contract(field, w_value[...], 1, 0).astype(BF16)
    for h in range(HEADS):
        k, v = slice(h * KEY, (h + 1) * KEY), slice(h * VALUE, (h + 1) * VALUE)
        slots[lax.rem(h - iy + HEADS, HEADS)] = jnp.concatenate(
            [keys[:, k], values[:, v], queries[:, k], d_att[:, v]], axis=1
        )
    for i, out in enumerate((m0, m1, m2, m3)):
        out[...] = slots[i]


def slopes(rows, near, gains, slope0, slope1):
    def fill(source, gain, out):
        def body(r):
            held = source[pl.ds(r, STEP), :].astype(F32)
            field = held * inverse_norm(held) * gain
            below = 0.5 * (1.0 + lax.erf(field * ROOT_HALF))
            out[pl.ds(r, STEP), :] = (
                below + field * (ROOT_TWO_PI * jnp.exp(-0.5 * field * field))
            ) * gain

        loop(source.shape[0], body)

    fill(near, gains[1:2, :], slope1)
    fill(rows, gains[0:1, :], slope0)


def attend(
    where, m0, m1, m2, m3, kv1, kv2, kv3, master,
    t, own, far, give, ask, kv0, score, pull, soft, d_soft,
):
    iy, c = where[0], where[3]
    tok = m0.shape[0]
    many = HEADS * tok
    for i, m in enumerate((m0, m1, m2, m3)):
        kv0[i * tok : (i + 1) * tok, :] = m[:, :WIDE]
        ask[i * tok : (i + 1) * tok, :] = m[:, WIDE:]
    both = ask[...]
    lane = lax.broadcasted_iota(jnp.int32, (1, WIDE), 1)
    is_key = lane < KEY
    zero = jnp.zeros_like(both)
    queries = jnp.where(is_key, both, zero)
    d_att = jnp.where(is_key, zero, both)
    blocks = (kv0, kv1, kv2, kv3)
    bands = [lax.rem(iy - i + HEADS, HEADS) for i in range(HEADS)]
    top = None
    for j, block in enumerate(blocks):
        other = jnp.bitwise_xor(c, j)
        for i in range(HEADS):
            at = j * many + i * tok
            part = contract(block[i * tok : (i + 1) * tok, :], queries, 1, 1)
            bias = jnp.concatenate(
                [
                    master[:, pl.ds(pl.multiple_of((4 * (q - bands[i]) + c - other + 15) * tok, tok), tok)]
                    for q in bands
                ],
                axis=1,
            )
            part = part + bias
            score[at : at + tok, :] = part
            peak = jnp.max(part, axis=0, keepdims=True)
            top = peak if top is None else jnp.maximum(top, peak)
    total = jnp.zeros_like(top)
    for at in range(0, 4 * many, tok):
        part = jnp.exp(score[at : at + tok, :] - top)
        score[at : at + tok, :] = part
        total = total + jnp.sum(part, axis=0, keepdims=True)
    scale = 1.0 / total
    delta = jnp.zeros_like(top)
    for j, block in enumerate(blocks):
        for i in range(HEADS):
            at = j * many + i * tok
            probs = score[at : at + tok, :] * scale
            score[at : at + tok, :] = probs
            soft[at : at + tok, :] = probs.astype(BF16)
            part = contract(block[i * tok : (i + 1) * tok, :], d_att, 1, 1)
            pull[at : at + tok, :] = part
            delta = delta + jnp.sum(part * probs, axis=0, keepdims=True)
    for at in range(0, 4 * many, tok):
        d_soft[at : at + tok, :] = (
            score[at : at + tok, :] * (pull[at : at + tok, :] - delta)
        ).astype(BF16)
    att = jnp.zeros((WIDE, many), F32)
    d_query = jnp.zeros((WIDE, many), F32)
    for j, block in enumerate(blocks):
        held = block[...]
        span = slice(j * many, (j + 1) * many)
        att = att + contract(held, soft[span, :], 0, 0)
        d_query = d_query + contract(held, d_soft[span, :], 0, 0)
        d_kv = jnp.where(
            is_key, contract(d_soft[span, :], both, 1, 0), contract(soft[span, :], both, 1, 0)
        )
        if j == 0:
            own[...] = d_kv
        elif j == 2:
            far[...] = d_kv
        else:
            give[(j // 2) * many : (j // 2 + 1) * many, :] = d_kv.astype(BF16)
    side = lax.broadcasted_iota(jnp.int32, (WIDE, 1), 0) < KEY
    mixed = jnp.where(side, d_query * KEY**-0.5, att).T.astype(BF16)
    for i, band in enumerate(bands):
        t[pl.ds(pl.multiple_of(band * tok, tok), tok), :] = mixed[i * tok : (i + 1) * tok, :]


def first_sum(own, far, got, near, send):
    many = own.shape[0]
    near[...] = own[...] + got[:many, :].astype(F32)
    send[...] = (far[...] + got[many:, :].astype(F32)).astype(BF16)


def second_sum(where, near, got, total):
    held = (near[...] + got[...].astype(F32)).astype(BF16)
    tok = held.shape[0] // HEADS
    for i in range(HEADS):
        band = lax.rem(where[0] - i + HEADS, HEADS)
        total[pl.ds(pl.multiple_of(band * tok, tok), tok), :] = held[i * tok : (i + 1) * tok, :]


def joined(parts, whole):
    half = parts[2].shape[0]
    whole[:half, :] = parts[2][...]
    whole[half:, :] = parts[3][...]
    return parts[0], parts[1], whole, parts[4]


def gathered(slots, parts, whole, iy):
    tok = slots.shape[1]
    for i, part in enumerate(joined(parts, whole)):
        held = part[pl.ds(pl.multiple_of(iy * tok, tok), tok), :]
        slots[lax.rem(iy - i + HEADS, HEADS)] = held


def heads_of(slots, low, high):
    return jnp.concatenate([slots[h][:, low:high] for h in range(HEADS)], axis=1)


def project(where, t0, t1, t2, t3, t4, z, w_out, result, slots, whole):
    gathered(slots, (t0, t1, t2, t3, t4), whole, where[0])
    att = heads_of(slots, KEY, WIDE)
    result[...] = (z[...].astype(F32) + contract(att, w_out[...], 1, 0)).astype(BF16)


def pull_norm(held, scaled):
    s = inverse_norm(held)
    return s * scaled - held * (s * s * s) * jnp.mean(scaled * held, axis=1, keepdims=True)


def grad_top(
    where, t0, t1, t2, t3, t4, d0, d1, d2, d3, d4, z, upstream, w_query, w_key, w_value, gains,
    out, slots, total, whole, slots_t, whole_t,
):
    gathered(slots_t, (t0, t1, t2, t3, t4), whole_t, where[0])
    d_query = heads_of(slots_t, 0, KEY)
    gathered(slots, (d0, d1, d2, d3, d4), whole, where[0])
    total[...] = (
        contract(d_query, w_query[...], 1, 1)
        + contract(heads_of(slots, 0, KEY), w_key[...], 1, 1)
        + contract(heads_of(slots, KEY, WIDE), w_value[...], 1, 1)
    )
    gain = gains[2:3, :]

    def body(r):
        at = pl.ds(r, STEP)
        grad = pull_norm(z[at, :].astype(F32), total[at, :] * gain)
        out[at, :] = (upstream[at, :].astype(F32) + grad).astype(BF16)

    loop(z.shape[0], body)


def backward(
    where, dil, left, right, grad, slope0, slope1, rows, near, taps, out, g_ext, p_ext, moved1, moved2
):
    iseq, nseq = where[1], where[2]
    tok = rows.shape[0]
    first, last = iseq == 0, iseq == nseq - 1
    g_ext[0:HALO, :] = left[...]
    g_ext[HALO : HALO + tok, :] = grad[...]
    g_ext[HALO + tok :, :] = right[...]
    gap, wide = dil[0], dil[1]
    count = tok + 2 * DMAX

    move(moved1, g_ext, wide)

    def middle(r):
        center = g_ext[pl.ds(pl.multiple_of(r + DMAX, STEP), STEP), :].astype(F32)
        mixed = tapped(taps, 1, moved1, center, r, 2, 0)
        at = pl.ds(r, STEP)
        held = pull_norm(near[at, :].astype(F32), mixed * slope1[at, :])
        keep = inside(r, first, last, DMAX, count)
        p_ext[at, :] = ((center + held) * keep).astype(BF16)

    loop(count, middle)
    move(moved2, p_ext, gap)

    def bottom(r):
        center = p_ext[pl.ds(pl.multiple_of(r + DMAX, STEP), STEP), :].astype(F32)
        mixed = tapped(taps, 0, moved2, center, r, 2, 0)
        at = pl.ds(r, STEP)
        held = pull_norm(rows[at, :].astype(F32), mixed * slope0[at, :])
        out[at, :] = (center + held).astype(BF16)

    loop(tok, bottom)


def placed(out, cuts, head, held):
    nxh, nz0, size = cuts
    at = 0
    for xh in range(nxh):
        for core in range(2):
            for xl in range(2):
                for z0 in range(nz0):
                    to = ((xl * nxh + xh) * nz0 + z0) * size
                    out[core, head, to : to + size, :] = held[at : at + size, :]
                    at += size


def naturally(parts, out, low, iy):
    tok, width = parts[0].shape[0], out.shape[1]
    for i, part in enumerate(parts):
        band = lax.rem(iy - i + HEADS, HEADS)
        out[pl.ds(pl.multiple_of(band * tok, tok), tok), :] = part[:, low : low + width]


def turn(where, f0, f1, f2, f3, n_turned, u_turned, n_all, u_all):
    parts = (f0, f1, f2, f3)
    for low, out, held in ((0, n_turned, n_all), (n_all.shape[1], u_turned, u_all)):
        naturally(parts, held, low, where[0])
        out[...] = held[...].astype(F32).T.astype(BF16)


def weigh_first(cuts, where, n_turned, u_turned, t0, t1, t2, t3, t4, out, whole):
    iy = where[0]
    is_key = lax.broadcasted_iota(jnp.int32, (1, WIDE), 1) < KEY
    for i, t in enumerate(joined((t0, t1, t2, t3, t4), whole)):
        held = t[...]
        first = jnp.where(
            is_key, contract(n_turned[...], held, 1, 0), contract(u_turned[...], held, 1, 0)
        )
        placed(out, cuts, lax.rem(iy - i + HEADS, HEADS), first)


def weigh_second(cuts, where, n_turned, d0, d1, d2, d3, d4, before, keep, give, out, whole):
    iy, core = where[0], where[4]
    for i, d in enumerate(joined((d0, d1, d2, d3, d4), whole)):
        head = lax.rem(iy - i + HEADS, HEADS)
        placed(out, cuts, head, contract(n_turned[...], d[...], 1, 0))
    keep[:, :, :WIDE] = before[core]
    keep[:, :, WIDE:] = out[core]
    give[:, :, :WIDE] = before[1 - core].astype(BF16)
    give[:, :, WIDE:] = out[1 - core].astype(BF16)


def fold(count, part_of, where, keep, *refs):
    got, outs, held = refs[:count], refs[count:-1], refs[-1]
    total = keep[...]
    for g in got:
        total = total + g[...].astype(F32)
    held[...] = total
    size = outs[0].shape[1]
    for i, out in enumerate(outs):
        at = part_of(where, i)
        out[...] = held[:, pl.ds(pl.multiple_of(at * size, 8), size), :].astype(out.dtype)


def fold_call(keep, got, where, part_of, count):
    heads, rows, width = keep.shape
    shape = (heads, rows // count, width)
    return call(
        functools.partial(fold, len(got), part_of),
        [(shape, F32)] + [(shape, BF16)] * (count - 1),
        (where, keep, *got),
        [pltpu.VMEM(keep.shape, F32)],
        smem=(0,),
        us=0.7,
    )


def last_fold(where, keep, got, *refs):
    outs, slots = refs[:-1], refs[-1]
    count = len(outs)
    total = keep[...] + got[...].astype(F32)
    size = total.shape[1] // count
    for i in range(count):
        slots[i] = total[:, i * size : (i + 1) * size, :]
    for i, out in enumerate(outs):
        out[...] = slots[lax.rem(where[9] + i, count)]


def arrange(where, *refs):
    held, out = refs[0][...], refs[-1]
    for g in refs[1:-1]:
        held = held + g[...]
    held = held * (1.0 / where[5].astype(F32))
    keys = HEADS * KEY
    for h in range(HEADS):
        part = held[h]
        out[:, h * KEY : (h + 1) * KEY] = part[:, :KEY]
        low = 2 * keys + HEADS * VALUE + h * VALUE
        out[:, low : low + VALUE] = part[:, KEY:WIDE]
        out[:, keys + h * KEY : keys + (h + 1) * KEY] = part[:, WIDE : WIDE + KEY]
        low = 2 * keys + h * VALUE
        out[:, low : low + VALUE] = part[:, WIDE + KEY :]


def column_order(nz0, nzh, size):
    y, core, xl, z0, zh, j = np.meshgrid(
        *(np.arange(n) for n in (4, 2, 2, nz0, nzh, size)), indexing="ij"
    )
    column = ((((zh * nz0 + z0) * 4 + y) * 2 + xl) * 2 + core) * size + j
    return column.reshape(1, -1).astype(np.int32)


def shift(array, axis, count, step):
    return lax.ppermute(array, axis, [(i, (i + step) % count) for i in range(count)])


def ring(array, axis, count):
    half = array.shape[0] // 2
    before, after = shift(array, axis, count, 1), shift(array, axis, count, -1)
    low = shift(before[:half], axis, count, 1)
    high = shift(after[half:], axis, count, -1)
    return [array, before, low, high, after]


def flip(array, axis):
    return lax.ppermute(array, axis, [(0, 1), (1, 0)])


def halo(rows, nseq):
    width = HALO
    left = lax.ppermute(rows[-width:], SEQ, [(i, i + 1) for i in range(nseq - 1)])
    right = lax.ppermute(rows[:width], SEQ, [(i + 1, i) for i in range(nseq - 1)])
    return left, right


def local(
    sizes, inputs, dilations, taps, gains, bias_table, buckets, w_query, w_key, w_value, w_out, cotangent
):
    nxh, nz, ny = sizes
    nz0 = 2 if nz % 2 == 0 else 1
    nzh = nz // nz0
    nseq = ny * 4
    rows, upstream = inputs[0], cotangent[0]
    tok, chan = rows.shape
    iy, ixl, icore = lax.axis_index("y"), lax.axis_index("xl"), lax.axis_index("core")
    ixh, iz = lax.axis_index("xh"), lax.axis_index("z")
    c = ixl * 2 + icore
    loci = inputs.shape[0] * nxh * nz
    where = jnp.stack(
        [iy, iy * 4 + c, jnp.int32(nseq), c, icore, jnp.int32(loci), ixl, ixh, iz % nz0, iz // nz0]
    ).astype(jnp.int32)
    taps = taps.transpose(1, 0, 2)
    big = (tok, chan)

    left, right = halo(rows, nseq)
    share = chan // (nxh * nz * nseq)
    order = jnp.asarray(column_order(nz0, nzh, share))
    act, d_att = call(
        prelude,
        [(big, BF16), ((tok, HEADS * VALUE), BF16)],
        (rows, gains, upstream, w_out),
        [pltpu.VMEM(big, BF16), pltpu.VMEM(big, BF16), pltpu.VMEM(w_out.shape, BF16),
         pltpu.SemaphoreType.DMA((3,))],
        hbm=(0, 2, 3),
        us=3.0,
        limit=LARGE,
    )
    ext = (tok + 2 * HALO, chan)
    mid = (tok + 2 * DMAX, chan)
    shifted = [pltpu.VMEM((2 * mid[0], chan), F32), pltpu.VMEM((2 * tok, chan), F32)]
    *ms, normed, z, near = call(
        forward,
        [((tok, 2 * WIDE), BF16)] * 4 + [(big, BF16), (big, BF16), (mid, BF16)],
        (dilations, left, right, rows, act, d_att, taps, gains, w_query, w_key, w_value),
        [pltpu.VMEM(ext, BF16), pltpu.VMEM(ext, BF16), pltpu.VMEM(mid, BF16),
         pltpu.VMEM((HEADS, tok, 2 * WIDE), BF16), *shifted,
         *(pltpu.VMEM(w.shape, BF16) for w in (w_query, w_key, w_value)),
         pltpu.VMEM((tok, HEADS * VALUE), BF16), pltpu.SemaphoreType.DMA((8,))],
        smem=(0,),
        anywhere=(1, 2, 3, 4, 5),
        hbm=(8, 9, 10),
        us=5.0,
        limit=LARGE,
    )
    ms = [ms[0]] + [shift(ms[k], "y", ny, k) for k in (1, 2, 3)]
    unit = order.shape[1]
    fs = call(
        shuffle,
        [((tok, 2 * nxh * unit // 4), BF16)] * 4,
        (where, order, normed, upstream),
        [pltpu.VMEM((4, tok, 2 * nxh * unit // 4), BF16)],
        smem=(0,),
        us=1.6,
    )
    ms, fs, table = lax.optimization_barrier((ms, fs, bias_table.T))
    size = buckets.shape[0]
    (master,) = call(
        expand,
        [((128, size + 1), F32)],
        (where, table, buckets[None]),
        [pltpu.VMEM((1, size + 1), F32)],
        smem=(0,),
        us=1.5,
    )
    kv0 = jnp.concatenate([m[:, :WIDE] for m in ms], axis=0)
    kv2 = flip(kv0, "xl")
    kv1 = flip(kv0, "core")
    fs = [fs[0]] + [shift(fs[k], "y", ny, k) for k in (1, 2, 3)]
    kv2, fs[1], fs[3], master = lax.optimization_barrier((kv2, fs[1], fs[3], master))
    kv3 = flip(kv2, "core")
    many = HEADS * tok
    t, own, far, give = call(
        attend,
        [((many, WIDE), BF16)] + [((many, WIDE), F32)] * 2 + [((2 * many, WIDE), BF16)],
        (where, *ms, kv1, kv2, kv3, master),
        [pltpu.VMEM((many, WIDE), BF16), pltpu.VMEM((many, WIDE), BF16),
         pltpu.VMEM((4 * many, many), F32), pltpu.VMEM((4 * many, many), F32),
         pltpu.VMEM((4 * many, many), BF16), pltpu.VMEM((4 * many, many), BF16)],
        smem=(0,),
        us=7.0,
        limit=24,
    )
    give, fs = lax.optimization_barrier((give, fs))
    got = flip(give, "core")
    own, far = call(
        first_sum, [((many, WIDE), F32), ((many, WIDE), BF16)], (own, far, got), us=0.5
    )
    far, t, near, held, fs = lax.optimization_barrier((far, t, near, rows, fs))
    got = flip(far, "xl")
    slope0, slope1 = call(slopes, [(big, F32), (mid, F32)], (held, near, gains), us=0.01)
    fields = (many, nxh * unit // 4)
    n_turned, u_turned = call(
        turn,
        [(fields[::-1], BF16)] * 2,
        (where, *fs),
        [pltpu.VMEM(fields, BF16)] * 2,
        smem=(0,),
        us=0.01,
    )
    got, slope0, slope1, n_turned, u_turned = lax.optimization_barrier(
        (got, slope0, slope1, n_turned, u_turned)
    )
    ts = ring(t, "y", ny)
    (d,) = call(second_sum, [((many, WIDE), BF16)], (where, own, got), smem=(0,), us=0.5)
    ds = ring(d, "y", ny)
    cuts = (nxh, nz0, nzh * share)
    half = nxh * nz * 2 * share
    whole = pltpu.VMEM((many, WIDE), BF16)
    (before,) = call(
        functools.partial(weigh_first, cuts),
        [((2, HEADS, half, WIDE), F32)],
        (where, n_turned, u_turned, *ts),
        [whole],
        smem=(0,),
        us=2.0,
    )
    ds, before = lax.optimization_barrier((ds, before))
    keep, give = call(
        functools.partial(weigh_second, cuts),
        [((HEADS, half, 2 * WIDE), F32), ((HEADS, half, 2 * WIDE), BF16)],
        (where, n_turned, *ds, before),
        [pltpu.VMEM((2, HEADS, half, WIDE), F32), whole],
        smem=(0,),
        us=1.5,
    )
    got = flip(give, "core")
    (grad,) = call(
        grad_top,
        [(big, BF16)],
        (where, *ts, *ds, z, upstream, w_query, w_key, w_value, gains),
        [pltpu.VMEM((HEADS, tok, WIDE), BF16), pltpu.VMEM(big, F32), whole,
         pltpu.VMEM((HEADS, tok, WIDE), BF16), whole],
        smem=(0,),
        us=3.0,
    )
    left, right = halo(grad, nseq)

    pairs = [(a, b) for b in range(nxh) for a in range(2)]

    def ring_part(where, i):
        a, b = pairs[i]
        return jnp.bitwise_xor(where[6], a) * nxh + jnp.bitwise_xor(where[7], b)

    keep, *sends = fold_call(keep, [got], where, ring_part, len(pairs))
    got = []
    for (a, b), send in zip(pairs[1:], sends):
        way = [(s, ((s // 2) ^ b) * 2 + ((s % 2) ^ a)) for s in range(2 * nxh)]
        got.append(lax.ppermute(send, ("xh", "xl"), way))
    left, right, got = lax.optimization_barrier((left, right, got))
    if nz0 == 2:
        keep, send = fold_call(
            keep, got, where, lambda where, i: jnp.bitwise_xor(where[8], i), 2
        )
        got = [lax.ppermute(send, "z", [(s, s ^ 1) for s in range(nz)])]
    (input_grad,) = call(
        backward,
        [(big, BF16)],
        (where, dilations, left, right, grad, slope0, slope1, rows, near, taps),
        [pltpu.VMEM(ext, BF16), pltpu.VMEM(mid, BF16), *shifted],
        smem=(0, 1),
        us=4.6,
    )
    input_grad, got = lax.optimization_barrier((input_grad, got))
    part = ((HEADS, share, 2 * WIDE), F32)
    parts = call(
        last_fold,
        [part] * nzh,
        (where, keep, got[0]),
        [pltpu.VMEM((nzh, *part[0]), F32)],
        smem=(0,),
        us=0.6,
    )
    away = sorted(range(1, nzh), key=lambda k: -min(k, nzh - k))
    *held, z = lax.optimization_barrier((*ts, z, parts[0]))[:-1]
    (result,) = call(
        project,
        [(big, BF16)],
        (where, *held, z, w_out),
        [pltpu.VMEM((HEADS, tok, WIDE), BF16), whole],
        smem=(0,),
        us=0.01,
    )
    parts = [parts[0]] + [shift(parts[k], "z", nz, k * nz0) for k in away]
    result, parts = lax.optimization_barrier((result, parts))
    (weight_sum,) = call(
        arrange, [((share, 8 * WIDE), F32)], (where, *parts), smem=(0,), us=1.0
    )
    return (result[None], input_grad[None], weight_sum)


def solution(mesh):
    nseq = mesh.shape["seq"]
    ny = nseq // 4
    ndp = mesh.shape["dp"]
    nxh = 2 if ndp % 2 == 0 else 1
    sizes = (nxh, ndp // nxh, ny)
    fine = Mesh(mesh.devices.reshape(*sizes, 2, 2), EVERY)
    cells = P(("xh", "z"), SEQ, None)
    return jax.shard_map(
        functools.partial(local, sizes),
        mesh=fine,
        in_specs=(cells, *(P() for _ in range(9)), cells),
        out_specs=(cells, cells, P(EVERY, None)),
        check_vma=False,
    )
```

```python
import functools

import jax
import jax.numpy as jnp
import numpy as np
from jax import lax
from jax.experimental import pallas as pl
from jax.experimental.pallas import tpu as pltpu
from jax.sharding import Mesh, PartitionSpec as P

HEADS = 4
KEY = 64
VALUE = 192
WIDE = KEY + VALUE
BLOCKS = 2
DMAX = 16
HALO = BLOCKS * DMAX
EPS = 1e-06
STEP = 16
LARGE = 60
SEQ = ("y", "xl", "core")
EVERY = ("xh", "z", "y", "xl", "core")
F32 = jnp.float32
BF16 = jnp.bfloat16
ROOT_HALF = 0.7071067811865476
ROOT_TWO_PI = 0.3989422804014327


def contract(left, right, left_dim, right_dim):
    return lax.dot_general(
        left, right, (((left_dim,), (right_dim,)), ((), ())), preferred_element_type=F32
    )


def call(body, outs, args, scratch=(), smem=(), hbm=(), anywhere=(), us=1.0, limit=24):
    spaces = [
        pltpu.SMEM if i in smem
        else pltpu.HBM if i in hbm
        else pl.ANY if i in anywhere
        else pltpu.VMEM
        for i in range(len(args))
    ]
    return pl.pallas_call(
        body,
        out_shape=tuple(jax.ShapeDtypeStruct(s, d) for s, d in outs),
        in_specs=[pl.BlockSpec(memory_space=s) for s in spaces],
        out_specs=tuple(pl.BlockSpec(memory_space=pltpu.VMEM) for _ in outs),
        scratch_shapes=list(scratch),
        compiler_params=pltpu.CompilerParams(vmem_limit_bytes=limit << 20),
        cost_estimate=pl.CostEstimate(
            flops=1000, bytes_accessed=int(us * 3.6e6), transcendentals=0
        ),
        name=body.__name__ if hasattr(body, "__name__") else body.func.__name__,
    )(*args)


def inverse_norm(rows):
    return lax.rsqrt(jnp.mean(rows * rows, axis=1, keepdims=True) + EPS)


def activate(rows, gain):
    field = rows * inverse_norm(rows) * gain
    return 0.5 * field * (1.0 + lax.erf(field * ROOT_HALF))


def rounded(rows):
    return rows.astype(BF16).astype(F32)


def loop(count, body):
    def step(i, carry):
        body(pl.multiple_of(i * STEP, STEP))
        return carry

    steps = count // STEP
    lax.fori_loop(0, steps, step, 0, unroll=True)


def inside(start, first, last, edge, count):
    out = (first & (start < edge)) | (last & (start >= count - edge))
    return jnp.where(out, 0.0, 1.0)


def move(moved, source, gap):
    count, total = moved.shape[0] // 2, source.shape[0]
    row = lax.broadcasted_iota(jnp.int32, (count, total), 0)
    col = lax.broadcasted_iota(jnp.int32, (count, total), 1)
    held = source[...]
    for i, at in enumerate((DMAX - gap, DMAX + gap)):
        pick = jnp.where(col == row + at, 1.0, 0.0).astype(BF16)
        moved[i * count : (i + 1) * count, :] = contract(pick, held, 1, 0)


def tapped(taps, first, moved, center, r, low=0, high=2):
    count = moved.shape[0] // 2
    return (
        taps[low, first : first + 1, :] * moved[pl.ds(r, STEP), :]
        + taps[1, first : first + 1, :] * center
        + taps[high, first : first + 1, :] * moved[pl.ds(pl.multiple_of(count + r, STEP), STEP), :]
    )


def shuffle(where, order, normed, upstream, f0, f1, f2, f3, slots):
    unit = order.shape[1]
    chan = normed.shape[1]
    row = lax.broadcasted_iota(jnp.int32, (unit, unit), 0)
    pick = jnp.where(row == order[...], 1.0, 0.0).astype(BF16)
    share = unit // 4
    to = 0
    for source in (normed, upstream):
        for low in range(0, chan, unit):
            mixed = contract(source[:, low : low + unit], pick, 1, 0).astype(BF16)
            for y in range(4):
                slots[lax.rem(y - where[0] + 4, 4), :, to : to + share] = mixed[
                    :, y * share : (y + 1) * share
                ]
            to += share
    for i, out in enumerate((f0, f1, f2, f3)):
        out[...] = slots[i]


def fetch(pairs, sems):
    copies = [pltpu.make_async_copy(a, b, sems.at[i]) for i, (a, b) in enumerate(pairs)]
    for copy in copies:
        copy.start()
    return copies


def expand(where, table, buckets, master, line_ref):
    head = where[0]
    count = buckets.shape[1]
    bucket = lax.broadcasted_iota(jnp.int32, (table.shape[1], count), 0)
    line = lax.dot_general(
        table[...],
        jnp.where(buckets[...] == bucket, 1.0, 0.0),
        (((1,), (0,)), ((), ())),
        precision=lax.Precision.HIGHEST,
        preferred_element_type=F32,
    )
    chosen = lax.broadcasted_iota(jnp.int32, line.shape, 0) == head
    line_ref[...] = jnp.zeros(line_ref.shape, F32)
    line_ref[:, :count] = jnp.sum(jnp.where(chosen, line, 0.0), axis=0, keepdims=True)
    line = line_ref[...]
    span = line.shape[1]
    for r in range(0, 128, 8):
        master[r : r + 8, :] = pltpu.roll(
            jnp.broadcast_to(line, (8, span)), (span - 127 + r) % span, 1, stride=1, stride_axis=0
        )


def prelude(
    rows_far, gains, upstream_far, w_out_far,
    act, d_att, rows, upstream, w_out, sems,
):
    copies = fetch(((rows_far, rows), (upstream_far, upstream), (w_out_far, w_out)), sems)
    gain = gains[0:1, :]
    copies[0].wait()

    def body(r):
        act[pl.ds(r, STEP), :] = activate(rows[pl.ds(r, STEP), :].astype(F32), gain).astype(BF16)

    loop(rows.shape[0], body)
    copies[1].wait()
    copies[2].wait()
    d_att[...] = contract(upstream[...], w_out[...], 1, 1).astype(BF16)


def forward(
    dil, left, right, rows, act, d_att_far, taps, gains, wq_far, wk_far, wv_far,
    m0, m1, m2, m3, normed, z, near,
    x_ext, a_ext, b_ext, slots, moved1, moved2, w_query, w_key, w_value, d_att, sems,
):
    tok = rows.shape[0]
    own = slice(HALO, HALO + tok)
    after = slice(HALO + tok, 2 * HALO + tok)
    copies = fetch(
        (
            (left, x_ext.at[0:HALO]),
            (right, x_ext.at[after]),
            (rows, x_ext.at[own]),
            (act, a_ext.at[own]),
            (d_att_far, d_att),
            (wq_far, w_query),
            (wk_far, w_key),
            (wv_far, w_value),
        ),
        sems,
    )
    iy = lax.axis_index("y")
    first = (iy == 0) & (lax.axis_index("xl") == 0) & (lax.axis_index("core") == 0)
    last = (iy == HEADS - 1) & (lax.axis_index("xl") == 1) & (lax.axis_index("core") == 1)
    copies[0].wait()
    copies[1].wait()
    gain = gains[0:1, :]
    for r in [*range(0, HALO, STEP), *range(HALO + tok, 2 * HALO + tok, STEP)]:
        a_ext[r : r + STEP, :] = activate(x_ext[r : r + STEP, :].astype(F32), gain).astype(BF16)
    gap, wide = dil[0], dil[1]
    count = tok + 2 * DMAX
    gain = gains[1:2, :]
    copies[2].wait()
    copies[3].wait()
    move(moved1, a_ext, gap)

    def middle(r):
        center = pl.ds(pl.multiple_of(r + DMAX, STEP), STEP)
        mixed = tapped(taps, 0, moved1, a_ext[center, :].astype(F32), r)
        hidden = (x_ext[center, :].astype(F32) + mixed).astype(BF16)
        near[pl.ds(r, STEP), :] = hidden
        keep = inside(r, first, last, DMAX, count)
        b_ext[pl.ds(r, STEP), :] = (activate(hidden.astype(F32), gain) * keep).astype(BF16)

    loop(count, middle)
    last_gain = gains[2:3, :]
    move(moved2, b_ext, wide)

    def top(r):
        center = pl.ds(pl.multiple_of(r + DMAX, STEP), STEP)
        mixed = tapped(taps, 1, moved2, b_ext[center, :].astype(F32), r)
        hidden = (near[center, :].astype(F32) + mixed).astype(BF16)
        z[pl.ds(r, STEP), :] = hidden
        hidden = hidden.astype(F32)
        normed[pl.ds(r, STEP), :] = (hidden * inverse_norm(hidden) * last_gain).astype(BF16)

    loop(tok, top)
    field = normed[...]
    for copy in copies[4:]:
        copy.wait()
    queries = (rounded(contract(field, w_query[...], 1, 0)) * KEY**-0.5).astype(BF16)
    keys = contract(field, w_key[...], 1, 0).astype(BF16)
    values = contract(field, w_value[...], 1, 0).astype(BF16)
    for h in range(HEADS):
        k, v = slice(h * KEY, (h + 1) * KEY), slice(h * VALUE, (h + 1) * VALUE)
        slots[lax.rem(h - iy + HEADS, HEADS)] = jnp.concatenate(
            [keys[:, k], values[:, v], queries[:, k], d_att[:, v]], axis=1
        )
    for i, out in enumerate((m0, m1, m2, m3)):
        out[...] = slots[i]


def slopes(rows, near, gains, slope0, slope1):
    def fill(source, gain, out):
        def body(r):
            held = source[pl.ds(r, STEP), :].astype(F32)
            field = held * inverse_norm(held) * gain
            below = 0.5 * (1.0 + lax.erf(field * ROOT_HALF))
            out[pl.ds(r, STEP), :] = (
                below + field * (ROOT_TWO_PI * jnp.exp(-0.5 * field * field))
            ) * gain

        loop(source.shape[0], body)

    fill(near, gains[1:2, :], slope1)
    fill(rows, gains[0:1, :], slope0)


def attend(
    where, m0, m1, m2, m3, kv1, kv2, kv3, master,
    t, own, far, give, ask, kv0, score, pull, soft, d_soft,
):
    iy, c = where[0], where[3]
    tok = m0.shape[0]
    many = HEADS * tok
    for i, m in enumerate((m0, m1, m2, m3)):
        kv0[i * tok : (i + 1) * tok, :] = m[:, :WIDE]
        ask[i * tok : (i + 1) * tok, :] = m[:, WIDE:]
    both = ask[...]
    lane = lax.broadcasted_iota(jnp.int32, (1, WIDE), 1)
    is_key = lane < KEY
    zero = jnp.zeros_like(both)
    queries = jnp.where(is_key, both, zero)
    d_att = jnp.where(is_key, zero, both)
    blocks = (kv0, kv1, kv2, kv3)
    bands = [lax.rem(iy - i + HEADS, HEADS) for i in range(HEADS)]
    top = None
    for j, block in enumerate(blocks):
        other = jnp.bitwise_xor(c, j)
        product = contract(block[...], queries, 1, 1)
        for i in range(HEADS):
            at = j * many + i * tok
            part = product[i * tok : (i + 1) * tok, :]
            bias = jnp.concatenate(
                [
                    master[:, pl.ds(pl.multiple_of((4 * (q - bands[i]) + c - other + 15) * tok, tok), tok)]
                    for q in bands
                ],
                axis=1,
            )
            part = part + bias
            score[at : at + tok, :] = part
            peak = jnp.max(part, axis=0, keepdims=True)
            top = peak if top is None else jnp.maximum(top, peak)
    total = jnp.zeros_like(top)
    for at in range(0, 4 * many, tok):
        part = jnp.exp(score[at : at + tok, :] - top)
        score[at : at + tok, :] = part
        total = total + jnp.sum(part, axis=0, keepdims=True)
    scale = 1.0 / total
    delta = jnp.zeros_like(top)
    for j, block in enumerate(blocks):
        product = contract(block[...], d_att, 1, 1)
        for i in range(HEADS):
            at = j * many + i * tok
            probs = score[at : at + tok, :] * scale
            score[at : at + tok, :] = probs
            soft[at : at + tok, :] = probs.astype(BF16)
            part = product[i * tok : (i + 1) * tok, :]
            pull[at : at + tok, :] = part
            delta = delta + jnp.sum(part * probs, axis=0, keepdims=True)
    for at in range(0, 4 * many, tok):
        d_soft[at : at + tok, :] = (
            score[at : at + tok, :] * (pull[at : at + tok, :] - delta)
        ).astype(BF16)
    att = jnp.zeros((WIDE, many), F32)
    d_query = jnp.zeros((WIDE, many), F32)
    for j, block in enumerate(blocks):
        held = block[...]
        span = slice(j * many, (j + 1) * many)
        att = att + contract(held, soft[span, :], 0, 0)
        d_query = d_query + contract(held, d_soft[span, :], 0, 0)
        d_kv = jnp.where(
            is_key, contract(d_soft[span, :], both, 1, 0), contract(soft[span, :], both, 1, 0)
        )
        if j == 0:
            own[...] = d_kv
        elif j == 2:
            far[...] = d_kv
        else:
            give[(j // 2) * many : (j // 2 + 1) * many, :] = d_kv.astype(BF16)
    side = lax.broadcasted_iota(jnp.int32, (WIDE, 1), 0) < KEY
    mixed = jnp.where(side, d_query * KEY**-0.5, att).T.astype(BF16)
    for i, band in enumerate(bands):
        t[pl.ds(pl.multiple_of(band * tok, tok), tok), :] = mixed[i * tok : (i + 1) * tok, :]


def first_sum(own, far, got, near, send):
    many = own.shape[0]
    near[...] = own[...] + got[:many, :].astype(F32)
    send[...] = (far[...] + got[many:, :].astype(F32)).astype(BF16)


def second_sum(where, near, got, total):
    held = (near[...] + got[...].astype(F32)).astype(BF16)
    tok = held.shape[0] // HEADS
    for i in range(HEADS):
        band = lax.rem(where[0] - i + HEADS, HEADS)
        total[pl.ds(pl.multiple_of(band * tok, tok), tok), :] = held[i * tok : (i + 1) * tok, :]


def joined(parts, whole):
    half = parts[2].shape[0]
    whole[:half, :] = parts[2][...]
    whole[half:, :] = parts[3][...]
    return parts[0], parts[1], whole, parts[4]


def gathered(slots, parts, whole, iy):
    tok = slots.shape[1]
    for i, part in enumerate(joined(parts, whole)):
        held = part[pl.ds(pl.multiple_of(iy * tok, tok), tok), :]
        slots[lax.rem(iy - i + HEADS, HEADS)] = held


def heads_of(slots, low, high):
    return jnp.concatenate([slots[h][:, low:high] for h in range(HEADS)], axis=1)


def project(where, t0, t1, t2, t3, t4, z, w_out, result, slots, whole):
    gathered(slots, (t0, t1, t2, t3, t4), whole, where[0])
    att = heads_of(slots, KEY, WIDE)
    result[...] = (z[...].astype(F32) + contract(att, w_out[...], 1, 0)).astype(BF16)


def pull_norm(held, scaled):
    s = inverse_norm(held)
    return s * scaled - held * (s * s * s) * jnp.mean(scaled * held, axis=1, keepdims=True)


def grad_top(
    where, t0, t1, t2, t3, t4, d0, d1, d2, d3, d4, z, upstream, w_query, w_key, w_value, gains,
    out, slots, total, whole, slots_t, whole_t,
):
    gathered(slots_t, (t0, t1, t2, t3, t4), whole_t, where[0])
    d_query = heads_of(slots_t, 0, KEY)
    gathered(slots, (d0, d1, d2, d3, d4), whole, where[0])
    total[...] = (
        contract(d_query, w_query[...], 1, 1)
        + contract(heads_of(slots, 0, KEY), w_key[...], 1, 1)
        + contract(heads_of(slots, KEY, WIDE), w_value[...], 1, 1)
    )
    gain = gains[2:3, :]

    def body(r):
        at = pl.ds(r, STEP)
        grad = pull_norm(z[at, :].astype(F32), total[at, :] * gain)
        out[at, :] = (upstream[at, :].astype(F32) + grad).astype(BF16)

    loop(z.shape[0], body)


def backward(
    where, dil, left, right, grad, slope0, slope1, rows, near, taps, out, g_ext, p_ext, moved1, moved2
):
    iseq, nseq = where[1], where[2]
    tok = rows.shape[0]
    first, last = iseq == 0, iseq == nseq - 1
    g_ext[0:HALO, :] = left[...]
    g_ext[HALO : HALO + tok, :] = grad[...]
    g_ext[HALO + tok :, :] = right[...]
    gap, wide = dil[0], dil[1]
    count = tok + 2 * DMAX

    move(moved1, g_ext, wide)

    def middle(r):
        center = g_ext[pl.ds(pl.multiple_of(r + DMAX, STEP), STEP), :].astype(F32)
        mixed = tapped(taps, 1, moved1, center, r, 2, 0)
        at = pl.ds(r, STEP)
        held = pull_norm(near[at, :].astype(F32), mixed * slope1[at, :])
        keep = inside(r, first, last, DMAX, count)
        p_ext[at, :] = ((center + held) * keep).astype(BF16)

    loop(count, middle)
    move(moved2, p_ext, gap)

    def bottom(r):
        center = p_ext[pl.ds(pl.multiple_of(r + DMAX, STEP), STEP), :].astype(F32)
        mixed = tapped(taps, 0, moved2, center, r, 2, 0)
        at = pl.ds(r, STEP)
        held = pull_norm(rows[at, :].astype(F32), mixed * slope0[at, :])
        out[at, :] = (center + held).astype(BF16)

    loop(tok, bottom)


def placed(out, cuts, head, held):
    nxh, nz0, size = cuts
    at = 0
    for xh in range(nxh):
        for core in range(2):
            for xl in range(2):
                for z0 in range(nz0):
                    to = ((xl * nxh + xh) * nz0 + z0) * size
                    out[core, head, to : to + size, :] = held[at : at + size, :]
                    at += size


def naturally(parts, out, low, iy):
    tok, width = parts[0].shape[0], out.shape[1]
    for i, part in enumerate(parts):
        band = lax.rem(iy - i + HEADS, HEADS)
        out[pl.ds(pl.multiple_of(band * tok, tok), tok), :] = part[:, low : low + width]


def turn(where, f0, f1, f2, f3, n_turned, u_turned, n_all, u_all):
    parts = (f0, f1, f2, f3)
    for low, out, held in ((0, n_turned, n_all), (n_all.shape[1], u_turned, u_all)):
        naturally(parts, held, low, where[0])
        out[...] = held[...].astype(F32).T.astype(BF16)


def weigh_first(cuts, where, n_turned, u_turned, t0, t1, t2, t3, t4, out, whole):
    iy = where[0]
    is_key = lax.broadcasted_iota(jnp.int32, (1, WIDE), 1) < KEY
    for i, t in enumerate(joined((t0, t1, t2, t3, t4), whole)):
        held = t[...]
        first = jnp.where(
            is_key, contract(n_turned[...], held, 1, 0), contract(u_turned[...], held, 1, 0)
        )
        placed(out, cuts, lax.rem(iy - i + HEADS, HEADS), first)


def weigh_second(cuts, where, n_turned, d0, d1, d2, d3, d4, before, keep, give, out, whole):
    iy, core = where[0], where[4]
    for i, d in enumerate(joined((d0, d1, d2, d3, d4), whole)):
        head = lax.rem(iy - i + HEADS, HEADS)
        placed(out, cuts, head, contract(n_turned[...], d[...], 1, 0))
    keep[:, :, :WIDE] = before[core]
    keep[:, :, WIDE:] = out[core]
    give[:, :, :WIDE] = before[1 - core].astype(BF16)
    give[:, :, WIDE:] = out[1 - core].astype(BF16)


def fold(count, part_of, where, keep, *refs):
    got, outs, held = refs[:count], refs[count:-1], refs[-1]
    total = keep[...]
    for g in got:
        total = total + g[...].astype(F32)
    held[...] = total
    size = outs[0].shape[1]
    for i, out in enumerate(outs):
        at = part_of(where, i)
        out[...] = held[:, pl.ds(pl.multiple_of(at * size, 8), size), :].astype(out.dtype)


def fold_call(keep, got, where, part_of, count):
    heads, rows, width = keep.shape
    shape = (heads, rows // count, width)
    return call(
        functools.partial(fold, len(got), part_of),
        [(shape, F32)] + [(shape, BF16)] * (count - 1),
        (where, keep, *got),
        [pltpu.VMEM(keep.shape, F32)],
        smem=(0,),
        us=0.7,
    )


def last_fold(where, keep, got, *refs):
    outs, slots = refs[:-1], refs[-1]
    count = len(outs)
    total = keep[...] + got[...].astype(F32)
    size = total.shape[1] // count
    for i in range(count):
        slots[i] = total[:, i * size : (i + 1) * size, :]
    for i, out in enumerate(outs):
        out[...] = slots[lax.rem(where[9] + i, count)]


def arrange(where, *refs):
    held, out = refs[0][...], refs[-1]
    for g in refs[1:-1]:
        held = held + g[...]
    held = held * (1.0 / where[5].astype(F32))
    keys = HEADS * KEY
    for h in range(HEADS):
        part = held[h]
        out[:, h * KEY : (h + 1) * KEY] = part[:, :KEY]
        low = 2 * keys + HEADS * VALUE + h * VALUE
        out[:, low : low + VALUE] = part[:, KEY:WIDE]
        out[:, keys + h * KEY : keys + (h + 1) * KEY] = part[:, WIDE : WIDE + KEY]
        low = 2 * keys + h * VALUE
        out[:, low : low + VALUE] = part[:, WIDE + KEY :]


def column_order(nz0, nzh, size):
    y, core, xl, z0, zh, j = np.meshgrid(
        *(np.arange(n) for n in (4, 2, 2, nz0, nzh, size)), indexing="ij"
    )
    column = ((((zh * nz0 + z0) * 4 + y) * 2 + xl) * 2 + core) * size + j
    return column.reshape(1, -1).astype(np.int32)


def shift(array, axis, count, step):
    return lax.ppermute(array, axis, [(i, (i + step) % count) for i in range(count)])


def ring(array, axis, count):
    half = array.shape[0] // 2
    before, after = shift(array, axis, count, 1), shift(array, axis, count, -1)
    low = shift(before[:half], axis, count, 1)
    high = shift(after[half:], axis, count, -1)
    return [array, before, low, high, after]


def flip(array, axis):
    return lax.ppermute(array, axis, [(0, 1), (1, 0)])


def halo(rows, nseq):
    width = HALO
    left = lax.ppermute(rows[-width:], SEQ, [(i, i + 1) for i in range(nseq - 1)])
    right = lax.ppermute(rows[:width], SEQ, [(i + 1, i) for i in range(nseq - 1)])
    return left, right


def local(
    sizes, inputs, dilations, taps, gains, bias_table, buckets, w_query, w_key, w_value, w_out, cotangent
):
    nxh, nz, ny = sizes
    nz0 = 2 if nz % 2 == 0 else 1
    nzh = nz // nz0
    nseq = ny * 4
    rows, upstream = inputs[0], cotangent[0]
    tok, chan = rows.shape
    iy, ixl, icore = lax.axis_index("y"), lax.axis_index("xl"), lax.axis_index("core")
    ixh, iz = lax.axis_index("xh"), lax.axis_index("z")
    c = ixl * 2 + icore
    loci = inputs.shape[0] * nxh * nz
    where = jnp.stack(
        [iy, iy * 4 + c, jnp.int32(nseq), c, icore, jnp.int32(loci), ixl, ixh, iz % nz0, iz // nz0]
    ).astype(jnp.int32)
    taps = taps.transpose(1, 0, 2)
    big = (tok, chan)

    left, right = halo(rows, nseq)
    share = chan // (nxh * nz * nseq)
    order = jnp.asarray(column_order(nz0, nzh, share))
    act, d_att = call(
        prelude,
        [(big, BF16), ((tok, HEADS * VALUE), BF16)],
        (rows, gains, upstream, w_out),
        [pltpu.VMEM(big, BF16), pltpu.VMEM(big, BF16), pltpu.VMEM(w_out.shape, BF16),
         pltpu.SemaphoreType.DMA((3,))],
        hbm=(0, 2, 3),
        us=3.0,
        limit=LARGE,
    )
    ext = (tok + 2 * HALO, chan)
    mid = (tok + 2 * DMAX, chan)
    shifted = [pltpu.VMEM((2 * mid[0], chan), F32), pltpu.VMEM((2 * tok, chan), F32)]
    *ms, normed, z, near = call(
        forward,
        [((tok, 2 * WIDE), BF16)] * 4 + [(big, BF16), (big, BF16), (mid, BF16)],
        (dilations, left, right, rows, act, d_att, taps, gains, w_query, w_key, w_value),
        [pltpu.VMEM(ext, BF16), pltpu.VMEM(ext, BF16), pltpu.VMEM(mid, BF16),
         pltpu.VMEM((HEADS, tok, 2 * WIDE), BF16), *shifted,
         *(pltpu.VMEM(w.shape, BF16) for w in (w_query, w_key, w_value)),
         pltpu.VMEM((tok, HEADS * VALUE), BF16), pltpu.SemaphoreType.DMA((8,))],
        smem=(0,),
        anywhere=(1, 2, 3, 4, 5),
        hbm=(8, 9, 10),
        us=5.0,
        limit=LARGE,
    )
    ms = [ms[0]] + [shift(ms[k], "y", ny, k) for k in (1, 2, 3)]
    unit = order.shape[1]
    fs = call(
        shuffle,
        [((tok, 2 * nxh * unit // 4), BF16)] * 4,
        (where, order, normed, upstream),
        [pltpu.VMEM((4, tok, 2 * nxh * unit // 4), BF16)],
        smem=(0,),
        us=1.6,
    )
    ms, fs, table = lax.optimization_barrier((ms, fs, bias_table.T))
    size = buckets.shape[0]
    (master,) = call(
        expand,
        [((128, size + 1), F32)],
        (where, table, buckets[None]),
        [pltpu.VMEM((1, size + 1), F32)],
        smem=(0,),
        us=1.5,
    )
    kv0 = jnp.concatenate([m[:, :WIDE] for m in ms], axis=0)
    kv2 = flip(kv0, "xl")
    kv1 = flip(kv0, "core")
    fs = [fs[0]] + [shift(fs[k], "y", ny, k) for k in (1, 2, 3)]
    kv2, fs[1], fs[3], master = lax.optimization_barrier((kv2, fs[1], fs[3], master))
    kv3 = flip(kv2, "core")
    many = HEADS * tok
    t, own, far, give = call(
        attend,
        [((many, WIDE), BF16)] + [((many, WIDE), F32)] * 2 + [((2 * many, WIDE), BF16)],
        (where, *ms, kv1, kv2, kv3, master),
        [pltpu.VMEM((many, WIDE), BF16), pltpu.VMEM((many, WIDE), BF16),
         pltpu.VMEM((4 * many, many), F32), pltpu.VMEM((4 * many, many), F32),
         pltpu.VMEM((4 * many, many), BF16), pltpu.VMEM((4 * many, many), BF16)],
        smem=(0,),
        us=7.0,
        limit=24,
    )
    give, fs = lax.optimization_barrier((give, fs))
    got = flip(give, "core")
    own, far = call(
        first_sum, [((many, WIDE), F32), ((many, WIDE), BF16)], (own, far, got), us=0.5
    )
    far, t, near, held, fs = lax.optimization_barrier((far, t, near, rows, fs))
    got = flip(far, "xl")
    slope0, slope1 = call(slopes, [(big, F32), (mid, F32)], (held, near, gains), us=0.01)
    fields = (many, nxh * unit // 4)
    n_turned, u_turned = call(
        turn,
        [(fields[::-1], BF16)] * 2,
        (where, *fs),
        [pltpu.VMEM(fields, BF16)] * 2,
        smem=(0,),
        us=0.01,
    )
    got, slope0, slope1, n_turned, u_turned = lax.optimization_barrier(
        (got, slope0, slope1, n_turned, u_turned)
    )
    ts = ring(t, "y", ny)
    (d,) = call(second_sum, [((many, WIDE), BF16)], (where, own, got), smem=(0,), us=0.5)
    ds = ring(d, "y", ny)
    cuts = (nxh, nz0, nzh * share)
    half = nxh * nz * 2 * share
    whole = pltpu.VMEM((many, WIDE), BF16)
    (before,) = call(
        functools.partial(weigh_first, cuts),
        [((2, HEADS, half, WIDE), F32)],
        (where, n_turned, u_turned, *ts),
        [whole],
        smem=(0,),
        us=2.0,
    )
    ds, before = lax.optimization_barrier((ds, before))
    keep, give = call(
        functools.partial(weigh_second, cuts),
        [((HEADS, half, 2 * WIDE), F32), ((HEADS, half, 2 * WIDE), BF16)],
        (where, n_turned, *ds, before),
        [pltpu.VMEM((2, HEADS, half, WIDE), F32), whole],
        smem=(0,),
        us=1.5,
    )
    got = flip(give, "core")
    (grad,) = call(
        grad_top,
        [(big, BF16)],
        (where, *ts, *ds, z, upstream, w_query, w_key, w_value, gains),
        [pltpu.VMEM((HEADS, tok, WIDE), BF16), pltpu.VMEM(big, F32), whole,
         pltpu.VMEM((HEADS, tok, WIDE), BF16), whole],
        smem=(0,),
        us=3.0,
    )
    left, right = halo(grad, nseq)

    pairs = [(a, b) for b in range(nxh) for a in range(2)]

    def ring_part(where, i):
        a, b = pairs[i]
        return jnp.bitwise_xor(where[6], a) * nxh + jnp.bitwise_xor(where[7], b)

    keep, *sends = fold_call(keep, [got], where, ring_part, len(pairs))
    got = []
    for (a, b), send in zip(pairs[1:], sends):
        way = [(s, ((s // 2) ^ b) * 2 + ((s % 2) ^ a)) for s in range(2 * nxh)]
        got.append(lax.ppermute(send, ("xh", "xl"), way))
    left, right, got = lax.optimization_barrier((left, right, got))
    if nz0 == 2:
        keep, send = fold_call(
            keep, got, where, lambda where, i: jnp.bitwise_xor(where[8], i), 2
        )
        got = [lax.ppermute(send, "z", [(s, s ^ 1) for s in range(nz)])]
    (input_grad,) = call(
        backward,
        [(big, BF16)],
        (where, dilations, left, right, grad, slope0, slope1, rows, near, taps),
        [pltpu.VMEM(ext, BF16), pltpu.VMEM(mid, BF16), *shifted],
        smem=(0, 1),
        us=4.6,
    )
    input_grad, got = lax.optimization_barrier((input_grad, got))
    part = ((HEADS, share, 2 * WIDE), F32)
    parts = call(
        last_fold,
        [part] * nzh,
        (where, keep, got[0]),
        [pltpu.VMEM((nzh, *part[0]), F32)],
        smem=(0,),
        us=0.6,
    )
    away = sorted(range(1, nzh), key=lambda k: -min(k, nzh - k))
    *held, z = lax.optimization_barrier((*ts, z, parts[0]))[:-1]
    (result,) = call(
        project,
        [(big, BF16)],
        (where, *held, z, w_out),
        [pltpu.VMEM((HEADS, tok, WIDE), BF16), whole],
        smem=(0,),
        us=0.01,
    )
    parts = [parts[0]] + [shift(parts[k], "z", nz, k * nz0) for k in away]
    result, parts = lax.optimization_barrier((result, parts))
    (weight_sum,) = call(
        arrange, [((share, 8 * WIDE), F32)], (where, *parts), smem=(0,), us=1.0
    )
    return (result[None], input_grad[None], weight_sum)


def solution(mesh):
    nseq = mesh.shape["seq"]
    ny = nseq // 4
    ndp = mesh.shape["dp"]
    nxh = 2 if ndp % 2 == 0 else 1
    sizes = (nxh, ndp // nxh, ny)
    fine = Mesh(mesh.devices.reshape(*sizes, 2, 2), EVERY)
    cells = P(("xh", "z"), SEQ, None)
    return jax.shard_map(
        functools.partial(local, sizes),
        mesh=fine,
        in_specs=(cells, *(P() for _ in range(9)), cells),
        out_specs=(cells, cells, P(EVERY, None)),
        check_vma=False,
    )
```

```python
import functools

import jax
import jax.numpy as jnp
import numpy as np
from jax import lax
from jax.experimental import pallas as pl
from jax.experimental.pallas import tpu as pltpu
from jax.sharding import Mesh, PartitionSpec as P

HEADS = 4
KEY = 64
VALUE = 192
WIDE = KEY + VALUE
BLOCKS = 2
DMAX = 16
HALO = BLOCKS * DMAX
EPS = 1e-06
STEP = 16
LARGE = 60
SEQ = ("y", "xl", "core")
EVERY = ("xh", "z", "y", "xl", "core")
F32 = jnp.float32
BF16 = jnp.bfloat16
ROOT_HALF = 0.7071067811865476
ROOT_TWO_PI = 0.3989422804014327


def contract(left, right, left_dim, right_dim):
    return lax.dot_general(
        left, right, (((left_dim,), (right_dim,)), ((), ())), preferred_element_type=F32
    )


def call(body, outs, args, scratch=(), smem=(), hbm=(), anywhere=(), us=1.0, limit=24):
    spaces = [
        pltpu.SMEM if i in smem
        else pltpu.HBM if i in hbm
        else pl.ANY if i in anywhere
        else pltpu.VMEM
        for i in range(len(args))
    ]
    return pl.pallas_call(
        body,
        out_shape=tuple(jax.ShapeDtypeStruct(s, d) for s, d in outs),
        in_specs=[pl.BlockSpec(memory_space=s) for s in spaces],
        out_specs=tuple(pl.BlockSpec(memory_space=pltpu.VMEM) for _ in outs),
        scratch_shapes=list(scratch),
        compiler_params=pltpu.CompilerParams(vmem_limit_bytes=limit << 20),
        cost_estimate=pl.CostEstimate(
            flops=1000, bytes_accessed=int(us * 3.6e6), transcendentals=0
        ),
        name=body.__name__ if hasattr(body, "__name__") else body.func.__name__,
    )(*args)


def inverse_norm(rows):
    return lax.rsqrt(jnp.mean(rows * rows, axis=1, keepdims=True) + EPS)


def activate(rows, gain):
    field = rows * inverse_norm(rows) * gain
    return 0.5 * field * (1.0 + lax.erf(field * ROOT_HALF))


def rounded(rows):
    return rows.astype(BF16).astype(F32)


def loop(count, body):
    def step(i, carry):
        body(pl.multiple_of(i * STEP, STEP))
        return carry

    steps = count // STEP
    lax.fori_loop(0, steps, step, 0, unroll=True)


def inside(start, first, last, edge, count):
    out = (first & (start < edge)) | (last & (start >= count - edge))
    return jnp.where(out, 0.0, 1.0)


def move(moved, source, gap):
    count, total = moved.shape[0] // 2, source.shape[0]
    row = lax.broadcasted_iota(jnp.int32, (count, total), 0)
    col = lax.broadcasted_iota(jnp.int32, (count, total), 1)
    held = source[...]
    for i, at in enumerate((DMAX - gap, DMAX + gap)):
        pick = jnp.where(col == row + at, 1.0, 0.0).astype(BF16)
        moved[i * count : (i + 1) * count, :] = contract(pick, held, 1, 0)


def tapped(taps, first, moved, center, r, low=0, high=2):
    count = moved.shape[0] // 2
    return (
        taps[low, first : first + 1, :] * moved[pl.ds(r, STEP), :]
        + taps[1, first : first + 1, :] * center
        + taps[high, first : first + 1, :] * moved[pl.ds(pl.multiple_of(count + r, STEP), STEP), :]
    )


def shuffle(where, order, normed, upstream, f0, f1, f2, f3, slots):
    unit = order.shape[1]
    chan = normed.shape[1]
    row = lax.broadcasted_iota(jnp.int32, (unit, unit), 0)
    pick = jnp.where(row == order[...], 1.0, 0.0).astype(BF16)
    share = unit // 4
    to = 0
    for source in (normed, upstream):
        for low in range(0, chan, unit):
            mixed = contract(source[:, low : low + unit], pick, 1, 0).astype(BF16)
            for y in range(4):
                slots[lax.rem(y - where[0] + 4, 4), :, to : to + share] = mixed[
                    :, y * share : (y + 1) * share
                ]
            to += share
    for i, out in enumerate((f0, f1, f2, f3)):
        out[...] = slots[i]


def fetch(pairs, sems):
    copies = [pltpu.make_async_copy(a, b, sems.at[i]) for i, (a, b) in enumerate(pairs)]
    for copy in copies:
        copy.start()
    return copies


def expand(where, table, buckets, master, line_ref):
    head = where[0]
    count = buckets.shape[1]
    bucket = lax.broadcasted_iota(jnp.int32, (table.shape[1], count), 0)
    line = lax.dot_general(
        table[...],
        jnp.where(buckets[...] == bucket, 1.0, 0.0),
        (((1,), (0,)), ((), ())),
        precision=lax.Precision.HIGHEST,
        preferred_element_type=F32,
    )
    chosen = lax.broadcasted_iota(jnp.int32, line.shape, 0) == head
    line_ref[...] = jnp.zeros(line_ref.shape, F32)
    line_ref[:, :count] = jnp.sum(jnp.where(chosen, line, 0.0), axis=0, keepdims=True)
    line = line_ref[...]
    span = line.shape[1]
    for r in range(0, 128, 8):
        master[r : r + 8, :] = pltpu.roll(
            jnp.broadcast_to(line, (8, span)), (span - 127 + r) % span, 1, stride=1, stride_axis=0
        )


def prelude(
    rows_far, gains, upstream_far, w_out_far,
    act, d_att, rows, upstream, w_out, sems,
):
    copies = fetch(((rows_far, rows), (upstream_far, upstream), (w_out_far, w_out)), sems)
    gain = gains[0:1, :]
    copies[0].wait()

    def body(r):
        act[pl.ds(r, STEP), :] = activate(rows[pl.ds(r, STEP), :].astype(F32), gain).astype(BF16)

    loop(rows.shape[0], body)
    copies[1].wait()
    copies[2].wait()
    d_att[...] = contract(upstream[...], w_out[...], 1, 1).astype(BF16)


def forward(
    dil, left, right, rows, act, d_att_far, taps, gains, wq_far, wk_far, wv_far,
    m0, m1, m2, m3, normed, z, near,
    x_ext, a_ext, b_ext, slots, moved1, moved2, w_query, w_key, w_value, d_att, sems,
):
    tok = rows.shape[0]
    own = slice(HALO, HALO + tok)
    after = slice(HALO + tok, 2 * HALO + tok)
    copies = fetch(
        (
            (left, x_ext.at[0:HALO]),
            (right, x_ext.at[after]),
            (rows, x_ext.at[own]),
            (act, a_ext.at[own]),
            (d_att_far, d_att),
            (wq_far, w_query),
            (wk_far, w_key),
            (wv_far, w_value),
        ),
        sems,
    )
    iy = lax.axis_index("y")
    first = (iy == 0) & (lax.axis_index("xl") == 0) & (lax.axis_index("core") == 0)
    last = (iy == HEADS - 1) & (lax.axis_index("xl") == 1) & (lax.axis_index("core") == 1)
    copies[0].wait()
    copies[1].wait()
    gain = gains[0:1, :]
    for r in [*range(0, HALO, STEP), *range(HALO + tok, 2 * HALO + tok, STEP)]:
        a_ext[r : r + STEP, :] = activate(x_ext[r : r + STEP, :].astype(F32), gain).astype(BF16)
    gap, wide = dil[0], dil[1]
    count = tok + 2 * DMAX
    gain = gains[1:2, :]
    copies[2].wait()
    copies[3].wait()
    move(moved1, a_ext, gap)

    def middle(r):
        center = pl.ds(pl.multiple_of(r + DMAX, STEP), STEP)
        mixed = tapped(taps, 0, moved1, a_ext[center, :].astype(F32), r)
        hidden = (x_ext[center, :].astype(F32) + mixed).astype(BF16)
        near[pl.ds(r, STEP), :] = hidden
        keep = inside(r, first, last, DMAX, count)
        b_ext[pl.ds(r, STEP), :] = (activate(hidden.astype(F32), gain) * keep).astype(BF16)

    loop(count, middle)
    last_gain = gains[2:3, :]
    move(moved2, b_ext, wide)

    def top(r):
        center = pl.ds(pl.multiple_of(r + DMAX, STEP), STEP)
        mixed = tapped(taps, 1, moved2, b_ext[center, :].astype(F32), r)
        hidden = (near[center, :].astype(F32) + mixed).astype(BF16)
        z[pl.ds(r, STEP), :] = hidden
        hidden = hidden.astype(F32)
        normed[pl.ds(r, STEP), :] = (hidden * inverse_norm(hidden) * last_gain).astype(BF16)

    loop(tok, top)
    field = normed[...]
    for copy in copies[4:]:
        copy.wait()
    queries = (rounded(contract(field, w_query[...], 1, 0)) * KEY**-0.5).astype(BF16)
    keys = contract(field, w_key[...], 1, 0).astype(BF16)
    values = contract(field, w_value[...], 1, 0).astype(BF16)
    for h in range(HEADS):
        k, v = slice(h * KEY, (h + 1) * KEY), slice(h * VALUE, (h + 1) * VALUE)
        slots[lax.rem(h - iy + HEADS, HEADS)] = jnp.concatenate(
            [keys[:, k], values[:, v], queries[:, k], d_att[:, v]], axis=1
        )
    for i, out in enumerate((m0, m1, m2, m3)):
        out[...] = slots[i]


def slopes(rows, near, gains, slope0, slope1):
    def fill(source, gain, out):
        def body(r):
            held = source[pl.ds(r, STEP), :].astype(F32)
            field = held * inverse_norm(held) * gain
            below = 0.5 * (1.0 + lax.erf(field * ROOT_HALF))
            out[pl.ds(r, STEP), :] = (
                below + field * (ROOT_TWO_PI * jnp.exp(-0.5 * field * field))
            ) * gain

        loop(source.shape[0], body)

    fill(near, gains[1:2, :], slope1)
    fill(rows, gains[0:1, :], slope0)


def attend(
    where, m0, m1, m2, m3, kv1, kv2, kv3, master,
    t, own, far, give, ask, kv0, score, pull, soft, d_soft,
):
    iy, c = where[0], where[3]
    tok = m0.shape[0]
    many = HEADS * tok
    for i, m in enumerate((m0, m1, m2, m3)):
        kv0[i * tok : (i + 1) * tok, :] = m[:, :WIDE]
        ask[i * tok : (i + 1) * tok, :] = m[:, WIDE:]
    both = ask[...]
    lane = lax.broadcasted_iota(jnp.int32, (1, WIDE), 1)
    is_key = lane < KEY
    zero = jnp.zeros_like(both)
    queries = jnp.where(is_key, both, zero)
    d_att = jnp.where(is_key, zero, both)
    blocks = (kv0, kv1, kv2, kv3)
    bands = [lax.rem(iy - i + HEADS, HEADS) for i in range(HEADS)]
    top = None
    for j, block in enumerate(blocks):
        other = jnp.bitwise_xor(c, j)
        product = contract(block[...], queries, 1, 1)
        for i in range(HEADS):
            at = j * many + i * tok
            part = product[i * tok : (i + 1) * tok, :]
            bias = jnp.concatenate(
                [
                    master[:, pl.ds(pl.multiple_of((4 * (q - bands[i]) + c - other + 15) * tok, tok), tok)]
                    for q in bands
                ],
                axis=1,
            )
            part = part + bias
            score[at : at + tok, :] = part
            peak = jnp.max(part, axis=0, keepdims=True)
            top = peak if top is None else jnp.maximum(top, peak)
    total = jnp.zeros_like(top)
    for at in range(0, 4 * many, tok):
        part = jnp.exp(score[at : at + tok, :] - top)
        score[at : at + tok, :] = part
        total = total + jnp.sum(part, axis=0, keepdims=True)
    scale = 1.0 / total
    delta = jnp.zeros_like(top)
    for j, block in enumerate(blocks):
        product = contract(block[...], d_att, 1, 1)
        for i in range(HEADS):
            at = j * many + i * tok
            probs = score[at : at + tok, :] * scale
            score[at : at + tok, :] = probs
            soft[at : at + tok, :] = probs.astype(BF16)
            part = product[i * tok : (i + 1) * tok, :]
            pull[at : at + tok, :] = part
            delta = delta + jnp.sum(part * probs, axis=0, keepdims=True)
    for at in range(0, 4 * many, tok):
        d_soft[at : at + tok, :] = (
            score[at : at + tok, :] * (pull[at : at + tok, :] - delta)
        ).astype(BF16)
    att = jnp.zeros((WIDE, many), F32)
    d_query = jnp.zeros((WIDE, many), F32)
    for j, block in enumerate(blocks):
        held = block[...]
        span = slice(j * many, (j + 1) * many)
        att = att + contract(held, soft[span, :], 0, 0)
        d_query = d_query + contract(held, d_soft[span, :], 0, 0)
        d_kv = jnp.where(
            is_key, contract(d_soft[span, :], both, 1, 0), contract(soft[span, :], both, 1, 0)
        )
        if j == 0:
            own[...] = d_kv
        elif j == 2:
            far[...] = d_kv
        else:
            give[(j // 2) * many : (j // 2 + 1) * many, :] = d_kv.astype(BF16)
    side = lax.broadcasted_iota(jnp.int32, (WIDE, 1), 0) < KEY
    mixed = jnp.where(side, d_query * KEY**-0.5, att).T.astype(BF16)
    for i, band in enumerate(bands):
        t[pl.ds(pl.multiple_of(band * tok, tok), tok), :] = mixed[i * tok : (i + 1) * tok, :]


def first_sum(own, far, got, near, send):
    many = own.shape[0]
    near[...] = own[...] + got[:many, :].astype(F32)
    send[...] = (far[...] + got[many:, :].astype(F32)).astype(BF16)


def second_sum(where, near, got, total):
    held = (near[...] + got[...].astype(F32)).astype(BF16)
    tok = held.shape[0] // HEADS
    for i in range(HEADS):
        band = lax.rem(where[0] - i + HEADS, HEADS)
        total[pl.ds(pl.multiple_of(band * tok, tok), tok), :] = held[i * tok : (i + 1) * tok, :]


def joined(parts, whole):
    half = parts[2].shape[0]
    whole[:half, :] = parts[2][...]
    whole[half:, :] = parts[3][...]
    return parts[0], parts[1], whole, parts[4]


def gathered(slots, parts, whole, iy):
    tok = slots.shape[1]
    for i, part in enumerate(joined(parts, whole)):
        held = part[pl.ds(pl.multiple_of(iy * tok, tok), tok), :]
        slots[lax.rem(iy - i + HEADS, HEADS)] = held


def heads_of(slots, low, high):
    return jnp.concatenate([slots[h][:, low:high] for h in range(HEADS)], axis=1)


def project(where, t0, t1, t2, t3, t4, z, w_out, result, slots, whole):
    gathered(slots, (t0, t1, t2, t3, t4), whole, where[0])
    att = heads_of(slots, KEY, WIDE)
    result[...] = (z[...].astype(F32) + contract(att, w_out[...], 1, 0)).astype(BF16)


def pull_norm(held, scaled):
    s = inverse_norm(held)
    return s * scaled - held * (s * s * s) * jnp.mean(scaled * held, axis=1, keepdims=True)


def grad_top(
    where, t0, t1, t2, t3, t4, d0, d1, d2, d3, d4, z, upstream, w_query, w_key, w_value, gains,
    out, slots, total, whole, slots_t, whole_t,
):
    gathered(slots_t, (t0, t1, t2, t3, t4), whole_t, where[0])
    d_query = heads_of(slots_t, 0, KEY)
    gathered(slots, (d0, d1, d2, d3, d4), whole, where[0])
    total[...] = (
        contract(d_query, w_query[...], 1, 1)
        + contract(heads_of(slots, 0, KEY), w_key[...], 1, 1)
        + contract(heads_of(slots, KEY, WIDE), w_value[...], 1, 1)
    )
    gain = gains[2:3, :]

    def body(r):
        at = pl.ds(r, STEP)
        grad = pull_norm(z[at, :].astype(F32), total[at, :] * gain)
        out[at, :] = (upstream[at, :].astype(F32) + grad).astype(BF16)

    loop(z.shape[0], body)


def backward(
    where, dil, left, right, grad, slope0, slope1, rows, near, taps, out, g_ext, p_ext, moved1, moved2
):
    iseq, nseq = where[1], where[2]
    tok = rows.shape[0]
    first, last = iseq == 0, iseq == nseq - 1
    g_ext[0:HALO, :] = left[...]
    g_ext[HALO : HALO + tok, :] = grad[...]
    g_ext[HALO + tok :, :] = right[...]
    gap, wide = dil[0], dil[1]
    count = tok + 2 * DMAX

    move(moved1, g_ext, wide)

    def middle(r):
        center = g_ext[pl.ds(pl.multiple_of(r + DMAX, STEP), STEP), :].astype(F32)
        mixed = tapped(taps, 1, moved1, center, r, 2, 0)
        at = pl.ds(r, STEP)
        held = pull_norm(near[at, :].astype(F32), mixed * slope1[at, :])
        keep = inside(r, first, last, DMAX, count)
        p_ext[at, :] = ((center + held) * keep).astype(BF16)

    loop(count, middle)
    move(moved2, p_ext, gap)

    def bottom(r):
        center = p_ext[pl.ds(pl.multiple_of(r + DMAX, STEP), STEP), :].astype(F32)
        mixed = tapped(taps, 0, moved2, center, r, 2, 0)
        at = pl.ds(r, STEP)
        held = pull_norm(rows[at, :].astype(F32), mixed * slope0[at, :])
        out[at, :] = (center + held).astype(BF16)

    loop(tok, bottom)


def placed(out, cuts, head, held):
    nxh, nz0, size = cuts
    at = 0
    for xh in range(nxh):
        for core in range(2):
            for xl in range(2):
                for z0 in range(nz0):
                    to = ((xl * nxh + xh) * nz0 + z0) * size
                    out[core, head, to : to + size, :] = held[at : at + size, :]
                    at += size


def naturally(parts, out, low, iy):
    tok, width = parts[0].shape[0], out.shape[1]
    for i, part in enumerate(parts):
        band = lax.rem(iy - i + HEADS, HEADS)
        out[pl.ds(pl.multiple_of(band * tok, tok), tok), :] = part[:, low : low + width]


def turn(where, f0, f1, f2, f3, n_turned, u_turned, n_all, u_all):
    parts = (f0, f1, f2, f3)
    for low, out, held in ((0, n_turned, n_all), (n_all.shape[1], u_turned, u_all)):
        naturally(parts, held, low, where[0])
        out[...] = held[...].astype(F32).T.astype(BF16)


def weigh_first(cuts, where, n_turned, u_turned, t0, t1, t2, t3, t4, out, whole):
    iy = where[0]
    is_key = lax.broadcasted_iota(jnp.int32, (1, WIDE), 1) < KEY
    for i, t in enumerate(joined((t0, t1, t2, t3, t4), whole)):
        held = t[...]
        first = jnp.where(
            is_key, contract(n_turned[...], held, 1, 0), contract(u_turned[...], held, 1, 0)
        )
        placed(out, cuts, lax.rem(iy - i + HEADS, HEADS), first)


def weigh_second(cuts, where, n_turned, d0, d1, d2, d3, d4, before, keep, give, out, whole):
    iy, core = where[0], where[4]
    for i, d in enumerate(joined((d0, d1, d2, d3, d4), whole)):
        head = lax.rem(iy - i + HEADS, HEADS)
        placed(out, cuts, head, contract(n_turned[...], d[...], 1, 0))
    keep[:, :, :WIDE] = before[core]
    keep[:, :, WIDE:] = out[core]
    give[:, :, :WIDE] = before[1 - core].astype(BF16)
    give[:, :, WIDE:] = out[1 - core].astype(BF16)


def fold(count, part_of, where, keep, *refs):
    got, outs, held = refs[:count], refs[count:-1], refs[-1]
    total = keep[...]
    for g in got:
        total = total + g[...].astype(F32)
    held[...] = total
    size = outs[0].shape[1]
    for i, out in enumerate(outs):
        at = part_of(where, i)
        out[...] = held[:, pl.ds(pl.multiple_of(at * size, 8), size), :].astype(out.dtype)


def fold_call(keep, got, where, part_of, count):
    heads, rows, width = keep.shape
    shape = (heads, rows // count, width)
    return call(
        functools.partial(fold, len(got), part_of),
        [(shape, F32)] + [(shape, BF16)] * (count - 1),
        (where, keep, *got),
        [pltpu.VMEM(keep.shape, F32)],
        smem=(0,),
        us=0.7,
    )


def last_fold(where, keep, got, *refs):
    outs, slots = refs[:-1], refs[-1]
    count = len(outs)
    total = keep[...] + got[...].astype(F32)
    size = total.shape[1] // count
    for i in range(count):
        slots[i] = total[:, i * size : (i + 1) * size, :]
    for i, out in enumerate(outs):
        out[...] = slots[lax.rem(where[9] + i, count)]


def arrange(where, *refs):
    held, out = refs[0][...], refs[-1]
    for g in refs[1:-1]:
        held = held + g[...]
    held = held * (1.0 / where[5].astype(F32))
    keys = HEADS * KEY
    for h in range(HEADS):
        part = held[h]
        out[:, h * KEY : (h + 1) * KEY] = part[:, :KEY]
        low = 2 * keys + HEADS * VALUE + h * VALUE
        out[:, low : low + VALUE] = part[:, KEY:WIDE]
        out[:, keys + h * KEY : keys + (h + 1) * KEY] = part[:, WIDE : WIDE + KEY]
        low = 2 * keys + h * VALUE
        out[:, low : low + VALUE] = part[:, WIDE + KEY :]


def column_order(nz0, nzh, size):
    y, core, xl, z0, zh, j = np.meshgrid(
        *(np.arange(n) for n in (4, 2, 2, nz0, nzh, size)), indexing="ij"
    )
    column = ((((zh * nz0 + z0) * 4 + y) * 2 + xl) * 2 + core) * size + j
    return column.reshape(1, -1).astype(np.int32)


def shift(array, axis, count, step):
    return lax.ppermute(array, axis, [(i, (i + step) % count) for i in range(count)])


def ring(array, axis, count):
    half = array.shape[0] // 2
    before, after = shift(array, axis, count, 1), shift(array, axis, count, -1)
    low = shift(before[:half], axis, count, 1)
    high = shift(after[half:], axis, count, -1)
    return [array, before, low, high, after]


def flip(array, axis):
    return lax.ppermute(array, axis, [(0, 1), (1, 0)])


def halo(rows, nseq):
    width = HALO
    left = lax.ppermute(rows[-width:], SEQ, [(i, i + 1) for i in range(nseq - 1)])
    right = lax.ppermute(rows[:width], SEQ, [(i + 1, i) for i in range(nseq - 1)])
    return left, right


def local(
    sizes, inputs, dilations, taps, gains, bias_table, buckets, w_query, w_key, w_value, w_out, cotangent
):
    nxh, nz, ny = sizes
    nz0 = 2 if nz % 2 == 0 else 1
    nzh = nz // nz0
    nseq = ny * 4
    rows, upstream = inputs[0], cotangent[0]
    tok, chan = rows.shape
    iy, ixl, icore = lax.axis_index("y"), lax.axis_index("xl"), lax.axis_index("core")
    ixh, iz = lax.axis_index("xh"), lax.axis_index("z")
    c = ixl * 2 + icore
    loci = inputs.shape[0] * nxh * nz
    where = jnp.stack(
        [iy, iy * 4 + c, jnp.int32(nseq), c, icore, jnp.int32(loci), ixl, ixh, iz % nz0, iz // nz0]
    ).astype(jnp.int32)
    taps = taps.transpose(1, 0, 2)
    big = (tok, chan)

    left, right = halo(rows, nseq)
    share = chan // (nxh * nz * nseq)
    order = jnp.asarray(column_order(nz0, nzh, share))
    act, d_att = call(
        prelude,
        [(big, BF16), ((tok, HEADS * VALUE), BF16)],
        (rows, gains, upstream, w_out),
        [pltpu.VMEM(big, BF16), pltpu.VMEM(big, BF16), pltpu.VMEM(w_out.shape, BF16),
         pltpu.SemaphoreType.DMA((3,))],
        hbm=(0, 2, 3),
        us=3.0,
        limit=LARGE,
    )
    ext = (tok + 2 * HALO, chan)
    mid = (tok + 2 * DMAX, chan)
    shifted = [pltpu.VMEM((2 * mid[0], chan), F32), pltpu.VMEM((2 * tok, chan), F32)]
    *ms, normed, z, near = call(
        forward,
        [((tok, 2 * WIDE), BF16)] * 4 + [(big, BF16), (big, BF16), (mid, BF16)],
        (dilations, left, right, rows, act, d_att, taps, gains, w_query, w_key, w_value),
        [pltpu.VMEM(ext, BF16), pltpu.VMEM(ext, BF16), pltpu.VMEM(mid, BF16),
         pltpu.VMEM((HEADS, tok, 2 * WIDE), BF16), *shifted,
         *(pltpu.VMEM(w.shape, BF16) for w in (w_query, w_key, w_value)),
         pltpu.VMEM((tok, HEADS * VALUE), BF16), pltpu.SemaphoreType.DMA((8,))],
        smem=(0,),
        anywhere=(1, 2, 3, 4, 5),
        hbm=(8, 9, 10),
        us=5.0,
        limit=LARGE,
    )
    sent = {k: shift(ms[k], "y", ny, k) for k in (2, 1, 3)}
    ms = [ms[0], sent[1], sent[2], sent[3]]
    unit = order.shape[1]
    fs = call(
        shuffle,
        [((tok, 2 * nxh * unit // 4), BF16)] * 4,
        (where, order, normed, upstream),
        [pltpu.VMEM((4, tok, 2 * nxh * unit // 4), BF16)],
        smem=(0,),
        us=1.6,
    )
    ms, fs, table = lax.optimization_barrier((ms, fs, bias_table.T))
    size = buckets.shape[0]
    (master,) = call(
        expand,
        [((128, size + 1), F32)],
        (where, table, buckets[None]),
        [pltpu.VMEM((1, size + 1), F32)],
        smem=(0,),
        us=1.5,
    )
    kv0 = jnp.concatenate([m[:, :WIDE] for m in ms], axis=0)
    kv2 = flip(kv0, "xl")
    kv1 = flip(kv0, "core")
    fs = [fs[0]] + [shift(fs[k], "y", ny, k) for k in (1, 2, 3)]
    kv2, fs[1], fs[3], master = lax.optimization_barrier((kv2, fs[1], fs[3], master))
    kv3 = flip(kv2, "core")
    many = HEADS * tok
    t, own, far, give = call(
        attend,
        [((many, WIDE), BF16)] + [((many, WIDE), F32)] * 2 + [((2 * many, WIDE), BF16)],
        (where, *ms, kv1, kv2, kv3, master),
        [pltpu.VMEM((many, WIDE), BF16), pltpu.VMEM((many, WIDE), BF16),
         pltpu.VMEM((4 * many, many), F32), pltpu.VMEM((4 * many, many), F32),
         pltpu.VMEM((4 * many, many), BF16), pltpu.VMEM((4 * many, many), BF16)],
        smem=(0,),
        us=7.0,
        limit=24,
    )
    give, fs = lax.optimization_barrier((give, fs))
    got = flip(give, "core")
    own, far = call(
        first_sum, [((many, WIDE), F32), ((many, WIDE), BF16)], (own, far, got), us=0.5
    )
    far, t, near, held, fs = lax.optimization_barrier((far, t, near, rows, fs))
    got = flip(far, "xl")
    slope0, slope1 = call(slopes, [(big, F32), (mid, F32)], (held, near, gains), us=0.01)
    fields = (many, nxh * unit // 4)
    n_turned, u_turned = call(
        turn,
        [(fields[::-1], BF16)] * 2,
        (where, *fs),
        [pltpu.VMEM(fields, BF16)] * 2,
        smem=(0,),
        us=0.01,
    )
    got, slope0, slope1, n_turned, u_turned = lax.optimization_barrier(
        (got, slope0, slope1, n_turned, u_turned)
    )
    ts = ring(t, "y", ny)
    (d,) = call(second_sum, [((many, WIDE), BF16)], (where, own, got), smem=(0,), us=0.5)
    ds = ring(d, "y", ny)
    cuts = (nxh, nz0, nzh * share)
    half = nxh * nz * 2 * share
    whole = pltpu.VMEM((many, WIDE), BF16)
    (before,) = call(
        functools.partial(weigh_first, cuts),
        [((2, HEADS, half, WIDE), F32)],
        (where, n_turned, u_turned, *ts),
        [whole],
        smem=(0,),
        us=2.0,
    )
    ds, before = lax.optimization_barrier((ds, before))
    keep, give = call(
        functools.partial(weigh_second, cuts),
        [((HEADS, half, 2 * WIDE), F32), ((HEADS, half, 2 * WIDE), BF16)],
        (where, n_turned, *ds, before),
        [pltpu.VMEM((2, HEADS, half, WIDE), F32), whole],
        smem=(0,),
        us=1.5,
    )
    got = flip(give, "core")
    (grad,) = call(
        grad_top,
        [(big, BF16)],
        (where, *ts, *ds, z, upstream, w_query, w_key, w_value, gains),
        [pltpu.VMEM((HEADS, tok, WIDE), BF16), pltpu.VMEM(big, F32), whole,
         pltpu.VMEM((HEADS, tok, WIDE), BF16), whole],
        smem=(0,),
        us=3.0,
    )
    left, right = halo(grad, nseq)

    pairs = [(a, b) for a in range(2) for b in range(nxh)]

    def ring_part(where, i):
        a, b = pairs[i]
        return jnp.bitwise_xor(where[6], a) * nxh + jnp.bitwise_xor(where[7], b)

    keep, *sends = fold_call(keep, [got], where, ring_part, len(pairs))
    got = []
    for (a, b), send in zip(pairs[1:], sends):
        way = [(s, ((s // 2) ^ b) * 2 + ((s % 2) ^ a)) for s in range(2 * nxh)]
        got.append(lax.ppermute(send, ("xh", "xl"), way))
    left, right, got = lax.optimization_barrier((left, right, got))
    if nz0 == 2:
        keep, send = fold_call(
            keep, got, where, lambda where, i: jnp.bitwise_xor(where[8], i), 2
        )
        got = [lax.ppermute(send, "z", [(s, s ^ 1) for s in range(nz)])]
    (input_grad,) = call(
        backward,
        [(big, BF16)],
        (where, dilations, left, right, grad, slope0, slope1, rows, near, taps),
        [pltpu.VMEM(ext, BF16), pltpu.VMEM(mid, BF16), *shifted],
        smem=(0, 1),
        us=4.6,
    )
    input_grad, got = lax.optimization_barrier((input_grad, got))
    part = ((HEADS, share, 2 * WIDE), F32)
    parts = call(
        last_fold,
        [part] * nzh,
        (where, keep, got[0]),
        [pltpu.VMEM((nzh, *part[0]), F32)],
        smem=(0,),
        us=0.6,
    )
    away = sorted(range(1, nzh), key=lambda k: -min(k, nzh - k))
    *held, z = lax.optimization_barrier((*ts, z, parts[0]))[:-1]
    (result,) = call(
        project,
        [(big, BF16)],
        (where, *held, z, w_out),
        [pltpu.VMEM((HEADS, tok, WIDE), BF16), whole],
        smem=(0,),
        us=0.01,
    )
    parts = [parts[0]] + [shift(parts[k], "z", nz, k * nz0) for k in away]
    result, parts = lax.optimization_barrier((result, parts))
    (weight_sum,) = call(
        arrange, [((share, 8 * WIDE), F32)], (where, *parts), smem=(0,), us=1.0
    )
    return (result[None], input_grad[None], weight_sum)


def solution(mesh):
    nseq = mesh.shape["seq"]
    ny = nseq // 4
    ndp = mesh.shape["dp"]
    nxh = 2 if ndp % 2 == 0 else 1
    sizes = (nxh, ndp // nxh, ny)
    fine = Mesh(mesh.devices.reshape(*sizes, 2, 2), EVERY)
    cells = P(("xh", "z"), SEQ, None)
    return jax.shard_map(
        functools.partial(local, sizes),
        mesh=fine,
        in_specs=(cells, *(P() for _ in range(9)), cells),
        out_specs=(cells, cells, P(EVERY, None)),
        check_vma=False,
    )
```
